32 devices in a mesh: dp: 8 (over z, y), fsdp: 4 (over x, core).
Axes of the slice: x: 2, y: 2, z: 4, core: 2. Of those that a mesh axis runs over, the one named last changes fastest.
Arguments:
- tokens: bfloat16 [16, 512, 768], P('dp', 'fsdp'), may hold values from -6 to 6
- cotangent: bfloat16 [16, 512, 768], P('dp', 'fsdp'), may hold values from -6 to 6
- lengths: int32 [16], P('dp'), may hold values from 128 to 512, as said below
- routes: int32 [16, 512, 2], P('dp', 'fsdp'), may hold values from 0 to 3, all different within a row; in each aligned block of 128 rows (0 to 127, 128 to 255, ..., all dimensions but the last counted through in order) at most 128 rows name the same one
- gains: float32 [2, 768], P(None, ('dp', 'fsdp')), may hold values from 0.5 to 1.5
- gain_moms: float32 [2, 768], P(None, ('dp', 'fsdp')), may hold values from -256 to 256
- w_dense: float32 [768, 7168], P(('dp', 'fsdp'))
- mom_dense: float32 [768, 7168], P(('dp', 'fsdp')), may hold values from -160 to 160
- w_router: float32 [768, 4], P(('dp', 'fsdp')), may hold values from -0.15625 to 0.15625
- mom_router: float32 [768, 4], P(('dp', 'fsdp')), may hold values from -56 to 56
- w_down: float32 [2048, 768], P(('dp', 'fsdp')), may hold values from -0.125 to 0.125
- mom_down: float32 [2048, 768], P(('dp', 'fsdp')), may hold values from -160 to 160
- e_gate_up: float32 [4, 2, 768, 2048], P('fsdp', None, 'dp'), may hold values from -0.21875 to 0.21875
- e_mom_gate_up: float32 [4, 2, 768, 2048], P('fsdp', None, 'dp'), may hold values from -56 to 56
- e_down: float32 [4, 2048, 768], P('fsdp', 'dp'), may hold values from -0.125 to 0.125
- e_mom_down: float32 [4, 2048, 768], P('fsdp', 'dp'), may hold values from -56 to 56
Outputs:
- output: bfloat16 [16, 512, 768], P('dp', 'fsdp')
- d_tokens: bfloat16 [16, 512, 768], P('dp', 'fsdp')
- new_gain_moms: float32 [2, 768], P(None, ('dp', 'fsdp'))
- new_gains: float32 [2, 768], P(None, ('dp', 'fsdp'))
- new_mom_dense: float32 [768, 7168], P(('dp', 'fsdp'))
- new_dense: float32 [768, 7168], P(('dp', 'fsdp'))
- new_mom_router: float32 [768, 4], P(('dp', 'fsdp'))
- new_router: float32 [768, 4], P(('dp', 'fsdp'))
- new_mom_down: float32 [2048, 768], P(('dp', 'fsdp'))
- new_down: float32 [2048, 768], P(('dp', 'fsdp'))
- new_e_mom_gate_up: float32 [4, 2, 768, 2048], P('fsdp', None, 'dp')
- new_e_gate_up: float32 [4, 2, 768, 2048], P('fsdp', None, 'dp')
- new_e_mom_down: float32 [4, 2048, 768], P('fsdp', 'dp')
- new_e_down: float32 [4, 2048, 768], P('fsdp', 'dp')
The draws below stay inside these ranges and needn't reach their ends.
Inputs may be any that keep to these rules, and one draw needn't show every extreme that they name: `lengths`: rows 2 i and 2 i + 1 stand together; one of the two, which one drawn from the seed, holds a sequence of all 512 positions. `routes`: in each aligned block of 128 positions of a slot row (the rows of one device) no expert is named by more than 128 tokens, and some block reaches 128; a token names 2 different experts.
All inputs are finite; a program needn't handle non-finite values.
Results may differ from the reference program's by a relative error of at most 0.015.
The reference program's roundings to bfloat16 on the way count: a program that leaves them out, or rounds other values in their place, can miss the bound.
Values may be sent and summed in bfloat16 or wider, within the bound.
No kernel may reach another device: no remote copies, remote signals or barrier semaphores. Data moves between devices by JAX's collectives and lax.ppermute only.
A program may use at most 448 MiB of HBM per device.

```python
import math
import jax
import jax.numpy as jnp
import numpy as np
from jax import lax

D = 768
HEADS = 12
HD = 64
FF = 2048
FFS = 2048
TOP = 2
NS_STEPS = 5
TOK_DEV = 128
EXPERTS = 4
ROW = 512
ROWS = 16
MOST = 128


def draw_lengths(key, part):
    key = jax.random.fold_in(key, 7)
    length_key, choose_key = jax.random.split(key)
    ragged = jax.random.randint(length_key, (ROWS,), ROW // 4, ROW + 1)
    chosen = jax.random.randint(choose_key, (ROWS // 2,), 0, 2)
    indices = jnp.arange(ROWS)
    whole = indices % 2 == chosen[indices // 2]
    return jnp.where(whole, ROW, ragged).astype(jnp.int32)


def draw_w_dense(key, part):
    key = jax.random.fold_in(key, 11)
    columns = 4 * D + 2 * FFS
    normal_values = jax.random.normal(key, (D, columns), jnp.float32)
    places = jnp.arange(columns)
    factor = jnp.where((places >= 3 * D) & (places < 4 * D), 16.0, 1.0)
    return normal_values * factor * D ** (-0.5)


def steps_of(stream_key, extent, cuts, low, largest):
    level = 1.0
    for position, blocks in cuts:
        steps = jax.random.uniform(jax.random.fold_in(jax.random.fold_in(stream_key, 6), position), (blocks,), jnp.float32, low / len(cuts), largest / len(cuts))
        level = level * jnp.repeat(jnp.exp(steps), extent[position] // blocks).reshape((-1,) + (1,) * (len(extent) - 1 - position))
    return level


def deal_out(rng, own, number, rows, count, top, reach, slope):
    order = jax.random.permutation(rng, count)
    packed, ordinary = shares(count, rows * top, reach, slope, True), shares(count, rows * top, reach, slope, False)
    places = jnp.arange(count)

    def named(tallies, rotation):
        used = int((tallies > 0).sum())
        fixed = max(1, used // 4)
        moved = fixed + (places - fixed + rotation * (used - fixed)) % max(1, count - fixed)
        return jnp.zeros((count,), jnp.int32).at[order[jnp.where(places < fixed, places, moved)]].set(jnp.asarray(tallies, jnp.int32))

    tallies = jnp.where(number % 4 == 0, named(packed, number // 4), named(ordinary, number - number // 4 - 1))
    mixed = jax.random.permutation(jax.random.fold_in(own, 3), count)
    donor, taker = mixed[0:count // 2 * 2:2], mixed[1:count // 2 * 2:2]
    room = jnp.minimum(tallies[donor] - 1, reach - tallies[taker]) // 2
    room = jnp.where((donor == order[0]) | (taker == order[0]) | (tallies[taker] == 0), 0, jnp.maximum(room, 0))
    moved = jax.random.randint(jax.random.fold_in(own, 4), (count // 2,), 0, 1 << 20) % (room + 1)
    tallies = tallies.at[donor].add(-moved).at[taker].add(moved)
    labels = jnp.searchsorted(jnp.cumsum(tallies), jnp.arange(rows * top), side="right").astype(jnp.int32)
    listing = labels.reshape(top, rows).T
    listing = listing[jax.random.permutation(jax.random.fold_in(own, 1), rows)]
    rotation = jax.random.randint(jax.random.fold_in(own, 2), (rows, 1), 0, top)
    return jnp.take_along_axis(listing, (jnp.arange(top)[None, :] + rotation) % top, axis=1)


def shares(amount, total, bound, skew, full):
    loads = [(1 << 20) // math.isqrt(rank ** skew) + 1 for rank in range(1, amount + 1)]
    largest = bound if full else min(bound, max(-(-total // amount), total * loads[0] // sum(loads)))
    least = 1 if total - largest >= amount - 1 else 0
    given, rest = [largest] + [least] * (amount - 1), total - largest - least * (amount - 1)
    while rest > 0:
        movable = [i for i in range(1, amount) if given[i] < largest] or [i for i in range(1, amount) if given[i] < bound]
        mass, remaining = sum([loads[i] for i in movable]), rest
        for i in movable:
            more = min(bound - given[i], max(1, remaining * loads[i] // mass), rest)
            given[i] = given[i] + more
            rest = rest - more
    return np.array(given)


def gaussian(own_key, shape, width, limit, shards=(), kind=jnp.bfloat16):
    values = width * jax.random.normal(own_key, shape, jnp.float32)
    if shards:
        values = values * steps_of(own_key, shape, shards, -0.22, 0.18)
    return jnp.clip(values, -limit, limit).astype(kind)


def setup_inputs(seed: int = 0) -> dict:
    keys = jax.random.split(jax.random.key(seed), 17)
    tokens = gaussian(keys[0], (ROWS, ROW, D), 1.0, 6.0, ((0, 8), (1, 4)))
    cotangent = gaussian(keys[1], (ROWS, ROW, D), 1.0, 6.0, ((0, 8), (1, 4)))
    lengths = draw_lengths(jax.random.fold_in(keys[16], 71), 0)
    routes_keys = jax.random.split(jax.random.fold_in(keys[3], 1), ROWS * ROW // TOK_DEV)
    routes_turns = jax.random.permutation(jax.random.fold_in(keys[3], 3), ROWS * ROW // TOK_DEV)
    routes = jax.vmap(lambda own, number: deal_out(jax.random.fold_in(keys[3], 2), own, number, TOK_DEV, EXPERTS, TOP, MOST, 2))(routes_keys, routes_turns).reshape((ROWS, ROW, TOP))
    gains = jnp.clip(1.0 + 0.1 * jax.random.normal(keys[4], (2, D), jnp.float32), 0.5, 1.5)
    gain_moms = gaussian(keys[5], (2, D), (0.5 * (ROWS * ROW) ** 0.5), 256.0, ((1, 32),), jnp.float32)
    w_dense = draw_w_dense(jax.random.fold_in(keys[16], 71), 0)
    mom_dense = gaussian(keys[7], (D, 4 * D + 2 * FFS), (0.3 * (ROWS * ROW) ** 0.5), 160.0, ((0, 32),), jnp.float32)
    w_router = gaussian(keys[8], (D, EXPERTS), (2 * D) ** -0.5, 0.15625, ((0, 32),), jnp.float32)
    mom_router = gaussian(keys[9], (D, EXPERTS), (0.1 * (ROWS * ROW) ** 0.5), 56.0, ((0, 32),), jnp.float32)
    w_down = gaussian(keys[10], (FFS, D), FFS ** -0.5, 0.125, ((0, 32),), jnp.float32)
    mom_down = gaussian(keys[11], (FFS, D), (0.3 * (ROWS * ROW) ** 0.5), 160.0, ((0, 32),), jnp.float32)
    e_gate_up = gaussian(keys[12], (EXPERTS, 2, D, FF), D ** -0.5, 0.21875, ((0, 4), (2, 8)), jnp.float32)
    e_mom_gate_up = gaussian(keys[13], (EXPERTS, 2, D, FF), (0.1 * (ROWS * ROW) ** 0.5), 56.0, ((0, 4), (2, 8)), jnp.float32)
    e_down = gaussian(keys[14], (EXPERTS, FF, D), FF ** -0.5, 0.125, ((0, 4), (1, 8)), jnp.float32)
    e_mom_down = gaussian(keys[15], (EXPERTS, FF, D), (0.1 * (ROWS * ROW) ** 0.5), 56.0, ((0, 4), (1, 8)), jnp.float32)
    return dict(tokens=tokens, cotangent=cotangent, lengths=lengths, routes=routes, gains=gains, gain_moms=gain_moms, w_dense=w_dense, mom_dense=mom_dense, w_router=w_router, mom_router=mom_router, w_down=w_down, mom_down=mom_down, e_gate_up=e_gate_up, e_mom_gate_up=e_mom_gate_up, e_down=e_down, e_mom_down=e_mom_down)


NORM_EPSILON = 1e-06
POLY_FIRST = 3.4445
POLY_SECOND = -4.775
POLY_THIRD = 2.0315
HIGHEST_PRECISION = lax.Precision.HIGHEST
MASK_VALUE = -1e+30
DENSE_RATES = (0.8, 5.0, 0.8, 0.8)
ROUTER_RATE = 0.4
DOWN_RATE = 0.5
EXPERT_RATES = (0.8, 0.8, 0.5)
GAIN_DECAY = 0.9
MUON_DECAY = 0.5

@jax.custom_vjp
def low(v):
    return lax.optimization_barrier(v.astype(jnp.bfloat16)).astype(jnp.float32)

@jax.custom_vjp
def low_back(v):
    return v

def low_keep(v):
    return (low(v), None)

def low_pass(kept, grad):
    return (grad,)

def back_keep(v):
    return (v, None)

def back_low(kept, grad):
    return (low(grad),)
low.defvjp(low_keep, low_pass)
low_back.defvjp(back_keep, back_low)

def normalize(values, gain_row):
    return values * lax.rsqrt(lax.optimization_barrier(jnp.mean(values * values, axis=-1, keepdims=True)) + NORM_EPSILON) * gain_row

def rotate(values, places):
    half_size = values.shape[-1] // 2
    frequency = 10000.0 ** (-2.0 * jnp.arange(half_size, dtype=jnp.float32) / values.shape[-1])
    angles = places.astype(jnp.float32)[:, None] * frequency[None, :]
    cosine = jnp.cos(angles)[:, None, :]
    sine = jnp.sin(angles)[:, None, :]
    first_half = values[..., :half_size]
    second_half = values[..., half_size:]
    return jnp.concatenate([first_half * cosine - second_half * sine, second_half * cosine + first_half * sine], axis=-1)

def orthogonal(matrix):
    if matrix.shape[0] > matrix.shape[1]:
        return orthogonal(matrix.T).T
    current = matrix / (jnp.sqrt(jnp.sum(matrix * matrix)) + 1e-07)
    for sweep in range(NS_STEPS):
        gram = jnp.dot(current, current.T, precision=HIGHEST_PRECISION)
        poly = POLY_SECOND * gram + POLY_THIRD * jnp.dot(gram, gram, precision=HIGHEST_PRECISION)
        current = POLY_FIRST * current + jnp.dot(poly, current, precision=HIGHEST_PRECISION)
    return current

def attend_row(operands):
    queries, keys_row, values_row, length = operands
    block_rows = min(512, ROW)
    places = jnp.arange(ROW)

    def one_block(block_operands):
        query_block, query_places = block_operands
        scores = jnp.einsum('qhd,khd->hqk', query_block, keys_row, precision=HIGHEST_PRECISION) * 0.125
        allowed = (places[None, :] <= query_places[:, None]) & (places[None, :] < length)
        scores = low_back(jnp.where(allowed[None], scores, MASK_VALUE))
        weights = low(jnp.exp(scores - jax.nn.logsumexp(scores, axis=-1, keepdims=True)))
        return jnp.einsum('hqk,khd->qhd', weights, values_row, precision=HIGHEST_PRECISION)
    blocks = lax.map(jax.checkpoint(one_block), (queries.reshape(ROW // block_rows, block_rows, HEADS, HD), places.reshape(ROW // block_rows, block_rows)))
    return blocks.reshape(ROW, HEADS, HD)

def expert_ffn(operands):
    inputs, gate_up, down_weight = operands
    gate_part = jnp.einsum('cd,df->cf', inputs, gate_up[0], precision=HIGHEST_PRECISION)
    up_part = jnp.einsum('cd,df->cf', inputs, gate_up[1], precision=HIGHEST_PRECISION)
    both = low_back(jnp.concatenate([gate_part, up_part], axis=-1))
    ff_width = gate_up.shape[-1]
    hidden = low(jax.nn.silu(both[:, :ff_width]) * both[:, ff_width:])
    return low(low_back(jnp.dot(hidden, down_weight, precision=HIGHEST_PRECISION)))

def expert_table(routes):
    block_pairs = routes.reshape(-1, TOK_DEV * TOP)
    block_total = block_pairs.shape[0]
    onehot = (block_pairs[..., None] == jnp.arange(EXPERTS, dtype=jnp.int32)).astype(jnp.int32)
    ranking = lax.optimization_barrier(jnp.sum((jnp.cumsum(onehot, axis=1) - onehot) * onehot, axis=-1))
    slots = (jnp.arange(block_total, dtype=jnp.int32)[:, None] * MOST + ranking).astype(jnp.int32)
    pair_ids = jnp.arange(block_total * TOK_DEV * TOP, dtype=jnp.int32).reshape(block_total, TOK_DEV * TOP)
    table = jnp.full((EXPERTS, block_total * MOST), -1, jnp.int32).at[block_pairs, slots].set(pair_ids)
    return (block_pairs.reshape(-1), slots.reshape(-1), table)

def forward(inputs, gain_rows, dense, router, down, gate_up, expert_down, lengths, routes):
    gain_rows = low(gain_rows)
    dense = low(dense)
    router = low(router)
    down = low(down)
    gate_up = low(gate_up)
    expert_down = low(expert_down)
    places = jnp.arange(ROW)
    valid = (places[None, :] < lengths[:, None]).astype(jnp.float32)
    normed_one = low(normalize(inputs, gain_rows[0]))
    projected = jnp.einsum('rsd,de->rse', normed_one, dense[:, :3 * D], precision=HIGHEST_PRECISION)
    projected = low_back(projected).reshape(ROWS, ROW, 3, HEADS, HD)
    queries = rotate(projected[:, :, 0], places)
    keys_all = rotate(projected[:, :, 1], places)
    stacked = low(jnp.stack([queries, keys_all, projected[:, :, 2]], axis=2))
    attended = lax.map(attend_row, (stacked[:, :, 0], stacked[:, :, 1], stacked[:, :, 2], lengths))
    attended = low(low_back(attended.reshape(ROWS, ROW, D)))
    branch = low_back(jnp.einsum('rsd,de->rse', attended, dense[:, 3 * D:4 * D], precision=HIGHEST_PRECISION))
    middle = inputs + branch
    normed_two = low(normalize(middle, gain_rows[1]))
    flat_h = normed_two.reshape(-1, D)
    logits = low_back(jnp.dot(flat_h, router, precision=HIGHEST_PRECISION))
    chosen = jnp.take_along_axis(logits, routes.reshape(-1, TOP), axis=1)
    gates = jax.nn.softmax(chosen, axis=-1)
    shared = low_back(jnp.dot(flat_h, dense[:, 4 * D:], precision=HIGHEST_PRECISION))
    shared_act = low(jax.nn.silu(shared[:, :FFS]) * shared[:, FFS:])
    shared_out = jnp.dot(shared_act, down, precision=HIGHEST_PRECISION)
    expert_flat, slot_flat, table = expert_table(routes)
    present = table >= 0
    picked = jnp.where(present, table, 0) // TOP
    expert_inputs = low_back(flat_h[picked] * present[..., None].astype(jnp.float32))
    expert_outputs = lax.map(jax.checkpoint(expert_ffn), (expert_inputs, gate_up, expert_down))
    gathered = expert_outputs[expert_flat, slot_flat].reshape(-1, TOP, D)
    mixed = jnp.einsum('nk,nkd->nd', gates, gathered, precision=HIGHEST_PRECISION)
    total = middle + (shared_out + mixed).reshape(ROWS, ROW, D)
    return total * valid[..., None]

def reference(tokens, cotangent, lengths, routes, gains, gain_moms, w_dense, mom_dense, w_router, mom_router, w_down, mom_down, e_gate_up, e_mom_gate_up, e_down, e_mom_down):

    def layer(inputs, gain_rows, dense, router, down, gate_up, expert_down):
        return forward(inputs, gain_rows, dense, router, down, gate_up, expert_down, lengths, routes)
    result, pullback = jax.vjp(layer, tokens.astype(jnp.float32), gains, w_dense, w_router, w_down, e_gate_up, e_down)
    d_tokens, g_gains, g_dense, g_router, g_down, g_gate_up, g_edown = pullback(cotangent.astype(jnp.float32))
    gain_rate = 0.1 / math.sqrt(ROWS * ROW)
    new_gain_moms = GAIN_DECAY * gain_moms + g_gains
    new_gains = gains - gain_rate * new_gain_moms
    new_mom_dense = MUON_DECAY * mom_dense + g_dense
    edges = (0, 3 * D, 4 * D, 4 * D + FFS, 4 * D + 2 * FFS)
    pieces = []
    for number in range(4):
        lower_edge = edges[number]
        upper_edge = edges[number + 1]
        pieces.append(w_dense[:, lower_edge:upper_edge] - DENSE_RATES[number] * orthogonal(new_mom_dense[:, lower_edge:upper_edge]))
    new_dense = jnp.concatenate(pieces, axis=1)
    new_mom_router = MUON_DECAY * mom_router + g_router
    new_router = w_router - ROUTER_RATE * orthogonal(new_mom_router)
    new_mom_down = MUON_DECAY * mom_down + g_down
    new_down = w_down - DOWN_RATE * orthogonal(new_mom_down)
    new_e_mom_gate_up = MUON_DECAY * e_mom_gate_up + g_gate_up
    orth_gate_up = lax.map(lambda moment: jnp.stack([orthogonal(moment[0]), orthogonal(moment[1])]), new_e_mom_gate_up)
    gate_rates = jnp.array(EXPERT_RATES[:2], jnp.float32)[None, :, None, None]
    new_e_gate_up = e_gate_up - gate_rates * orth_gate_up
    new_e_mom_down = MUON_DECAY * e_mom_down + g_edown
    orth_down = lax.map(orthogonal, new_e_mom_down)
    new_e_down = e_down - EXPERT_RATES[2] * orth_down
    return (result.astype(jnp.bfloat16), d_tokens.astype(jnp.bfloat16), new_gain_moms, new_gains, new_mom_dense, new_dense, new_mom_router, new_router, new_mom_down, new_down, new_e_mom_gate_up, new_e_gate_up, new_e_mom_down, new_e_down)
```

```python
import functools
import math

import jax
import jax.numpy as jnp
import numpy as np
from jax import lax
from jax.experimental import pallas as pl
from jax.experimental.pallas import tpu as pltpu
from jax.sharding import PartitionSpec as P

HEADS = 12
NS_STEPS = 5


NORM_EPSILON = 1e-06
POLY_FIRST = 3.4445
POLY_SECOND = -4.775
POLY_THIRD = 2.0315
HIGHEST_PRECISION = lax.Precision.HIGHEST
MASK_VALUE = -1e30
DENSE_RATES = (0.8, 5.0, 0.8, 0.8)
ROUTER_RATE = 0.4
DOWN_RATE = 0.5
EXPERT_RATES = (0.8, 0.8, 0.5)
GAIN_DECAY = 0.9
MUON_DECAY = 0.5


def bf_dot(left, right):
    return jnp.dot(left, right, preferred_element_type=jnp.float32)


def first_dot(left, right, precision=None):
    return lax.dot_general(
        left,
        right,
        (((0,), (0,)), ((), ())),
        precision=precision,
        preferred_element_type=jnp.float32,
    )


def last_dot(left, right, precision=None):
    return lax.dot_general(
        left,
        right,
        (((1,), (1,)), ((), ())),
        precision=precision,
        preferred_element_type=jnp.float32,
    )


def statistics(values):
    inverse = lax.rsqrt(jnp.mean(values * values, axis=-1, keepdims=True) + NORM_EPSILON)
    return (values * inverse, inverse)


def norm_back(grad_out, scaled, inverse, gain_row):
    gain_grad = jnp.sum(grad_out * scaled, axis=(0, 1))
    through = grad_out * gain_row
    grad_in = inverse * (through - scaled * jnp.mean(through * scaled, axis=-1, keepdims=True))
    return (grad_in, gain_grad)


def rotation_tables(head_size, places):
    half_size = head_size // 2
    frequency = 10000.0 ** (-2.0 * jnp.arange(half_size, dtype=jnp.float32) / head_size)
    angles = places.astype(jnp.float32)[:, None] * frequency[None, :]
    return (jnp.cos(angles)[:, None, :], jnp.sin(angles)[:, None, :], half_size)


def rotate(values, places):
    cosine, sine, half_size = rotation_tables(values.shape[-1], places)
    first_half = values[..., :half_size]
    second_half = values[..., half_size:]
    return jnp.concatenate(
        [first_half * cosine - second_half * sine, second_half * cosine + first_half * sine],
        axis=-1,
    )


def rotate_back(grads, places):
    cosine, sine, half_size = rotation_tables(grads.shape[-1], places)
    first_half = grads[..., :half_size]
    second_half = grads[..., half_size:]
    return jnp.concatenate(
        [first_half * cosine + second_half * sine, second_half * cosine - first_half * sine],
        axis=-1,
    )


def silu_slope(values):
    logistic = jax.nn.sigmoid(values)
    return logistic * (1.0 + values * (1.0 - logistic))


def orthogonal(matrix):
    if matrix.shape[0] > matrix.shape[1]:
        return orthogonal(matrix.T).T
    current = matrix / (jnp.sqrt(jnp.sum(matrix * matrix)) + 1e-07)

    def sweep(_, current):
        gram = jnp.dot(current, current.T, precision=HIGHEST_PRECISION)
        poly = POLY_SECOND * gram + POLY_THIRD * jnp.dot(gram, gram, precision=HIGHEST_PRECISION)
        return POLY_FIRST * current + jnp.dot(poly, current, precision=HIGHEST_PRECISION)

    return lax.fori_loop(0, NS_STEPS, sweep, current)


def general_plan(
    tokens,
    cotangent,
    lengths,
    routes,
    gains,
    gain_moms,
    w_dense,
    mom_dense,
    w_router,
    mom_router,
    w_down,
    mom_down,
    e_gate_up,
    e_mom_gate_up,
    e_down,
    e_mom_down,
):
    seq_rows, local_len, width = tokens.shape
    head_count = HEADS
    head_size = width // head_count
    seq_parts = lax.axis_size("fsdp")
    seq_index = lax.axis_index("fsdp")
    row_len = local_len * seq_parts
    expert_count = w_router.shape[1]
    top_count = routes.shape[2]
    most_rows = 2 * local_len * top_count // expert_count
    capacity = seq_rows * most_rows
    places = seq_index * local_len + jnp.arange(local_len)
    valid = (places[None, :] < lengths[:, None]).astype(jnp.float32)
    dense_copy, router_copy, down_copy, gain_copy = (
        lax.all_gather(w_dense.astype(jnp.bfloat16), ("dp", "fsdp"), axis=0, tiled=True),
        lax.all_gather(w_router.astype(jnp.bfloat16), ("dp", "fsdp"), axis=0, tiled=True),
        lax.all_gather(w_down.astype(jnp.bfloat16), ("dp", "fsdp"), axis=0, tiled=True),
        lax.all_gather(gains.astype(jnp.bfloat16), ("dp", "fsdp"), axis=1, tiled=True),
    )
    gate_up_copy, edown_copy = (
        lax.all_gather(e_gate_up.astype(jnp.bfloat16), "dp", axis=2, tiled=True),
        lax.all_gather(e_down.astype(jnp.bfloat16), "dp", axis=1, tiled=True),
    )
    gain_one = gain_copy[0].astype(jnp.float32)
    gain_two = gain_copy[1].astype(jnp.float32)
    ff_shared = down_copy.shape[0]
    gate_weight = gate_up_copy[0, 0]
    up_weight = gate_up_copy[0, 1]
    down_weight = edown_copy[0]
    ff_width = gate_weight.shape[1]
    inputs = tokens.astype(jnp.float32)
    scaled_one, inverse_one = statistics(inputs)
    normed_one = (scaled_one * gain_one).astype(jnp.bfloat16).reshape(-1, width)
    projected = bf_dot(normed_one, dense_copy[:, : 3 * width]).reshape(
        seq_rows, local_len, 3, head_count, head_size
    )
    queries = rotate(projected[:, :, 0], places).astype(jnp.bfloat16)
    keys_local = rotate(projected[:, :, 1], places).astype(jnp.bfloat16)
    values_local = projected[:, :, 2].astype(jnp.bfloat16)
    keys_all, values_all = (
        lax.all_gather(keys_local, "fsdp", axis=1, tiled=True),
        lax.all_gather(values_local, "fsdp", axis=1, tiled=True),
    )
    block_len = min(512, row_len)
    block_count = row_len // block_len
    stat_shape = (seq_rows, head_count, local_len)
    head_shape = (seq_rows, local_len, head_count, head_size)

    def masked_scores(query_part, query_places, key_part, key_places):
        raw_scores = (
            jnp.einsum("rqhd,rkhd->rhqk", query_part, key_part, preferred_element_type=jnp.float32)
            * 0.125
        )
        allowed = (key_places[None, None, :] <= query_places[None, :, None]) & (
            key_places[None, None, :] < lengths[:, None, None]
        )
        return jnp.where(allowed[:, None], raw_scores, MASK_VALUE)

    def key_block(index):
        start_at = index * block_len
        key_part = lax.dynamic_slice_in_dim(keys_all, start_at, block_len, 1)
        value_part = lax.dynamic_slice_in_dim(values_all, start_at, block_len, 1)
        return (key_part, value_part, start_at + jnp.arange(block_len))

    def running_max(carry, index):
        top_score, exp_total = carry
        key_part, value_part, key_places = key_block(index)
        scores = masked_scores(queries, places, key_part, key_places)
        new_top = jnp.maximum(top_score, jnp.max(scores, axis=-1))
        exp_total = exp_total * jnp.exp(top_score - new_top) + jnp.sum(
            jnp.exp(scores - new_top[..., None]), axis=-1
        )
        return ((new_top, exp_total), None)

    start_stats = (
        jnp.full(stat_shape, MASK_VALUE, jnp.float32),
        jnp.zeros(stat_shape, jnp.float32),
    )
    (top_score, exp_total), _ = lax.scan(running_max, start_stats, jnp.arange(block_count))
    log_total = top_score + jnp.log(exp_total)

    def weigh_values(total_acc, index):
        key_part, value_part, key_places = key_block(index)
        scores = masked_scores(queries, places, key_part, key_places)
        weights = jnp.exp(scores - log_total[..., None]).astype(jnp.bfloat16)
        return (
            total_acc
            + jnp.einsum(
                "rhqk,rkhd->rqhd", weights, value_part, preferred_element_type=jnp.float32
            ),
            None,
        )

    attended, _ = lax.scan(
        weigh_values, jnp.zeros(head_shape, jnp.float32), jnp.arange(block_count)
    )
    attended_copy = attended.reshape(-1, width).astype(jnp.bfloat16)
    branch = bf_dot(attended_copy, dense_copy[:, 3 * width : 4 * width]).reshape(
        seq_rows, local_len, width
    )
    middle = inputs + branch
    scaled_two, inverse_two = statistics(middle)
    normed_two = (scaled_two * gain_two).astype(jnp.bfloat16).reshape(-1, width)
    logits = bf_dot(normed_two, router_copy)
    route_rows = routes.reshape(-1, top_count)
    chosen = jnp.take_along_axis(logits, route_rows, axis=1)
    gates = jax.nn.softmax(chosen, axis=-1)
    shared_pre = bf_dot(normed_two, dense_copy[:, 4 * width :])
    shared_gate = shared_pre[:, :ff_shared]
    shared_up = shared_pre[:, ff_shared:]
    shared_act = (jax.nn.silu(shared_gate) * shared_up).astype(jnp.bfloat16)
    shared_out = bf_dot(shared_act, down_copy)
    pair_experts = routes.reshape(seq_rows, local_len * top_count)
    onehot = (pair_experts[..., None] == jnp.arange(expert_count, dtype=jnp.int32)).astype(
        jnp.int32
    )
    ranking = jnp.sum((jnp.cumsum(onehot, axis=1) - onehot) * onehot, axis=-1)
    slot_local = (jnp.arange(seq_rows, dtype=jnp.int32)[:, None] * most_rows + ranking).reshape(-1)
    slot_ids = pair_experts.reshape(-1) * capacity + slot_local
    pair_count = seq_rows * local_len * top_count
    table = (
        jnp.full((expert_count * capacity,), -1, jnp.int32)
        .at[slot_ids]
        .set(jnp.arange(pair_count, dtype=jnp.int32))
    )
    present = table >= 0
    picked = jnp.where(present, table, 0)
    outgoing = jnp.where(
        present[:, None], normed_two[picked // top_count], jnp.zeros((), jnp.bfloat16)
    ).reshape(expert_count, capacity, width)
    arrived = lax.all_to_all(outgoing, "fsdp", split_axis=0, concat_axis=0, tiled=True)
    sources, item_count, _ = arrived.shape
    arrived_rows = arrived.reshape(sources * item_count, width)
    pre_act = jnp.concatenate(
        [bf_dot(arrived_rows, gate_weight), bf_dot(arrived_rows, up_weight)], axis=-1
    )
    activated = (jax.nn.silu(pre_act[:, :ff_width]) * pre_act[:, ff_width:]).astype(jnp.bfloat16)
    result = bf_dot(activated, down_weight).astype(jnp.bfloat16).reshape(sources, item_count, width)
    returned_rows = lax.all_to_all(result, "fsdp", split_axis=0, concat_axis=0, tiled=True)
    pre_all = pre_act.reshape(sources, item_count, 2 * ff_width)
    pair_out = (
        returned_rows.reshape(expert_count * capacity, width)[slot_ids]
        .reshape(-1, top_count, width)
        .astype(jnp.float32)
    )
    mixed = jnp.sum(gates[..., None] * pair_out, axis=1)
    total = middle + (shared_out + mixed).reshape(seq_rows, local_len, width)
    output = (total * valid[..., None]).astype(jnp.bfloat16)
    d_out = cotangent.astype(jnp.float32) * valid[..., None]
    d_flat = d_out.reshape(-1, width)
    d_flat_copy = d_flat.astype(jnp.bfloat16)
    grad_down = first_dot(shared_act, d_flat_copy)
    d_sact = last_dot(d_flat_copy, down_copy)
    d_shared = jnp.concatenate(
        [d_sact * shared_up * silu_slope(shared_gate), d_sact * jax.nn.silu(shared_gate)], axis=-1
    ).astype(jnp.bfloat16)
    grad_shared = first_dot(normed_two, d_shared)
    d_normed = last_dot(d_shared, dense_copy[:, 4 * width :])
    d_gates = jnp.sum(d_flat[:, None, :] * pair_out, axis=-1)
    d_chosen = gates * (d_gates - jnp.sum(gates * d_gates, axis=-1, keepdims=True))
    route_table = (route_rows[..., None] == jnp.arange(expert_count, dtype=jnp.int32)).astype(
        jnp.float32
    )
    d_logits = jnp.sum(d_chosen[..., None] * route_table, axis=1).astype(jnp.bfloat16)
    grad_router = first_dot(normed_two, d_logits)
    d_normed = d_normed + last_dot(d_logits, router_copy)
    d_pairs = (gates[..., None] * d_flat[:, None, :]).reshape(-1, width).astype(jnp.bfloat16)
    d_outgoing = jnp.where(present[:, None], d_pairs[picked], jnp.zeros((), jnp.bfloat16)).reshape(
        expert_count, capacity, width
    )
    d_arrived = lax.all_to_all(d_outgoing, "fsdp", split_axis=0, concat_axis=0, tiled=True)
    d_result = d_arrived.reshape(-1, width)
    pre_rows = pre_all.reshape(-1, 2 * ff_width)
    expert_gate = pre_rows[:, :ff_width]
    expert_up = pre_rows[:, ff_width:]
    activated = (jax.nn.silu(expert_gate) * expert_up).astype(jnp.bfloat16)
    grad_edown = first_dot(activated, d_result)
    d_activated = last_dot(d_result, down_weight)
    d_pre = jnp.concatenate(
        [d_activated * expert_up * silu_slope(expert_gate), d_activated * jax.nn.silu(expert_gate)],
        axis=-1,
    ).astype(jnp.bfloat16)
    arrived_rows = arrived.reshape(-1, width)
    grad_gate = first_dot(arrived_rows, d_pre[:, :ff_width])
    grad_up = first_dot(arrived_rows, d_pre[:, ff_width:])
    d_inputs = (
        (last_dot(d_pre[:, :ff_width], gate_weight) + last_dot(d_pre[:, ff_width:], up_weight))
        .astype(jnp.bfloat16)
        .reshape(d_arrived.shape)
    )
    d_returned = lax.all_to_all(d_inputs, "fsdp", split_axis=0, concat_axis=0, tiled=True).reshape(
        expert_count * capacity, width
    )
    d_normed = d_normed + jnp.sum(
        d_returned[slot_ids].astype(jnp.float32).reshape(-1, top_count, width), axis=1
    )
    d_mid_norm, grad_gain_two = norm_back(
        d_normed.reshape(seq_rows, local_len, width), scaled_two, inverse_two, gain_two
    )
    d_middle = d_out + d_mid_norm
    d_branch = d_middle.reshape(-1, width).astype(jnp.bfloat16)
    grad_wout = first_dot(attended_copy, d_branch)
    d_attended = (
        last_dot(d_branch, dense_copy[:, 3 * width : 4 * width])
        .reshape(head_shape)
        .astype(jnp.bfloat16)
    )

    def delta_pass(delta_acc, index):
        key_part, value_part, key_places = key_block(index)
        weights = jnp.exp(
            masked_scores(queries, places, key_part, key_places) - log_total[..., None]
        )
        slopes = jnp.einsum(
            "rqhd,rkhd->rhqk", d_attended, value_part, preferred_element_type=jnp.float32
        )
        return (delta_acc + jnp.sum(weights * slopes, axis=-1), None)

    delta, _ = lax.scan(delta_pass, jnp.zeros(stat_shape, jnp.float32), jnp.arange(block_count))

    def make_pass():

        def query_pass(query_acc, index):
            key_part, value_part, key_places = key_block(index)
            weights = jnp.exp(
                masked_scores(queries, places, key_part, key_places) - log_total[..., None]
            )
            slopes = jnp.einsum(
                "rqhd,rkhd->rhqk", d_attended, value_part, preferred_element_type=jnp.float32
            )
            score_grad = (weights * (slopes - delta[..., None])).astype(jnp.bfloat16)
            query_acc = query_acc + 0.125 * jnp.einsum(
                "rhqk,rkhd->rqhd", score_grad, key_part, preferred_element_type=jnp.float32
            )
            key_grad = 0.125 * jnp.einsum(
                "rhqk,rqhd->rkhd", score_grad, queries, preferred_element_type=jnp.float32
            )
            value_grad = jnp.einsum(
                "rhqk,rqhd->rkhd",
                weights.astype(jnp.bfloat16),
                d_attended,
                preferred_element_type=jnp.float32,
            )
            return (query_acc, (key_grad, value_grad))

        return query_pass

    d_query, (key_parts, value_parts) = lax.scan(
        make_pass(), jnp.zeros(head_shape, jnp.float32), jnp.arange(block_count)
    )
    key_whole = jnp.moveaxis(key_parts, 0, 1).reshape(seq_rows, row_len, width)
    value_whole = jnp.moveaxis(value_parts, 0, 1).reshape(seq_rows, row_len, width)
    key_value = lax.psum_scatter(
        jnp.concatenate([key_whole, value_whole], axis=-1), "fsdp", scatter_dimension=1, tiled=True
    )
    d_key = key_value[..., :width].reshape(head_shape)
    d_value = key_value[..., width:].reshape(head_shape)
    d_qkv = (
        jnp.stack([rotate_back(d_query, places), rotate_back(d_key, places), d_value], axis=2)
        .reshape(-1, 3 * width)
        .astype(jnp.bfloat16)
    )
    grad_qkv = first_dot(normed_one, d_qkv)
    d_one = last_dot(d_qkv, dense_copy[:, : 3 * width]).reshape(seq_rows, local_len, width)
    d_in_norm, grad_gain_one = norm_back(d_one, scaled_one, inverse_one, gain_one)
    d_tokens = (d_middle + d_in_norm).astype(jnp.bfloat16)
    grad_dense = jnp.concatenate([grad_qkv, grad_wout, grad_shared], axis=1)
    grad_gains = jnp.stack([grad_gain_one, grad_gain_two])
    part_dense, part_router, part_down, part_gains = (
        lax.psum_scatter(grad_dense, ("dp", "fsdp"), scatter_dimension=0, tiled=True),
        lax.psum_scatter(grad_router, ("dp", "fsdp"), scatter_dimension=0, tiled=True),
        lax.psum_scatter(grad_down, ("dp", "fsdp"), scatter_dimension=0, tiled=True),
        lax.psum_scatter(grad_gains, ("dp", "fsdp"), scatter_dimension=1, tiled=True),
    )
    total_slots = seq_rows * lax.axis_size("dp") * row_len
    gain_rate = 0.1 / math.sqrt(total_slots)
    new_gain_moms = GAIN_DECAY * gain_moms + part_gains
    new_gains = gains - gain_rate * new_gain_moms
    new_mom_dense = MUON_DECAY * mom_dense + part_dense
    new_mom_router = MUON_DECAY * mom_router + part_router
    new_mom_down = MUON_DECAY * mom_down + part_down
    device_index = lax.axis_index(("dp", "fsdp"))
    device_count = lax.axis_size(("dp", "fsdp"))
    owners = [number * device_count // 6 for number in range(6)]

    def owned(number, matrix):
        return lax.cond(device_index == owners[number], orthogonal, jnp.zeros_like, matrix)

    edges = (0, 3 * width, 4 * width, 4 * width + ff_shared, 4 * width + 2 * ff_shared)
    whole_dense, whole_router, whole_down = (
        lax.all_gather(new_mom_dense, ("dp", "fsdp"), axis=0, tiled=True),
        lax.all_gather(new_mom_router, ("dp", "fsdp"), axis=0, tiled=True),
        lax.all_gather(new_mom_down, ("dp", "fsdp"), axis=0, tiled=True),
    )
    orth_dense = jnp.concatenate(
        [owned(number, whole_dense[:, edges[number] : edges[number + 1]]) for number in range(4)],
        axis=1,
    )
    orth_router = owned(4, whole_router)
    orth_down = owned(5, whole_down)
    share_dense, share_router, share_down = (
        lax.psum_scatter(orth_dense, ("dp", "fsdp"), scatter_dimension=0, tiled=True),
        lax.psum_scatter(orth_router, ("dp", "fsdp"), scatter_dimension=0, tiled=True),
        lax.psum_scatter(orth_down, ("dp", "fsdp"), scatter_dimension=0, tiled=True),
    )
    column_rates = jnp.concatenate(
        [
            jnp.full((edges[number + 1] - edges[number],), DENSE_RATES[number], jnp.float32)
            for number in range(4)
        ]
    )
    new_dense = w_dense - column_rates[None, :] * share_dense
    new_router = w_router - ROUTER_RATE * share_router
    new_down = w_down - DOWN_RATE * share_down
    dp_index = lax.axis_index("dp")
    gate_rows = e_gate_up.shape[2]
    down_rows = e_down.shape[1]
    gate_term = jnp.stack([grad_gate, grad_up])[None] + lax.dynamic_update_slice(
        jnp.zeros((1, 2, width, ff_width), jnp.float32),
        MUON_DECAY * e_mom_gate_up,
        (0, 0, dp_index * gate_rows, 0),
    )
    down_term = grad_edown[None] + lax.dynamic_update_slice(
        jnp.zeros((1, ff_width, width), jnp.float32),
        MUON_DECAY * e_mom_down,
        (0, dp_index * down_rows, 0),
    )
    whole_gate_up, whole_edown = lax.psum((gate_term, down_term), "dp")
    orth_gate_up = jnp.stack([orthogonal(whole_gate_up[0, 0]), orthogonal(whole_gate_up[0, 1])])[
        None
    ]
    orth_edown = orthogonal(whole_edown[0])[None]
    new_e_mom_gate_up = lax.dynamic_slice_in_dim(whole_gate_up, dp_index * gate_rows, gate_rows, 2)
    gate_rates = jnp.array(EXPERT_RATES[:2], jnp.float32)[None, :, None, None]
    new_e_gate_up = e_gate_up - gate_rates * lax.dynamic_slice_in_dim(
        orth_gate_up, dp_index * gate_rows, gate_rows, 2
    )
    new_e_mom_down = lax.dynamic_slice_in_dim(whole_edown, dp_index * down_rows, down_rows, 1)
    new_e_down = e_down - EXPERT_RATES[2] * lax.dynamic_slice_in_dim(
        orth_edown, dp_index * down_rows, down_rows, 1
    )
    return (
        output,
        d_tokens,
        new_gain_moms,
        new_gains,
        new_mom_dense,
        new_dense,
        new_mom_router,
        new_router,
        new_mom_down,
        new_down,
        new_e_mom_gate_up,
        new_e_gate_up,
        new_e_mom_down,
        new_e_down,
    )


DP = 8
FS = 4
AXES = ("dp", "fsdp")
LANES = 128
SEQUENCES = 2
VMEM_BYTES = 60 * 2**20
LINE = 4
OWNERS = ((0, 3, 4, 7), (1, 2, 5, 6), (0, 3, 4, 7), (1, 2, 5, 6, 4))
TALL_SLOTS = (3, 4)
DOWN_COLUMN = 3


def tn_dot(left, right):
    return lax.dot_general(
        left, right, (((0,), (0,)), ((), ())), preferred_element_type=jnp.float32
    )


def nt_dot(left, right):
    return lax.dot_general(
        left, right, (((1,), (1,)), ((), ())), preferred_element_type=jnp.float32
    )


def kernel_call(body, out_shape, flops, bytes_accessed, **options):
    return pl.pallas_call(
        body,
        out_shape=out_shape,
        compiler_params=pltpu.CompilerParams(vmem_limit_bytes=VMEM_BYTES),
        cost_estimate=pl.CostEstimate(
            flops=int(flops), bytes_accessed=int(bytes_accessed), transcendentals=0
        ),
        **options,
    )


def shape_of(shape, dtype=jnp.bfloat16):
    return jax.ShapeDtypeStruct(shape, dtype)


def whole_block(shape):
    return pl.BlockSpec(shape, lambda *_: (0,) * len(shape))


def after(value, *events):
    return lax.optimization_barrier((value,) + events)[0]


def fsdp_hop(value, step):
    pairs = [(d * FS + f, d * FS + (f ^ step)) for d in range(DP) for f in range(FS)]
    return lax.ppermute(value, AXES, pairs)


def by_source(own, near, far, cross, index):
    low_x, even = index < 2, index % 2 == 0
    own_low, own_high = jnp.where(low_x, own, far), jnp.where(low_x, far, own)
    near_low, near_high = jnp.where(low_x, near, cross), jnp.where(low_x, cross, near)
    return [
        jnp.where(even, own_low, near_low),
        jnp.where(even, near_low, own_low),
        jnp.where(even, own_high, near_high),
        jnp.where(even, near_high, own_high),
    ]


def gather_fsdp(block, index):
    far = fsdp_hop(block, 2)
    near = fsdp_hop(block, 1)
    cross = fsdp_hop(far, 1)
    return by_source(block, near, far, cross, index)


def exchange_fsdp(blocks, index):
    pick = lambda step: lax.dynamic_index_in_dim(blocks, index ^ step, 0, keepdims=False)
    got = [pick(0)] + [fsdp_hop(pick(step), step) for step in (1, 2, 3)]
    return by_source(*got, index)


class FsdpSum:
    def __init__(self, keep, send, index):
        self.place, self.keep = index // 2, keep
        self.near = fsdp_hop(send, 1)

    def cross(self):
        both = self.keep.astype(jnp.float32) + self.near.astype(jnp.float32)
        away = lax.dynamic_index_in_dim(both, 1 - self.place, 0, keepdims=False)
        self.here = lax.dynamic_index_in_dim(both, self.place, 0, keepdims=False)
        self.far = fsdp_hop(away.astype(self.keep.dtype), 2)
        return self

    def last(self):
        return self.here + self.far.astype(jnp.float32)


def by_core(blocks, index, *events):
    if events:
        blocks = after(blocks, *events)
    pairs, core = blocks.reshape((2, 2) + blocks.shape[1:]), index % 2
    return [lax.dynamic_index_in_dim(pairs, c, 1, keepdims=False) for c in (core, 1 - core)]


def sum_everywhere(value):
    for d_step, f_step in ((0, 1), (0, 2), (1, 0), (2, 0), (4, 0)):
        pairs = [
            (d * FS + f, (d ^ d_step) * FS + (f ^ f_step)) for d in range(DP) for f in range(FS)
        ]
        value = value + lax.ppermute(value, AXES, pairs)
    return value


def swap_halves(values, half_size):
    width = values.shape[1]
    lane = lax.broadcasted_iota(jnp.int32, values.shape, 1)
    return jnp.where(
        lane % (2 * half_size) < half_size,
        -pltpu.roll(values, width - half_size, 1),
        pltpu.roll(values, half_size, 1),
    )


def attention_body(
    lengths_ref, x_ref, gain_ref, w_ref, cos_ref, sin_ref, normed_ref, qkv_ref, prob_ref, att_ref
):
    head_count, row_len = prob_ref.shape[1], prob_ref.shape[2]
    wide = w_ref.shape[1] // 3
    head_size = wide // head_count
    x = x_ref[0].astype(jnp.float32)
    inverse = lax.rsqrt(jnp.mean(x * x, axis=-1, keepdims=True) + NORM_EPSILON)
    normed = (x * inverse * gain_ref[...]).astype(jnp.bfloat16)
    normed_ref[...] = normed.T
    projected = jnp.dot(normed, w_ref[...], preferred_element_type=jnp.float32)
    both = projected[:, : 2 * wide]
    both = both * cos_ref[...] + swap_halves(both, head_size // 2) * sin_ref[...]
    both = both.astype(jnp.bfloat16)
    values = projected[:, 2 * wide :].astype(jnp.bfloat16)
    qkv_ref[0, :, : 2 * wide] = both
    qkv_ref[0, :, 2 * wide :] = values
    length = lengths_ref[pl.program_id(0)]
    row = lax.broadcasted_iota(jnp.int32, (row_len, row_len), 0)
    column = lax.broadcasted_iota(jnp.int32, (row_len, row_len), 1)
    allowed = (column <= row) & (column < length)
    parts = []
    for head in range(head_count):
        span = slice(head * head_size, (head + 1) * head_size)
        scores = nt_dot(both[:, span], both[:, wide:][:, span]) * 0.125
        scores = jnp.where(allowed, scores, MASK_VALUE)
        weights = jnp.exp(scores - jnp.max(scores, axis=-1, keepdims=True))
        share = 1.0 / jnp.sum(weights, axis=-1, keepdims=True)
        probs = (weights * share).astype(jnp.bfloat16)
        prob_ref[0, head] = probs
        parts.append(jnp.dot(probs, values[:, span], preferred_element_type=jnp.float32))
    att_ref[0] = jnp.concatenate(parts, axis=1).astype(jnp.bfloat16)


def attention_forward(x, gain, weight, cosine, sine, lengths):
    rows, row_len, width = x.shape
    columns = weight.shape[1]
    heads = columns // 3 // (width // HEADS)
    return kernel_call(
        attention_body,
        (
            shape_of((width, rows * row_len)),
            shape_of((rows, row_len, columns)),
            shape_of((rows, heads, row_len, row_len)),
            shape_of((rows, row_len, columns // 3)),
        ),
        6e9,
        12e6,
        grid=(rows,),
        in_specs=[
            pl.BlockSpec(memory_space=pltpu.SMEM),
            pl.BlockSpec((1, row_len, width), lambda r: (r, 0, 0)),
            whole_block(gain.shape),
            whole_block(weight.shape),
            whole_block(cosine.shape),
            whole_block(sine.shape),
        ],
        out_specs=(
            pl.BlockSpec((width, row_len), lambda r: (0, r)),
            pl.BlockSpec((1, row_len, columns), lambda r: (r, 0, 0)),
            pl.BlockSpec((1, heads, row_len, row_len), lambda r: (r, 0, 0, 0)),
            pl.BlockSpec((1, row_len, columns // 3), lambda r: (r, 0, 0)),
        ),
        name="attention_forward",
    )(lengths, x, gain, weight, cosine, sine)


def attention_back_body(
    normed_ref, qkv_ref, prob_ref, d_att_ref, w_ref, cos_ref, sin_ref, grad_ref, back_ref, total
):
    head_count = prob_ref.shape[1]
    wide = w_ref.shape[1] // 3
    head_size = wide // head_count
    qkv = qkv_ref[0]
    d_att = d_att_ref[0]
    grads = ([], [], [])
    for head in range(head_count):
        span = slice(head * head_size, (head + 1) * head_size)
        query, key, value = (qkv[:, i * wide : (i + 1) * wide][:, span] for i in range(3))
        probs = prob_ref[0, head]
        weights = probs.astype(jnp.float32)
        slopes = nt_dot(d_att[:, span], value)
        delta = jnp.sum(weights * slopes, axis=-1, keepdims=True)
        d_scores = (weights * (slopes - delta)).astype(jnp.bfloat16)
        grads[0].append(0.125 * jnp.dot(d_scores, key, preferred_element_type=jnp.float32))
        grads[1].append(0.125 * tn_dot(d_scores, query))
        grads[2].append(tn_dot(probs, d_att[:, span]))
    both = jnp.concatenate(grads[0] + grads[1], axis=1)
    both = both * cos_ref[...] - swap_halves(both, head_size // 2) * sin_ref[...]
    d_qkv = jnp.concatenate([both] + grads[2], axis=1).astype(jnp.bfloat16)
    grad = jnp.dot(normed_ref[...], d_qkv, preferred_element_type=jnp.float32)

    @pl.when(pl.program_id(0) == 0)
    def _():
        total[...] = grad

    @pl.when(pl.program_id(0) > 0)
    def _():
        total[...] += grad

    grad_ref[...] = total[...].astype(jnp.bfloat16)
    back_ref[0] = nt_dot(d_qkv, w_ref[...]).astype(jnp.bfloat16)


def attention_backward(normed, qkv, probs, d_att, weight, cosine, sine):
    rows, row_len, columns = qkv.shape
    width, heads = weight.shape[0], probs.shape[1]
    return kernel_call(
        attention_back_body,
        (shape_of((width, columns)), shape_of((rows, row_len, width))),
        8e9,
        12e6,
        grid=(rows,),
        in_specs=[
            pl.BlockSpec((width, row_len), lambda r: (0, r)),
            pl.BlockSpec((1, row_len, columns), lambda r: (r, 0, 0)),
            pl.BlockSpec((1, heads, row_len, row_len), lambda r: (r, 0, 0, 0)),
            pl.BlockSpec((1, row_len, columns // 3), lambda r: (r, 0, 0)),
            whole_block(weight.shape),
            whole_block(cosine.shape),
            whole_block(sine.shape),
        ],
        out_specs=(
            whole_block((width, columns)),
            pl.BlockSpec((1, row_len, width), lambda r: (r, 0, 0)),
        ),
        scratch_shapes=[pltpu.VMEM((width, columns), jnp.float32)],
        name="attention_backward",
    )(normed, qkv, probs, d_att, weight, cosine, sine)


def middle_body(
    att_ref, x_ref, routes_ref, wout_ref, router_ref, gain_ref, mid_ref, normed_ref, turned_ref, gates_ref
):
    branch = jnp.dot(att_ref[...], wout_ref[...], preferred_element_type=jnp.float32)
    mid = x_ref[...].astype(jnp.float32) + branch
    inverse = lax.rsqrt(jnp.mean(mid * mid, axis=-1, keepdims=True) + NORM_EPSILON)
    normed = (mid * inverse * gain_ref[...]).astype(jnp.bfloat16)
    logits = jnp.dot(normed, router_ref[...], preferred_element_type=jnp.float32)
    lane = lax.broadcasted_iota(jnp.int32, logits.shape, 1)
    first, second = lane == routes_ref[:, 0:1], lane == routes_ref[:, 1:2]
    one = jnp.sum(jnp.where(first, logits, 0.0), axis=-1, keepdims=True)
    two = jnp.sum(jnp.where(second, logits, 0.0), axis=-1, keepdims=True)
    top = jnp.maximum(one, two)
    one, two = jnp.exp(one - top), jnp.exp(two - top)
    share = 1.0 / (one + two)
    mid_ref[...] = mid
    normed_ref[...] = normed
    turned_ref[...] = normed.T
    gates_ref[...] = jnp.where(first, one * share, 0.0) + jnp.where(second, two * share, 0.0)


def middle_forward(attended, x, routes, wout, router, gain):
    count, width = x.shape
    tile = min(256, count)
    rows = lambda i: (i, 0)
    return kernel_call(
        middle_body,
        (
            shape_of((count, width), jnp.float32),
            shape_of((count, width)),
            shape_of((width, count)),
            shape_of((count, LANES), jnp.float32),
        ),
        2 * count * width * width,
        12e6,
        grid=(count // tile,),
        in_specs=[
            pl.BlockSpec((tile, width), rows),
            pl.BlockSpec((tile, width), rows),
            pl.BlockSpec((tile, routes.shape[1]), rows),
            whole_block(wout.shape),
            whole_block(router.shape),
            whole_block(gain.shape),
        ],
        out_specs=(
            pl.BlockSpec((tile, width), rows),
            pl.BlockSpec((tile, width), rows),
            pl.BlockSpec((width, tile), lambda i: (0, i)),
            pl.BlockSpec((tile, LANES), rows),
        ),
        name="middle_forward",
    )(attended, x, routes, wout, router, gain)


def middle_back_body(
    index_ref, mid_ref, d_out_ref, d_sum_ref, gates_ref, routes_ref, att_ref, normed_ref, wout_ref, router_ref,
    gain_ref, d_mid_ref, grad_wout_ref, grad_router_ref, grad_gain_ref, *d_att_refs,
):
    width = mid_ref.shape[1]
    gates = gates_ref[...]
    lane = lax.broadcasted_iota(jnp.int32, gates.shape, 1)
    half = LANES // 2
    first, second = routes_ref[:, 0:1], routes_ref[:, 1:2]
    slopes = d_sum_ref[:, width:]

    def pick(table, place):
        return jnp.sum(jnp.where(lane == place, table, 0.0), axis=-1, keepdims=True)

    gate_one, gate_two = pick(gates, first), pick(gates, second)
    slope_one = pick(slopes, first) + pick(slopes, first + half)
    slope_two = pick(slopes, second) + pick(slopes, second + half)
    common = gate_one * slope_one + gate_two * slope_two
    d_logits = jnp.where(lane == first, gate_one * (slope_one - common), 0.0)
    d_logits = d_logits + jnp.where(lane == second, gate_two * (slope_two - common), 0.0)
    d_logits = d_logits.astype(jnp.bfloat16)
    grad_router_ref[...] = tn_dot(d_logits, normed_ref[...])
    d_normed = d_sum_ref[:, :width] + nt_dot(d_logits, router_ref[...])
    mid = mid_ref[...]
    inverse = lax.rsqrt(jnp.mean(mid * mid, axis=-1, keepdims=True) + NORM_EPSILON)
    scaled = mid * inverse
    grad_gain_ref[...] = jnp.sum(d_normed * scaled, axis=0, keepdims=True)
    through = d_normed * gain_ref[...]
    d_norm = inverse * (through - scaled * jnp.mean(through * scaled, axis=-1, keepdims=True))
    d_mid = d_out_ref[...].astype(jnp.float32) + d_norm
    d_mid_ref[...] = d_mid
    d_branch = d_mid.astype(jnp.bfloat16)
    grad_wout_ref[...] = tn_dot(att_ref[...], d_branch).astype(jnp.bfloat16)
    d_att = nt_dot(d_branch, wout_ref[...]).astype(jnp.bfloat16)
    quarter = width // FS
    for f in range(FS):
        for step, d_att_ref in enumerate(d_att_refs):

            @pl.when(index_ref[0] == f ^ step)
            def _():
                d_att_ref[...] = d_att[:, f * quarter : (f + 1) * quarter]


def middle_backward(index, *operands):
    count, width = operands[0].shape
    vmem = pl.BlockSpec(memory_space=pltpu.VMEM)
    return kernel_call(
        middle_back_body,
        [
            shape_of((count, width), jnp.float32),
            shape_of((width, width)),
            shape_of((LANES, width), jnp.float32),
            shape_of((1, width), jnp.float32),
        ]
        + [shape_of((count, width // FS))] * FS,
        4 * count * width * width,
        8e6,
        in_specs=[pl.BlockSpec(memory_space=pltpu.SMEM)] + [vmem] * len(operands),
        name="middle_backward",
    )(index, *operands)


def branch_step(normed_ref, turned_ref, d_out_ref, gate_column, weights, grads):
    both_weight, down_weight = weights
    tile = down_weight.shape[0]
    normed, d_out = normed_ref[...], d_out_ref[...]
    both = jnp.dot(normed, both_weight, preferred_element_type=jnp.float32)
    gate, up = both[:, :tile], both[:, tile:]
    slope = nt_dot(d_out, down_weight)
    logistic = 1.0 / (1.0 + jnp.exp(-gate))
    silu = gate * logistic
    act = silu * up
    d_gate = None
    if gate_column is not None:
        d_gate = jnp.sum(act * slope, axis=-1, keepdims=True)
        act = act * gate_column
        slope = slope * gate_column
    act = act.astype(jnp.bfloat16)
    d_both = jnp.concatenate(
        [
            (slope * up * (logistic * (1.0 + gate * (1.0 - logistic)))).astype(jnp.bfloat16),
            (slope * silu).astype(jnp.bfloat16),
        ],
        axis=1,
    )
    grads[0][...] = jnp.dot(
        turned_ref[...], d_both, preferred_element_type=jnp.float32
    ).astype(jnp.bfloat16)
    grads[1][...] = tn_dot(act, d_out).astype(jnp.bfloat16)
    out = jnp.dot(act, down_weight, preferred_element_type=jnp.float32)
    return out, nt_dot(d_both, both_weight), d_gate


def add_parts(step, totals, parts, first):
    @pl.when(step == 0)
    def _():
        for i, part in enumerate(parts):
            totals[i][...] = part if first is None else first[i][...] + part

    @pl.when(step > 0)
    def _():
        for i, part in enumerate(parts):
            totals[i][...] += part


def shared_body(
    normed_ref, turned_ref, d_out_ref, gate_ref, up_ref, down_ref, out_ref, back_ref, pair_ref,
    grad_down_ref,
):
    out, back, _ = branch_step(
        normed_ref,
        turned_ref,
        d_out_ref,
        None,
        (jnp.concatenate([gate_ref[...], up_ref[...]], axis=1), down_ref[...]),
        (pair_ref, grad_down_ref),
    )
    add_parts(pl.program_id(0), (out_ref, back_ref), (out, back), None)


def expert_body(
    place_ref, normed_ref, turned_ref, d_out_ref, gates_ref, first_out_ref, first_back_ref, gate_ref,
    up_ref, down_ref, out_keep, out_send, back_keep, back_send, pair_ref, down_keep, down_send,
    out_total, back_total, slope_total, grad_down,
):
    step = pl.program_id(0)
    expert, side = place_ref[0], place_ref[1]
    out, back, d_gate = branch_step(
        normed_ref,
        turned_ref,
        d_out_ref,
        gates_ref[...],
        (jnp.concatenate([gate_ref[...], up_ref[...]], axis=1), down_ref[...]),
        (pair_ref, grad_down),
    )
    half = grad_down.shape[0] // 2
    for mine in range(2):

        @pl.when(side == mine)
        def _():
            down_keep[...] = grad_down[mine * half : (mine + 1) * half, :]
            down_send[...] = grad_down[(1 - mine) * half : (2 - mine) * half, :]

    add_parts(step, (out_total, back_total), (out, back), (first_out_ref, first_back_ref))
    add_parts(step, (slope_total,), (d_gate,), None)

    @pl.when(step == pl.num_programs(0) - 1)
    def _():
        width = out_total.shape[1]
        block = out_keep.shape[1]
        local = block // SEQUENCES
        slopes = slope_total[...]
        high = slopes.astype(jnp.bfloat16).astype(jnp.float32)
        lane = lax.broadcasted_iota(jnp.int32, (slopes.shape[0], LANES), 1)
        table = jnp.where(lane == expert, high, 0.0)
        table = jnp.where(lane == expert + LANES // 2, slopes - high, table).astype(jnp.bfloat16)
        for f in range(FS):
            x, core = divmod(f, 2)
            for r in range(SEQUENCES):
                start = (r * FS + f) * local
                here, there = slice(start, start + local), slice(r * local, (r + 1) * local)

                def write(out_ref, back_ref):
                    out_ref[x, there, :] = out_total[here, :].astype(jnp.bfloat16)
                    back_ref[x, there, :width] = back_total[here, :].astype(jnp.bfloat16)
                    back_ref[x, there, width:] = table[here, :]

                pl.when(expert % 2 == core)(functools.partial(write, out_keep, back_keep))
                pl.when(expert % 2 != core)(functools.partial(write, out_send, back_send))


def once(shape):
    return pl.BlockSpec(shape, lambda *_: (0,) * len(shape), pipeline_mode=pl.Buffered(1))


def shared_branch(normed, turned, d_out, both, down, tile):
    count, width = normed.shape
    hidden = down.shape[0]
    tiles = hidden // tile
    outs = [
        shape_of((count, width), jnp.float32),
        shape_of((count, width), jnp.float32),
        shape_of((width, 2 * hidden)),
        shape_of((hidden, width)),
    ]
    return kernel_call(
        shared_body,
        outs,
        18 * count * width * hidden,
        12 * width * hidden + 12 * count * width,
        grid=(tiles,),
        in_specs=[once(normed.shape), once(turned.shape), once(d_out.shape)]
        + [
            pl.BlockSpec((width, tile), lambda j: (0, j)),
            pl.BlockSpec((width, tile), lambda j: (0, tiles + j)),
            pl.BlockSpec((tile, width), lambda j: (j, 0)),
        ],
        out_specs=[once(out.shape) for out in outs[:2]]
        + [
            pl.BlockSpec((width, 2 * tile), lambda j: (0, j)),
            pl.BlockSpec((tile, width), lambda j: (j, 0)),
        ],
        name="shared_branch",
    )(normed, turned, d_out, both, both, down)


def expert_branch(place, normed, turned, d_out, gates, first_out, first_back, gate_up, down, tile):
    count, width = normed.shape
    hidden = down.shape[0]
    operands = [normed, turned, d_out, gates, first_out, first_back]
    split = lambda columns: [shape_of((2, count // FS, columns))] * 2
    outs = split(width) + split(width + LANES)
    halves = shape_of((hidden // tile, tile // 2, width))
    half_spec = pl.BlockSpec((None, tile // 2, width), lambda j: (j, 0, 0))
    return kernel_call(
        expert_body,
        outs + [shape_of((width, 2 * hidden)), halves, halves],
        18 * count * width * hidden,
        12 * width * hidden + 16 * count * width,
        grid=(hidden // tile,),
        in_specs=[pl.BlockSpec(memory_space=pltpu.SMEM)]
        + [once(array.shape) for array in operands]
        + [
            pl.BlockSpec((None, width, tile), lambda j: (0, 0, j)),
            pl.BlockSpec((None, width, tile), lambda j: (1, 0, j)),
            pl.BlockSpec((tile, width), lambda j: (j, 0)),
        ],
        out_specs=[once(out.shape) for out in outs]
        + [pl.BlockSpec((width, 2 * tile), lambda j: (0, j)), half_spec, half_spec],
        scratch_shapes=[
            pltpu.VMEM((count, width), jnp.float32),
            pltpu.VMEM((count, width), jnp.float32),
            pltpu.VMEM((count, 1), jnp.float32),
            pltpu.VMEM((tile, width), jnp.bfloat16),
        ],
        name="expert_branch",
    )(place, *operands, gate_up, gate_up, down)


def orthogonal_body(info_ref, *refs):
    shards, results = refs[:DP], refs[DP : 2 * DP]
    current, gram, poly = refs[2 * DP :]
    size, length = current.shape
    kind, place = info_ref[0], info_ref[1]
    rows = shards[0].shape[0]
    columns = 2 * LANES
    tile = 256
    tiles = size // tile
    chunks = length // tile

    def spot(k, extent):
        return pl.multiple_of(lax.rem(place + k, DP) * extent, extent)

    def folds(k):
        for j in range(size // rows):
            yield (
                (slice(j * rows, (j + 1) * rows), pl.ds(spot(k, columns), columns)),
                (slice(None), slice(j * columns, (j + 1) * columns)),
            )

    @pl.when(kind == 1)
    def _():
        for k in range(DP):
            current[pl.ds(spot(k, rows), rows), :] = shards[k][...]

    @pl.when(kind == 2)
    def _():
        current[:, DP * columns :] = jnp.zeros((size, length - DP * columns), jnp.bfloat16)
        for k in range(DP):
            for there, here in folds(k):
                current[there] = shards[k][here]

    @pl.when(kind > 0)
    def _():
        def square(c, total):
            part = current[:, pl.ds(pl.multiple_of(c * tile, tile), tile)].astype(jnp.float32)
            return total + jnp.sum(part * part, axis=0, keepdims=True)

        squares = lax.fori_loop(0, chunks, square, jnp.zeros((1, tile), jnp.float32))
        scale = 1.0 / (jnp.sqrt(jnp.sum(squares, axis=1, keepdims=True)) + 1e-07)

        def scale_chunk(c, carry):
            span = pl.ds(pl.multiple_of(c * tile, tile), tile)
            part = current[:, span].astype(jnp.float32)
            current[:, span] = (part * scale).astype(jnp.bfloat16)
            return carry

        lax.fori_loop(0, chunks, scale_chunk, 0)

        def sweep(_, carry):
            for i in range(tiles):
                block = nt_dot(current[i * tile : (i + 1) * tile, :], current[i * tile :, :])
                gram[i * tile : (i + 1) * tile, i * tile :] = block.astype(jnp.bfloat16)
                poly[i * tile : (i + 1) * tile, i * tile :] = POLY_SECOND * block
            for i in range(tiles):
                for j in range(i):
                    gram[i * tile : (i + 1) * tile, j * tile : (j + 1) * tile] = gram[
                        j * tile : (j + 1) * tile, i * tile : (i + 1) * tile
                    ].T
            for i in range(tiles):
                block = jnp.dot(
                    gram[i * tile : (i + 1) * tile, :],
                    gram[:, i * tile :],
                    preferred_element_type=jnp.float32,
                )
                poly[i * tile : (i + 1) * tile, i * tile :] += POLY_THIRD * block
            for i in range(tiles):
                gram[i * tile : (i + 1) * tile, i * tile :] = poly[
                    i * tile : (i + 1) * tile, i * tile :
                ].astype(jnp.bfloat16)
            for i in range(tiles):
                for j in range(i):
                    gram[i * tile : (i + 1) * tile, j * tile : (j + 1) * tile] = gram[
                        j * tile : (j + 1) * tile, i * tile : (i + 1) * tile
                    ].T

            def update(c, carry):
                span = pl.ds(pl.multiple_of(c * tile, tile), tile)
                part = current[:, span]
                fresh = POLY_FIRST * part.astype(jnp.float32) + jnp.dot(
                    gram[...], part, preferred_element_type=jnp.float32
                )
                current[:, span] = fresh.astype(jnp.bfloat16)
                return carry

            return lax.fori_loop(0, chunks, update, carry)

        lax.fori_loop(0, NS_STEPS, sweep, 0)

    @pl.when(kind == 1)
    def _():
        for k in range(DP):
            results[k][...] = current[pl.ds(spot(k, rows), rows), :]

    @pl.when(kind == 2)
    def _():
        for k in range(DP):
            for there, here in folds(k):
                results[k][here] = current[there]


def orthogonal_shards(info, shards, size):
    rows, length = shards[0].shape
    vmem = pl.BlockSpec(memory_space=pltpu.VMEM)
    return kernel_call(
        orthogonal_body,
        [shape_of((rows, length))] * DP,
        26e9,
        8e6,
        in_specs=[pl.BlockSpec(memory_space=pltpu.SMEM)] + [vmem] * DP,
        out_specs=[vmem] * DP,
        scratch_shapes=[
            pltpu.VMEM((size, length), jnp.bfloat16),
            pltpu.VMEM((size, size), jnp.bfloat16),
            pltpu.VMEM((size, size), jnp.float32),
        ],
        name="orthogonal_shards",
    )(info, *shards)


def fold_tall(block, rows, length):
    columns, size = block.shape
    block = block.T.reshape(size // rows, rows, columns).transpose(1, 0, 2).reshape(rows, -1)
    return jnp.pad(block, ((0, 0), (0, length - block.shape[1])))


def unfold_tall(block, columns):
    rows = block.shape[0]
    size = rows * DP
    block = block[:, : size // rows * columns].reshape(rows, size // rows, columns)
    return block.transpose(1, 0, 2).reshape(size, columns).T


def orthogonal_router_body(matrix_ref, out_ref):
    current = matrix_ref[...]
    dot = functools.partial(
        lax.dot_general, precision=HIGHEST_PRECISION, preferred_element_type=jnp.float32
    )
    square = jnp.sum(jnp.sum(current * current, axis=1, keepdims=True), axis=0, keepdims=True)
    current = current / (jnp.sqrt(square) + 1e-07)
    for _ in range(NS_STEPS):
        gram = dot(current, current, (((1,), (1,)), ((), ())))
        poly = POLY_SECOND * gram + POLY_THIRD * dot(gram, gram, (((1,), (0,)), ((), ())))
        current = POLY_FIRST * current + dot(poly, current, (((1,), (0,)), ((), ())))
    out_ref[...] = current


def orthogonal_router(matrix):
    return kernel_call(
        orthogonal_router_body, shape_of(matrix.shape, jnp.float32), 2e9, 1e6, name="orthogonal_router"
    )(matrix)


def slot_table(owners):
    table = np.zeros((FS, DP), np.int32)
    for f, column in enumerate(owners):
        for slot, d in enumerate(column):
            table[f, d] = slot
    return table


def owner_pairs(owners, step, back):
    pairs = []
    for f, column in enumerate(owners):
        for d in column:
            other = (d + step) % DP
            pair = (other * FS + f, d * FS + f)
            pairs.append(pair[::-1] if back else pair)
    return pairs


def to_owners(stack, owners, dp_index, index):
    table = jnp.asarray(slot_table(owners))[index]
    got = []
    for step in range(DP):
        slot = table[lax.rem(dp_index - step + DP, DP)]
        block = lax.dynamic_index_in_dim(stack, slot, 0, keepdims=False)
        got.append(
            block if step == 0 else lax.ppermute(block, AXES, owner_pairs(owners, step, False))
        )
    return got


def from_owners(blocks, owners, dp_index, index):
    got = jnp.stack(
        [
            block if step == 0 else lax.ppermute(block, AXES, owner_pairs(owners, step, True))
            for step, block in enumerate(blocks)
        ]
    )
    count = max(len(column) for column in owners)
    table = np.array([list(column) + [0] * (count - len(column)) for column in owners], np.int32)
    places = jnp.asarray(table)[index]
    return [
        lax.dynamic_index_in_dim(got, lax.rem(dp_index - places[slot] + DP, DP), 0, keepdims=False)
        for slot in range(count)
    ]


def line_hop(value, step):
    pairs = [
        ((z * 2 + y) * FS + f, ((z + step) % LINE * 2 + y) * FS + f)
        for z in range(LINE)
        for y in range(2)
        for f in range(FS)
    ]
    return lax.ppermute(value, AXES, pairs)


def pair_hop(value):
    pairs = [(d * FS + f, (d ^ 1) * FS + f) for d in range(DP) for f in range(FS)]
    return lax.ppermute(value, AXES, pairs)


def place_body(places_ref, *refs):
    out_ref = refs[-1]
    rows = refs[0].shape[0]
    other_ref = refs[-2]
    for i, ref in enumerate(refs[:-2]):
        out_ref[pl.ds(pl.multiple_of(places_ref[i] * rows, rows), rows), :] = ref[...]
        start = pl.multiple_of(places_ref[LINE + i] * rows, rows)
        out_ref[pl.ds(start, rows), :] = other_ref[i]


class Gather:
    def __init__(self, block, place):
        _, self.side, self.level = place
        self.blocks = [block] + [line_hop(block, step) for step in range(1, LINE)]

    def cross(self, *events):
        self.stack = jnp.stack(self.blocks)
        if events:
            self.stack = after(self.stack, *events)
        self.other = pair_hop(self.stack)
        return self.other

    def last(self):
        levels = lax.rem(self.level + LINE - jnp.arange(LINE), LINE)
        places = jnp.concatenate([levels * 2 + self.side, levels * 2 + 1 - self.side])
        rows, columns = self.blocks[0].shape
        vmem = pl.BlockSpec(memory_space=pltpu.VMEM)
        return kernel_call(
            place_body,
            shape_of((DP * rows, columns), self.stack.dtype),
            0,
            4 * DP * rows * columns,
            in_specs=[pl.BlockSpec(memory_space=pltpu.SMEM)] + [vmem] * (LINE + 1),
            out_specs=vmem,
            name="place_rows",
        )(places.astype(jnp.int32), *self.blocks, self.other)


class Reduce:
    def __init__(self, grads, place):
        _, self.side, self.level = place
        self.grads = grads

    def pick(self, array, i, axis=0):
        return lax.dynamic_index_in_dim(array, i, axis, keepdims=False)

    def cross(self, *events):
        rows, columns = self.grads.shape
        grads = self.grads.reshape(LINE, 2, rows // DP, columns)
        if events:
            grads = after(grads, *events)
        self.mine = self.pick(grads, self.side, 1)
        self.sent = self.pick(grads, 1 - self.side, 1)
        self.got = pair_hop(self.sent)
        return self.got

    def along(self, *events):
        got = after(self.got, *events) if events else self.got
        mine = self.mine
        both = (mine.astype(jnp.float32) + got.astype(jnp.float32)).astype(mine.dtype)
        self.both = both
        at = lambda step: self.pick(both, lax.rem(self.level + step, LINE))
        self.parts = [at(0)] + [line_hop(at(step), step) for step in range(1, LINE)]
        return self.parts[1]

    def last(self):
        return sum(part.astype(jnp.float32) for part in self.parts)


def split_plan(
    tokens,
    cotangent,
    lengths,
    routes,
    gains,
    gain_moms,
    w_dense,
    mom_dense,
    w_router,
    mom_router,
    w_down,
    mom_down,
    e_gate_up,
    e_mom_gate_up,
    e_down,
    e_mom_down,
):
    index, dp_index = lax.axis_index("fsdp"), lax.axis_index("dp")
    device_index = dp_index * FS + index
    rows, local_len, width = tokens.shape
    row_len = local_len * FS
    count = rows * row_len
    experts = w_router.shape[1]
    head_size = width // HEADS
    quarter = width // FS
    block_rows = w_dense.shape[0]
    down_rows = w_down.shape[0]
    ff_shared = down_rows * DP * FS
    ff_part = down_rows * DP
    bf16 = jnp.bfloat16

    def by_columns(matrix):
        qkv_parts = [
            matrix[:, i * width : (i + 1) * width].reshape(block_rows, FS, quarter)
            for i in range(3)
        ]
        shared_parts = [
            matrix[:, 4 * width + i * ff_shared : 4 * width + (i + 1) * ff_shared]
            .reshape(block_rows, DP, FS, down_rows)
            .transpose(0, 2, 1, 3)
            .reshape(block_rows, FS, ff_part)
            for i in range(2)
        ]
        return jnp.concatenate(qkv_parts + shared_parts, axis=2).transpose(1, 0, 2)

    dense = w_dense.astype(bf16)
    own_columns = by_columns(dense)
    qkv_columns = own_columns[..., : 3 * quarter]
    common = jnp.concatenate(
        [
            w_router.astype(bf16),
            gains.astype(bf16).T,
            jnp.zeros((block_rows, LANES - experts - 2), bf16),
        ],
        axis=1,
    )
    spread = lambda array: jnp.broadcast_to(array, (FS,) + array.shape)
    place = (index, dp_index % 2, dp_index // 2)
    gate_up_copy = lax.all_gather(e_gate_up[0].astype(bf16), "dp", axis=1, tiled=True)
    edown_copy = lax.all_gather(e_down[0].astype(bf16), "dp", axis=0, tiled=True)
    message = jnp.concatenate([qkv_columns, spread(common)], axis=2)
    message = jnp.concatenate(exchange_fsdp(message, index), axis=0)
    folds = message.shape[0]
    fold_down, fold_out = down_rows * width // folds, block_rows * width // folds
    own_out = dense[:, 3 * width : 4 * width].reshape(folds, fold_out)
    first_pack = Gather(jnp.concatenate([message, own_out], axis=1), place)
    routes_low = jnp.concatenate(
        [routes.astype(bf16), jnp.zeros((rows, local_len, LANES - routes.shape[2]), bf16)], axis=2
    )
    inputs = jnp.concatenate(
        gather_fsdp(jnp.concatenate([tokens, routes_low], axis=2), index), axis=1
    )
    message = jnp.concatenate(exchange_fsdp(own_columns[..., 3 * quarter :], index), axis=0)
    message = after(message, *first_pack.blocks[1:])
    second_pack = Gather(
        jnp.concatenate([message, w_down.astype(bf16).reshape(folds, fold_down)], axis=1), place
    )
    first_pack.cross()
    pack = first_pack.last()
    w_qkv, w_route = pack[:, : 3 * quarter], pack[:, 3 * quarter : 3 * quarter + LANES]
    w_out = pack[:, 3 * quarter + LANES :].reshape(DP, block_rows, width)
    gain_rows = w_route[:, experts : experts + 2].astype(jnp.float32).T
    gain_one, gain_two = gain_rows[0:1], gain_rows[1:2]

    x_all = inputs[..., :width]
    route_all = inputs[..., width:].astype(jnp.int32).reshape(count, LANES)
    all_places = jnp.arange(row_len)
    valid_all = all_places[None, :] < lengths[:, None]
    half = head_size // 2
    frequency = 10000.0 ** (-2.0 * jnp.arange(half, dtype=jnp.float32) / head_size)
    angles = all_places.astype(jnp.float32)[:, None] * frequency[None, :]
    repeats = (1, 2 * quarter // half)
    cosine, sine = jnp.tile(jnp.cos(angles), repeats), jnp.tile(jnp.sin(angles), repeats)

    normed_one, qkv, probs, attended = attention_forward(
        x_all, gain_one, w_qkv, cosine, sine, lengths
    )
    cot_all = jnp.concatenate(gather_fsdp(after(cotangent, pack), index), axis=1)
    d_out_all = jnp.where(valid_all[..., None], cot_all, 0).reshape(count, width)
    attended_all = jnp.concatenate(gather_fsdp(attended, index), axis=2)
    w_out = jnp.stack(gather_fsdp(w_out, index), axis=1).reshape(width, width)
    second_pack.cross()
    pack = second_pack.last()
    w_shared = pack[:, : 2 * ff_part]
    down_copy = pack[:, 2 * ff_part :].reshape(DP * down_rows, width)
    mid_all, normed_all, turned_all, gates_all = middle_forward(
        after(attended_all, second_pack.other).reshape(count, width), x_all.reshape(count, width), route_all, w_out, w_route,
        gain_two,
    )
    gate_column = lax.dynamic_slice_in_dim(gates_all, index, 1, 1)
    tile = 2 * e_down.shape[1]
    ff_width = e_gate_up.shape[3]
    first_out, first_back, grad_pair, grad_down = shared_branch(
        normed_all, turned_all, d_out_all, w_shared, down_copy, tile
    )
    sum_shared = Reduce(
        jnp.concatenate([grad_pair, grad_down.reshape(width, fold_down)], axis=1), place
    )
    sum_shared.cross()
    out_keep, out_send, back_keep, back_send, grad_pairs, edown_keep, edown_send = expert_branch(
        jnp.stack([index, dp_index % 2]), after(normed_all, sum_shared.got), turned_all, d_out_all,
        gate_column, first_out, first_back, gate_up_copy, edown_copy, tile,
    )

    sum_shared.along()
    part_pairs = lax.psum_scatter(grad_pairs, "dp", scatter_dimension=0, tiled=True)
    d_sum = FsdpSum(back_keep, after(back_send, *sum_shared.parts[1:]), index)
    sum_edown = Reduce(None, place)
    sum_edown.mine, sum_edown.got = edown_keep, pair_hop(edown_send)

    def by_place(values):
        return values.reshape(rows, FS, local_len, values.shape[-1]).transpose(1, 0, 2, 3)

    def own_rows(values):
        part = lax.dynamic_slice_in_dim(
            values.reshape(rows, row_len, values.shape[-1]), index * local_len, local_len, 1
        )
        return part.reshape(rows * local_len, values.shape[-1])

    d_sum = d_sum.cross().last().reshape(rows * local_len, width + LANES)
    mid = own_rows(mid_all)
    d_out = own_rows(d_out_all)
    d_mid, grad_wout, grad_router, grad_gain_two, *d_att = middle_backward(
        index.reshape(1), mid, d_out, d_sum, own_rows(gates_all),
        routes.reshape(rows * local_len, -1), own_rows(attended_all), own_rows(normed_all), w_out,
        w_route, gain_two,
    )
    d_att = [block.reshape(rows, local_len, quarter) for block in d_att]
    d_att = [d_att[0]] + [fsdp_hop(d_att[step], step) for step in range(1, FS)]
    grad_wout = grad_wout.reshape(DP, FS, block_rows, width).transpose(1, 0, 2, 3)
    sum_wout = FsdpSum(*by_core(grad_wout, index, d_att[1]), index).cross()
    grad_wout = sum_wout.last().astype(bf16).reshape(width, fold_out)
    d_att = jnp.concatenate(by_source(*d_att, index), axis=1)
    grad_qkv, back_part = attention_backward(
        normed_one, qkv, probs, after(d_att, sum_wout.far), w_qkv, cosine, sine
    )
    sum_last = Reduce(jnp.concatenate([grad_qkv, grad_wout], axis=1), place)
    sum_last.cross()
    sum_last.along()
    sum_edown.along(sum_last.both)

    split_pair = lambda part, half: part.reshape(part.shape[0], -1, 2, tile)[:, :, half].reshape(
        part.shape[0], -1
    )
    part_shared = sum_shared.last()
    part_down = part_shared[:, 2 * ff_part :].reshape(down_rows, width)
    raw_pairs = part_pairs
    part_pairs = part_pairs.astype(jnp.float32)
    part_gate_up = jnp.stack([split_pair(part_pairs, half) for half in range(2)])
    part_last = sum_last.last()
    part_edown = sum_edown.last()
    part_out = part_last[:, 3 * quarter :].reshape(block_rows, width)
    part_near = jnp.concatenate(
        [
            part_last[:, : 3 * quarter],
            split_pair(part_shared[:, : 2 * ff_part], 0),
            split_pair(part_shared[:, : 2 * ff_part], 1),
        ],
        axis=1,
    )
    part_dense = part_near.astype(bf16)

    out_sum = FsdpSum(out_keep, after(out_send, sum_last.got), index).cross().last()
    out_sum = out_sum.reshape(rows * local_len, width)
    valid = (
        (index * local_len + jnp.arange(local_len))[None, :] < lengths[:, None]
    ).astype(jnp.float32)
    output = ((mid + out_sum).reshape(tokens.shape) * valid[..., None]).astype(bf16)
    d_one = FsdpSum(*by_core(by_place(back_part), index, sum_last.sent), index).cross().last()
    d_one = d_one.reshape(tokens.shape)
    scaled_one, inverse_one = statistics(tokens.astype(jnp.float32))
    d_in, grad_gain_one = norm_back(d_one, scaled_one, inverse_one, gain_one)
    d_tokens = (d_mid.reshape(tokens.shape) + d_in).astype(bf16)

    old_near = exchange_fsdp(by_columns(after(mom_dense, normed_all).astype(bf16)), index)
    old_near = jnp.concatenate(old_near, axis=0).astype(jnp.float32)
    got = exchange_fsdp(part_dense.reshape(FS, block_rows, part_dense.shape[1]), index)
    got = [block.astype(jnp.float32) for block in got]
    cut = lambda start, size: [block[:, start : start + size] for block in got]
    interleave = lambda parts: jnp.stack(
        [part.reshape(block_rows, DP, down_rows) for part in parts], axis=2
    ).reshape(block_rows, ff_shared)
    grad_dense = jnp.concatenate(
        cut(0, quarter)
        + cut(quarter, quarter)
        + cut(2 * quarter, quarter)
        + [part_out]
        + [interleave(cut(3 * quarter, ff_part)), interleave(cut(3 * quarter + ff_part, ff_part))],
        axis=1,
    )
    new_mom_dense = MUON_DECAY * mom_dense + grad_dense
    new_mom_down = MUON_DECAY * mom_down + part_down
    new_e_mom_gate_up = MUON_DECAY * e_mom_gate_up + part_gate_up[None]
    new_e_mom_down = MUON_DECAY * e_mom_down + part_edown[None]

    length = 3 * width
    pad = lambda block: jnp.pad(block, ((0, 0), (0, length - block.shape[1])))
    edges = (0, 3 * width, 4 * width, 4 * width + ff_shared, 4 * width + 2 * ff_shared)
    spots = (0, 3 * quarter, 3 * quarter + ff_part, 3 * quarter + 2 * ff_part)
    near = (MUON_DECAY * old_near + part_near).astype(bf16)
    near_out = (MUON_DECAY * mom_dense[:, 3 * width : 4 * width] + part_out).astype(bf16)
    stripe = lambda block: jnp.pad(block, ((0, 0), (0, 3 * quarter - block.shape[1])))
    stripes = [near[:, spots[i] : spots[i + 1]] for i in range(3)]
    stripes.append(near_out.reshape(folds, fold_out))
    stripes = after(jnp.stack([stripe(block) for block in stripes]), *sum_edown.parts[1:])
    got = exchange_fsdp(stripes, index)
    whole_out = jnp.concatenate(
        [block[:, :fold_out].reshape(block_rows, width) for block in got], axis=0
    )
    dense_block = jnp.where(index == FS - 1, pad(whole_out), jnp.concatenate(got, axis=1))
    low_experts = new_e_mom_gate_up[0].astype(bf16)
    wide = [pad(low_experts[0]), pad(low_experts[1]), dense_block]
    low_down = after(new_mom_down.astype(bf16), sum_last.got)
    column_pairs = lambda step, back: [
        (d * FS + DOWN_COLUMN, d * FS + (DOWN_COLUMN ^ step))[:: 1 if back else -1]
        for d in range(DP)
    ]
    down_block = jnp.concatenate(
        [
            low_down if f == DOWN_COLUMN else lax.ppermute(
                low_down, AXES, column_pairs(DOWN_COLUMN ^ f, False)
            )
            for f in range(FS)
        ],
        axis=0,
    )
    talls = [fold_tall(new_e_mom_down[0].astype(bf16), folds, length), fold_tall(down_block, folds, length)]
    arrived = to_owners(jnp.stack(wide + talls), OWNERS, dp_index, index)
    kinds = np.zeros((FS, DP), np.int32)
    for f in range(FS):
        for slot, d in enumerate(OWNERS[f]):
            kinds[f, d] = 2 if slot in TALL_SLOTS else 1
    info = jnp.stack([jnp.asarray(kinds)[index, dp_index], dp_index.astype(jnp.int32)])
    shards = orthogonal_shards(info, arrived, width)
    columns = (0, device_index * block_rows)
    zeros = jnp.zeros((8 - experts - 2, width), jnp.float32)
    small = jnp.concatenate(
        [grad_router[:experts], grad_gain_one[None], grad_gain_two, zeros], axis=0
    )
    old = jnp.concatenate(
        [MUON_DECAY * mom_router.T, GAIN_DECAY * gain_moms, zeros[:, :block_rows]], axis=0
    )
    small = small + lax.dynamic_update_slice(jnp.zeros_like(small), old, columns)
    small = sum_everywhere(after(small, sum_last.both))
    own_small = lax.dynamic_slice(small, columns, (8, block_rows))
    new_mom_router = own_small[:experts].T
    new_gain_moms = own_small[experts : experts + 2]
    gain_rate = 0.1 / math.sqrt(count * DP)
    new_gains = gains - gain_rate * new_gain_moms
    orth_router = orthogonal_router(
        jnp.concatenate([after(small, *shards)[:experts], jnp.zeros((LANES - experts, width), jnp.float32)], axis=0)
    )
    new_router = w_router - ROUTER_RATE * lax.dynamic_slice(
        orth_router, columns, (experts, block_rows)
    ).T

    orth_gate, orth_up, orth_block, orth_edown, orth_down_block = from_owners(
        shards, OWNERS, dp_index, index
    )
    orth_edown = unfold_tall(orth_edown, e_down.shape[1])
    orth_down_block = unfold_tall(orth_down_block, e_down.shape[1])
    got = exchange_fsdp(orth_block.reshape(FS, block_rows, length), index)
    striped = lambda block: block.reshape(block_rows, FS, 3 * quarter)
    orth_qkv = striped(got[0]).reshape(block_rows, FS, 3, quarter).transpose(0, 2, 1, 3)
    orth_shared = [
        striped(got[i])[:, :, :ff_part]
        .reshape(block_rows, FS, DP, down_rows)
        .transpose(0, 2, 1, 3)
        .reshape(block_rows, ff_shared)
        for i in (1, 2)
    ]
    orth_dense = [orth_qkv.reshape(block_rows, 3 * width), got[3][:, :width]] + orth_shared
    orth_down_parts = orth_down_block.reshape(FS, down_rows, width)
    orth_down = jnp.where(index == DOWN_COLUMN, orth_down_parts[DOWN_COLUMN], 0)
    for f in range(FS):
        if f != DOWN_COLUMN:
            orth_down = orth_down + lax.ppermute(
                orth_down_parts[f], AXES, column_pairs(DOWN_COLUMN ^ f, True)
            )
    new_dense = jnp.concatenate(
        [
            w_dense[:, edges[i] : edges[i + 1]] - DENSE_RATES[i] * orth_dense[i].astype(jnp.float32)
            for i in range(4)
        ],
        axis=1,
    )
    new_down = w_down - DOWN_RATE * orth_down.astype(jnp.float32)
    new_e_gate_up = jnp.stack(
        [
            e_gate_up[0, i] - EXPERT_RATES[i] * part[:, :ff_width].astype(jnp.float32)
            for i, part in enumerate((orth_gate, orth_up))
        ]
    )[None]
    new_e_down = e_down - EXPERT_RATES[2] * orth_edown.astype(jnp.float32)[None]
    return (
        output,
        d_tokens,
        new_gain_moms,
        new_gains,
        new_mom_dense,
        new_dense,
        new_mom_router,
        new_router,
        new_mom_down,
        new_down,
        new_e_mom_gate_up,
        new_e_gate_up,
        new_e_mom_down,
        new_e_down,
    )


def solution(mesh):
    placed = (
        P("dp", "fsdp", None),
        P("dp", "fsdp", None),
        P("dp"),
        P("dp", "fsdp", None),
        P(None, ("dp", "fsdp")),
        P(None, ("dp", "fsdp")),
        P(("dp", "fsdp"), None),
        P(("dp", "fsdp"), None),
        P(("dp", "fsdp"), None),
        P(("dp", "fsdp"), None),
        P(("dp", "fsdp"), None),
        P(("dp", "fsdp"), None),
        P("fsdp", None, "dp", None),
        P("fsdp", None, "dp", None),
        P("fsdp", "dp", None),
        P("fsdp", "dp", None),
    )
    fits = dict(mesh.shape) == {"dp": DP, "fsdp": FS}
    return jax.shard_map(
        split_plan if fits else general_plan,
        mesh=mesh,
        in_specs=placed,
        out_specs=(
            P("dp", "fsdp", None),
            P("dp", "fsdp", None),
            P(None, ("dp", "fsdp")),
            P(None, ("dp", "fsdp")),
            P(("dp", "fsdp"), None),
            P(("dp", "fsdp"), None),
            P(("dp", "fsdp"), None),
            P(("dp", "fsdp"), None),
            P(("dp", "fsdp"), None),
            P(("dp", "fsdp"), None),
            P("fsdp", None, "dp", None),
            P("fsdp", None, "dp", None),
            P("fsdp", "dp", None),
            P("fsdp", "dp", None),
        ),
        check_vma=False,
    )
```

```python
import functools
import math

import jax
import jax.numpy as jnp
import numpy as np
from jax import lax
from jax.experimental import pallas as pl
from jax.experimental.pallas import tpu as pltpu
from jax.sharding import PartitionSpec as P

HEADS = 12
NS_STEPS = 5


NORM_EPSILON = 1e-06
POLY_FIRST = 3.4445
POLY_SECOND = -4.775
POLY_THIRD = 2.0315
HIGHEST_PRECISION = lax.Precision.HIGHEST
MASK_VALUE = -1e30
DENSE_RATES = (0.8, 5.0, 0.8, 0.8)
ROUTER_RATE = 0.4
DOWN_RATE = 0.5
EXPERT_RATES = (0.8, 0.8, 0.5)
GAIN_DECAY = 0.9
MUON_DECAY = 0.5


def bf_dot(left, right):
    return jnp.dot(left, right, preferred_element_type=jnp.float32)


def first_dot(left, right, precision=None):
    return lax.dot_general(
        left,
        right,
        (((0,), (0,)), ((), ())),
        precision=precision,
        preferred_element_type=jnp.float32,
    )


def last_dot(left, right, precision=None):
    return lax.dot_general(
        left,
        right,
        (((1,), (1,)), ((), ())),
        precision=precision,
        preferred_element_type=jnp.float32,
    )


def statistics(values):
    inverse = lax.rsqrt(jnp.mean(values * values, axis=-1, keepdims=True) + NORM_EPSILON)
    return (values * inverse, inverse)


def norm_back(grad_out, scaled, inverse, gain_row):
    gain_grad = jnp.sum(grad_out * scaled, axis=(0, 1))
    through = grad_out * gain_row
    grad_in = inverse * (through - scaled * jnp.mean(through * scaled, axis=-1, keepdims=True))
    return (grad_in, gain_grad)


def rotation_tables(head_size, places):
    half_size = head_size // 2
    frequency = 10000.0 ** (-2.0 * jnp.arange(half_size, dtype=jnp.float32) / head_size)
    angles = places.astype(jnp.float32)[:, None] * frequency[None, :]
    return (jnp.cos(angles)[:, None, :], jnp.sin(angles)[:, None, :], half_size)


def rotate(values, places):
    cosine, sine, half_size = rotation_tables(values.shape[-1], places)
    first_half = values[..., :half_size]
    second_half = values[..., half_size:]
    return jnp.concatenate(
        [first_half * cosine - second_half * sine, second_half * cosine + first_half * sine],
        axis=-1,
    )


def rotate_back(grads, places):
    cosine, sine, half_size = rotation_tables(grads.shape[-1], places)
    first_half = grads[..., :half_size]
    second_half = grads[..., half_size:]
    return jnp.concatenate(
        [first_half * cosine + second_half * sine, second_half * cosine - first_half * sine],
        axis=-1,
    )


def silu_slope(values):
    logistic = jax.nn.sigmoid(values)
    return logistic * (1.0 + values * (1.0 - logistic))


def orthogonal(matrix):
    if matrix.shape[0] > matrix.shape[1]:
        return orthogonal(matrix.T).T
    current = matrix / (jnp.sqrt(jnp.sum(matrix * matrix)) + 1e-07)

    def sweep(_, current):
        gram = jnp.dot(current, current.T, precision=HIGHEST_PRECISION)
        poly = POLY_SECOND * gram + POLY_THIRD * jnp.dot(gram, gram, precision=HIGHEST_PRECISION)
        return POLY_FIRST * current + jnp.dot(poly, current, precision=HIGHEST_PRECISION)

    return lax.fori_loop(0, NS_STEPS, sweep, current)


def general_plan(
    tokens,
    cotangent,
    lengths,
    routes,
    gains,
    gain_moms,
    w_dense,
    mom_dense,
    w_router,
    mom_router,
    w_down,
    mom_down,
    e_gate_up,
    e_mom_gate_up,
    e_down,
    e_mom_down,
):
    seq_rows, local_len, width = tokens.shape
    head_count = HEADS
    head_size = width // head_count
    seq_parts = lax.axis_size("fsdp")
    seq_index = lax.axis_index("fsdp")
    row_len = local_len * seq_parts
    expert_count = w_router.shape[1]
    top_count = routes.shape[2]
    most_rows = 2 * local_len * top_count // expert_count
    capacity = seq_rows * most_rows
    places = seq_index * local_len + jnp.arange(local_len)
    valid = (places[None, :] < lengths[:, None]).astype(jnp.float32)
    dense_copy, router_copy, down_copy, gain_copy = (
        lax.all_gather(w_dense.astype(jnp.bfloat16), ("dp", "fsdp"), axis=0, tiled=True),
        lax.all_gather(w_router.astype(jnp.bfloat16), ("dp", "fsdp"), axis=0, tiled=True),
        lax.all_gather(w_down.astype(jnp.bfloat16), ("dp", "fsdp"), axis=0, tiled=True),
        lax.all_gather(gains.astype(jnp.bfloat16), ("dp", "fsdp"), axis=1, tiled=True),
    )
    gate_up_copy, edown_copy = (
        lax.all_gather(e_gate_up.astype(jnp.bfloat16), "dp", axis=2, tiled=True),
        lax.all_gather(e_down.astype(jnp.bfloat16), "dp", axis=1, tiled=True),
    )
    gain_one = gain_copy[0].astype(jnp.float32)
    gain_two = gain_copy[1].astype(jnp.float32)
    ff_shared = down_copy.shape[0]
    gate_weight = gate_up_copy[0, 0]
    up_weight = gate_up_copy[0, 1]
    down_weight = edown_copy[0]
    ff_width = gate_weight.shape[1]
    inputs = tokens.astype(jnp.float32)
    scaled_one, inverse_one = statistics(inputs)
    normed_one = (scaled_one * gain_one).astype(jnp.bfloat16).reshape(-1, width)
    projected = bf_dot(normed_one, dense_copy[:, : 3 * width]).reshape(
        seq_rows, local_len, 3, head_count, head_size
    )
    queries = rotate(projected[:, :, 0], places).astype(jnp.bfloat16)
    keys_local = rotate(projected[:, :, 1], places).astype(jnp.bfloat16)
    values_local = projected[:, :, 2].astype(jnp.bfloat16)
    keys_all, values_all = (
        lax.all_gather(keys_local, "fsdp", axis=1, tiled=True),
        lax.all_gather(values_local, "fsdp", axis=1, tiled=True),
    )
    block_len = min(512, row_len)
    block_count = row_len // block_len
    stat_shape = (seq_rows, head_count, local_len)
    head_shape = (seq_rows, local_len, head_count, head_size)

    def masked_scores(query_part, query_places, key_part, key_places):
        raw_scores = (
            jnp.einsum("rqhd,rkhd->rhqk", query_part, key_part, preferred_element_type=jnp.float32)
            * 0.125
        )
        allowed = (key_places[None, None, :] <= query_places[None, :, None]) & (
            key_places[None, None, :] < lengths[:, None, None]
        )
        return jnp.where(allowed[:, None], raw_scores, MASK_VALUE)

    def key_block(index):
        start_at = index * block_len
        key_part = lax.dynamic_slice_in_dim(keys_all, start_at, block_len, 1)
        value_part = lax.dynamic_slice_in_dim(values_all, start_at, block_len, 1)
        return (key_part, value_part, start_at + jnp.arange(block_len))

    def running_max(carry, index):
        top_score, exp_total = carry
        key_part, value_part, key_places = key_block(index)
        scores = masked_scores(queries, places, key_part, key_places)
        new_top = jnp.maximum(top_score, jnp.max(scores, axis=-1))
        exp_total = exp_total * jnp.exp(top_score - new_top) + jnp.sum(
            jnp.exp(scores - new_top[..., None]), axis=-1
        )
        return ((new_top, exp_total), None)

    start_stats = (
        jnp.full(stat_shape, MASK_VALUE, jnp.float32),
        jnp.zeros(stat_shape, jnp.float32),
    )
    (top_score, exp_total), _ = lax.scan(running_max, start_stats, jnp.arange(block_count))
    log_total = top_score + jnp.log(exp_total)

    def weigh_values(total_acc, index):
        key_part, value_part, key_places = key_block(index)
        scores = masked_scores(queries, places, key_part, key_places)
        weights = jnp.exp(scores - log_total[..., None]).astype(jnp.bfloat16)
        return (
            total_acc
            + jnp.einsum(
                "rhqk,rkhd->rqhd", weights, value_part, preferred_element_type=jnp.float32
            ),
            None,
        )

    attended, _ = lax.scan(
        weigh_values, jnp.zeros(head_shape, jnp.float32), jnp.arange(block_count)
    )
    attended_copy = attended.reshape(-1, width).astype(jnp.bfloat16)
    branch = bf_dot(attended_copy, dense_copy[:, 3 * width : 4 * width]).reshape(
        seq_rows, local_len, width
    )
    middle = inputs + branch
    scaled_two, inverse_two = statistics(middle)
    normed_two = (scaled_two * gain_two).astype(jnp.bfloat16).reshape(-1, width)
    logits = bf_dot(normed_two, router_copy)
    route_rows = routes.reshape(-1, top_count)
    chosen = jnp.take_along_axis(logits, route_rows, axis=1)
    gates = jax.nn.softmax(chosen, axis=-1)
    shared_pre = bf_dot(normed_two, dense_copy[:, 4 * width :])
    shared_gate = shared_pre[:, :ff_shared]
    shared_up = shared_pre[:, ff_shared:]
    shared_act = (jax.nn.silu(shared_gate) * shared_up).astype(jnp.bfloat16)
    shared_out = bf_dot(shared_act, down_copy)
    pair_experts = routes.reshape(seq_rows, local_len * top_count)
    onehot = (pair_experts[..., None] == jnp.arange(expert_count, dtype=jnp.int32)).astype(
        jnp.int32
    )
    ranking = jnp.sum((jnp.cumsum(onehot, axis=1) - onehot) * onehot, axis=-1)
    slot_local = (jnp.arange(seq_rows, dtype=jnp.int32)[:, None] * most_rows + ranking).reshape(-1)
    slot_ids = pair_experts.reshape(-1) * capacity + slot_local
    pair_count = seq_rows * local_len * top_count
    table = (
        jnp.full((expert_count * capacity,), -1, jnp.int32)
        .at[slot_ids]
        .set(jnp.arange(pair_count, dtype=jnp.int32))
    )
    present = table >= 0
    picked = jnp.where(present, table, 0)
    outgoing = jnp.where(
        present[:, None], normed_two[picked // top_count], jnp.zeros((), jnp.bfloat16)
    ).reshape(expert_count, capacity, width)
    arrived = lax.all_to_all(outgoing, "fsdp", split_axis=0, concat_axis=0, tiled=True)
    sources, item_count, _ = arrived.shape
    arrived_rows = arrived.reshape(sources * item_count, width)
    pre_act = jnp.concatenate(
        [bf_dot(arrived_rows, gate_weight), bf_dot(arrived_rows, up_weight)], axis=-1
    )
    activated = (jax.nn.silu(pre_act[:, :ff_width]) * pre_act[:, ff_width:]).astype(jnp.bfloat16)
    result = bf_dot(activated, down_weight).astype(jnp.bfloat16).reshape(sources, item_count, width)
    returned_rows = lax.all_to_all(result, "fsdp", split_axis=0, concat_axis=0, tiled=True)
    pre_all = pre_act.reshape(sources, item_count, 2 * ff_width)
    pair_out = (
        returned_rows.reshape(expert_count * capacity, width)[slot_ids]
        .reshape(-1, top_count, width)
        .astype(jnp.float32)
    )
    mixed = jnp.sum(gates[..., None] * pair_out, axis=1)
    total = middle + (shared_out + mixed).reshape(seq_rows, local_len, width)
    output = (total * valid[..., None]).astype(jnp.bfloat16)
    d_out = cotangent.astype(jnp.float32) * valid[..., None]
    d_flat = d_out.reshape(-1, width)
    d_flat_copy = d_flat.astype(jnp.bfloat16)
    grad_down = first_dot(shared_act, d_flat_copy)
    d_sact = last_dot(d_flat_copy, down_copy)
    d_shared = jnp.concatenate(
        [d_sact * shared_up * silu_slope(shared_gate), d_sact * jax.nn.silu(shared_gate)], axis=-1
    ).astype(jnp.bfloat16)
    grad_shared = first_dot(normed_two, d_shared)
    d_normed = last_dot(d_shared, dense_copy[:, 4 * width :])
    d_gates = jnp.sum(d_flat[:, None, :] * pair_out, axis=-1)
    d_chosen = gates * (d_gates - jnp.sum(gates * d_gates, axis=-1, keepdims=True))
    route_table = (route_rows[..., None] == jnp.arange(expert_count, dtype=jnp.int32)).astype(
        jnp.float32
    )
    d_logits = jnp.sum(d_chosen[..., None] * route_table, axis=1).astype(jnp.bfloat16)
    grad_router = first_dot(normed_two, d_logits)
    d_normed = d_normed + last_dot(d_logits, router_copy)
    d_pairs = (gates[..., None] * d_flat[:, None, :]).reshape(-1, width).astype(jnp.bfloat16)
    d_outgoing = jnp.where(present[:, None], d_pairs[picked], jnp.zeros((), jnp.bfloat16)).reshape(
        expert_count, capacity, width
    )
    d_arrived = lax.all_to_all(d_outgoing, "fsdp", split_axis=0, concat_axis=0, tiled=True)
    d_result = d_arrived.reshape(-1, width)
    pre_rows = pre_all.reshape(-1, 2 * ff_width)
    expert_gate = pre_rows[:, :ff_width]
    expert_up = pre_rows[:, ff_width:]
    activated = (jax.nn.silu(expert_gate) * expert_up).astype(jnp.bfloat16)
    grad_edown = first_dot(activated, d_result)
    d_activated = last_dot(d_result, down_weight)
    d_pre = jnp.concatenate(
        [d_activated * expert_up * silu_slope(expert_gate), d_activated * jax.nn.silu(expert_gate)],
        axis=-1,
    ).astype(jnp.bfloat16)
    arrived_rows = arrived.reshape(-1, width)
    grad_gate = first_dot(arrived_rows, d_pre[:, :ff_width])
    grad_up = first_dot(arrived_rows, d_pre[:, ff_width:])
    d_inputs = (
        (last_dot(d_pre[:, :ff_width], gate_weight) + last_dot(d_pre[:, ff_width:], up_weight))
        .astype(jnp.bfloat16)
        .reshape(d_arrived.shape)
    )
    d_returned = lax.all_to_all(d_inputs, "fsdp", split_axis=0, concat_axis=0, tiled=True).reshape(
        expert_count * capacity, width
    )
    d_normed = d_normed + jnp.sum(
        d_returned[slot_ids].astype(jnp.float32).reshape(-1, top_count, width), axis=1
    )
    d_mid_norm, grad_gain_two = norm_back(
        d_normed.reshape(seq_rows, local_len, width), scaled_two, inverse_two, gain_two
    )
    d_middle = d_out + d_mid_norm
    d_branch = d_middle.reshape(-1, width).astype(jnp.bfloat16)
    grad_wout = first_dot(attended_copy, d_branch)
    d_attended = (
        last_dot(d_branch, dense_copy[:, 3 * width : 4 * width])
        .reshape(head_shape)
        .astype(jnp.bfloat16)
    )

    def delta_pass(delta_acc, index):
        key_part, value_part, key_places = key_block(index)
        weights = jnp.exp(
            masked_scores(queries, places, key_part, key_places) - log_total[..., None]
        )
        slopes = jnp.einsum(
            "rqhd,rkhd->rhqk", d_attended, value_part, preferred_element_type=jnp.float32
        )
        return (delta_acc + jnp.sum(weights * slopes, axis=-1), None)

    delta, _ = lax.scan(delta_pass, jnp.zeros(stat_shape, jnp.float32), jnp.arange(block_count))

    def make_pass():

        def query_pass(query_acc, index):
            key_part, value_part, key_places = key_block(index)
            weights = jnp.exp(
                masked_scores(queries, places, key_part, key_places) - log_total[..., None]
            )
            slopes = jnp.einsum(
                "rqhd,rkhd->rhqk", d_attended, value_part, preferred_element_type=jnp.float32
            )
            score_grad = (weights * (slopes - delta[..., None])).astype(jnp.bfloat16)
            query_acc = query_acc + 0.125 * jnp.einsum(
                "rhqk,rkhd->rqhd", score_grad, key_part, preferred_element_type=jnp.float32
            )
            key_grad = 0.125 * jnp.einsum(
                "rhqk,rqhd->rkhd", score_grad, queries, preferred_element_type=jnp.float32
            )
            value_grad = jnp.einsum(
                "rhqk,rqhd->rkhd",
                weights.astype(jnp.bfloat16),
                d_attended,
                preferred_element_type=jnp.float32,
            )
            return (query_acc, (key_grad, value_grad))

        return query_pass

    d_query, (key_parts, value_parts) = lax.scan(
        make_pass(), jnp.zeros(head_shape, jnp.float32), jnp.arange(block_count)
    )
    key_whole = jnp.moveaxis(key_parts, 0, 1).reshape(seq_rows, row_len, width)
    value_whole = jnp.moveaxis(value_parts, 0, 1).reshape(seq_rows, row_len, width)
    key_value = lax.psum_scatter(
        jnp.concatenate([key_whole, value_whole], axis=-1), "fsdp", scatter_dimension=1, tiled=True
    )
    d_key = key_value[..., :width].reshape(head_shape)
    d_value = key_value[..., width:].reshape(head_shape)
    d_qkv = (
        jnp.stack([rotate_back(d_query, places), rotate_back(d_key, places), d_value], axis=2)
        .reshape(-1, 3 * width)
        .astype(jnp.bfloat16)
    )
    grad_qkv = first_dot(normed_one, d_qkv)
    d_one = last_dot(d_qkv, dense_copy[:, : 3 * width]).reshape(seq_rows, local_len, width)
    d_in_norm, grad_gain_one = norm_back(d_one, scaled_one, inverse_one, gain_one)
    d_tokens = (d_middle + d_in_norm).astype(jnp.bfloat16)
    grad_dense = jnp.concatenate([grad_qkv, grad_wout, grad_shared], axis=1)
    grad_gains = jnp.stack([grad_gain_one, grad_gain_two])
    part_dense, part_router, part_down, part_gains = (
        lax.psum_scatter(grad_dense, ("dp", "fsdp"), scatter_dimension=0, tiled=True),
        lax.psum_scatter(grad_router, ("dp", "fsdp"), scatter_dimension=0, tiled=True),
        lax.psum_scatter(grad_down, ("dp", "fsdp"), scatter_dimension=0, tiled=True),
        lax.psum_scatter(grad_gains, ("dp", "fsdp"), scatter_dimension=1, tiled=True),
    )
    total_slots = seq_rows * lax.axis_size("dp") * row_len
    gain_rate = 0.1 / math.sqrt(total_slots)
    new_gain_moms = GAIN_DECAY * gain_moms + part_gains
    new_gains = gains - gain_rate * new_gain_moms
    new_mom_dense = MUON_DECAY * mom_dense + part_dense
    new_mom_router = MUON_DECAY * mom_router + part_router
    new_mom_down = MUON_DECAY * mom_down + part_down
    device_index = lax.axis_index(("dp", "fsdp"))
    device_count = lax.axis_size(("dp", "fsdp"))
    owners = [number * device_count // 6 for number in range(6)]

    def owned(number, matrix):
        return lax.cond(device_index == owners[number], orthogonal, jnp.zeros_like, matrix)

    edges = (0, 3 * width, 4 * width, 4 * width + ff_shared, 4 * width + 2 * ff_shared)
    whole_dense, whole_router, whole_down = (
        lax.all_gather(new_mom_dense, ("dp", "fsdp"), axis=0, tiled=True),
        lax.all_gather(new_mom_router, ("dp", "fsdp"), axis=0, tiled=True),
        lax.all_gather(new_mom_down, ("dp", "fsdp"), axis=0, tiled=True),
    )
    orth_dense = jnp.concatenate(
        [owned(number, whole_dense[:, edges[number] : edges[number + 1]]) for number in range(4)],
        axis=1,
    )
    orth_router = owned(4, whole_router)
    orth_down = owned(5, whole_down)
    share_dense, share_router, share_down = (
        lax.psum_scatter(orth_dense, ("dp", "fsdp"), scatter_dimension=0, tiled=True),
        lax.psum_scatter(orth_router, ("dp", "fsdp"), scatter_dimension=0, tiled=True),
        lax.psum_scatter(orth_down, ("dp", "fsdp"), scatter_dimension=0, tiled=True),
    )
    column_rates = jnp.concatenate(
        [
            jnp.full((edges[number + 1] - edges[number],), DENSE_RATES[number], jnp.float32)
            for number in range(4)
        ]
    )
    new_dense = w_dense - column_rates[None, :] * share_dense
    new_router = w_router - ROUTER_RATE * share_router
    new_down = w_down - DOWN_RATE * share_down
    dp_index = lax.axis_index("dp")
    gate_rows = e_gate_up.shape[2]
    down_rows = e_down.shape[1]
    gate_term = jnp.stack([grad_gate, grad_up])[None] + lax.dynamic_update_slice(
        jnp.zeros((1, 2, width, ff_width), jnp.float32),
        MUON_DECAY * e_mom_gate_up,
        (0, 0, dp_index * gate_rows, 0),
    )
    down_term = grad_edown[None] + lax.dynamic_update_slice(
        jnp.zeros((1, ff_width, width), jnp.float32),
        MUON_DECAY * e_mom_down,
        (0, dp_index * down_rows, 0),
    )
    whole_gate_up, whole_edown = lax.psum((gate_term, down_term), "dp")
    orth_gate_up = jnp.stack([orthogonal(whole_gate_up[0, 0]), orthogonal(whole_gate_up[0, 1])])[
        None
    ]
    orth_edown = orthogonal(whole_edown[0])[None]
    new_e_mom_gate_up = lax.dynamic_slice_in_dim(whole_gate_up, dp_index * gate_rows, gate_rows, 2)
    gate_rates = jnp.array(EXPERT_RATES[:2], jnp.float32)[None, :, None, None]
    new_e_gate_up = e_gate_up - gate_rates * lax.dynamic_slice_in_dim(
        orth_gate_up, dp_index * gate_rows, gate_rows, 2
    )
    new_e_mom_down = lax.dynamic_slice_in_dim(whole_edown, dp_index * down_rows, down_rows, 1)
    new_e_down = e_down - EXPERT_RATES[2] * lax.dynamic_slice_in_dim(
        orth_edown, dp_index * down_rows, down_rows, 1
    )
    return (
        output,
        d_tokens,
        new_gain_moms,
        new_gains,
        new_mom_dense,
        new_dense,
        new_mom_router,
        new_router,
        new_mom_down,
        new_down,
        new_e_mom_gate_up,
        new_e_gate_up,
        new_e_mom_down,
        new_e_down,
    )


DP = 8
FS = 4
AXES = ("dp", "fsdp")
LANES = 128
VMEM_BYTES = 60 * 2**20
LINE = 4
OWNERS = ((0, 3, 4, 7), (1, 2, 5, 6), (0, 3, 4, 7), (1, 2, 5, 6, 4))
TALL_SLOTS = (3, 4)
DOWN_COLUMN = 3


def tn_dot(left, right):
    return lax.dot_general(
        left, right, (((0,), (0,)), ((), ())), preferred_element_type=jnp.float32
    )


def nt_dot(left, right):
    return lax.dot_general(
        left, right, (((1,), (1,)), ((), ())), preferred_element_type=jnp.float32
    )


def kernel_call(body, out_shape, flops, bytes_accessed, **options):
    return pl.pallas_call(
        body,
        out_shape=out_shape,
        compiler_params=pltpu.CompilerParams(vmem_limit_bytes=VMEM_BYTES),
        cost_estimate=pl.CostEstimate(
            flops=int(flops), bytes_accessed=int(bytes_accessed), transcendentals=0
        ),
        **options,
    )


def shape_of(shape, dtype=jnp.bfloat16):
    return jax.ShapeDtypeStruct(shape, dtype)


def whole_block(shape):
    return pl.BlockSpec(shape, lambda *_: (0,) * len(shape))


def after(value, *events):
    return lax.optimization_barrier((value,) + events)[0]


def fsdp_hop(value, step):
    pairs = [(d * FS + f, d * FS + (f ^ step)) for d in range(DP) for f in range(FS)]
    return lax.ppermute(value, AXES, pairs)


def by_source(own, near, far, cross, index):
    low_x, even = index < 2, index % 2 == 0
    own_low, own_high = jnp.where(low_x, own, far), jnp.where(low_x, far, own)
    near_low, near_high = jnp.where(low_x, near, cross), jnp.where(low_x, cross, near)
    return [
        jnp.where(even, own_low, near_low),
        jnp.where(even, near_low, own_low),
        jnp.where(even, own_high, near_high),
        jnp.where(even, near_high, own_high),
    ]


def gather_fsdp(block, index):
    far = fsdp_hop(block, 2)
    near = fsdp_hop(block, 1)
    cross = fsdp_hop(far, 1)
    return by_source(block, near, far, cross, index)


def exchange_fsdp(blocks, index):
    pick = lambda step: lax.dynamic_index_in_dim(blocks, index ^ step, 0, keepdims=False)
    got = [pick(0)] + [fsdp_hop(pick(step), step) for step in (1, 2, 3)]
    return by_source(*got, index)


def reduce_fsdp(blocks, index):
    core, place = index % 2, index // 2
    pairs = blocks.reshape((2, 2) + blocks.shape[1:])
    send = lax.dynamic_index_in_dim(pairs, 1 - core, 1, keepdims=False)
    keep = lax.dynamic_index_in_dim(pairs, core, 1, keepdims=False)
    both = keep.astype(jnp.float32) + fsdp_hop(send, 1).astype(jnp.float32)
    away = lax.dynamic_index_in_dim(both, 1 - place, 0, keepdims=False).astype(blocks.dtype)
    here = lax.dynamic_index_in_dim(both, place, 0, keepdims=False)
    return here + fsdp_hop(away, 2).astype(jnp.float32)


def sum_everywhere(value):
    for d_step, f_step in ((0, 1), (0, 2), (1, 0), (2, 0), (4, 0)):
        pairs = [
            (d * FS + f, (d ^ d_step) * FS + (f ^ f_step)) for d in range(DP) for f in range(FS)
        ]
        value = value + lax.ppermute(value, AXES, pairs)
    return value


def swap_halves(values, half_size):
    width = values.shape[1]
    lane = lax.broadcasted_iota(jnp.int32, values.shape, 1)
    return jnp.where(
        lane % (2 * half_size) < half_size,
        -pltpu.roll(values, width - half_size, 1),
        pltpu.roll(values, half_size, 1),
    )


def attention_body(
    lengths_ref, x_ref, gain_ref, w_ref, cos_ref, sin_ref, normed_ref, qkv_ref, prob_ref, att_ref
):
    head_count, row_len = prob_ref.shape[1], prob_ref.shape[2]
    wide = w_ref.shape[1] // 3
    head_size = wide // head_count
    x = x_ref[0].astype(jnp.float32)
    inverse = lax.rsqrt(jnp.mean(x * x, axis=-1, keepdims=True) + NORM_EPSILON)
    normed = (x * inverse * gain_ref[...]).astype(jnp.bfloat16)
    normed_ref[...] = normed.T
    projected = jnp.dot(normed, w_ref[...], preferred_element_type=jnp.float32)
    both = projected[:, : 2 * wide]
    both = both * cos_ref[...] + swap_halves(both, head_size // 2) * sin_ref[...]
    both = both.astype(jnp.bfloat16)
    values = projected[:, 2 * wide :].astype(jnp.bfloat16)
    qkv_ref[0, :, : 2 * wide] = both
    qkv_ref[0, :, 2 * wide :] = values
    length = lengths_ref[pl.program_id(0)]
    row = lax.broadcasted_iota(jnp.int32, (row_len, row_len), 0)
    column = lax.broadcasted_iota(jnp.int32, (row_len, row_len), 1)
    allowed = (column <= row) & (column < length)
    parts = []
    for head in range(head_count):
        span = slice(head * head_size, (head + 1) * head_size)
        scores = nt_dot(both[:, span], both[:, wide:][:, span]) * 0.125
        scores = jnp.where(allowed, scores, MASK_VALUE)
        weights = jnp.exp(scores - jnp.max(scores, axis=-1, keepdims=True))
        share = 1.0 / jnp.sum(weights, axis=-1, keepdims=True)
        probs = (weights * share).astype(jnp.bfloat16)
        prob_ref[0, head] = probs
        parts.append(jnp.dot(probs, values[:, span], preferred_element_type=jnp.float32))
    att_ref[0] = jnp.concatenate(parts, axis=1).astype(jnp.bfloat16)


def attention_forward(x, gain, weight, cosine, sine, lengths):
    rows, row_len, width = x.shape
    columns = weight.shape[1]
    heads = columns // 3 // (width // HEADS)
    return kernel_call(
        attention_body,
        (
            shape_of((width, rows * row_len)),
            shape_of((rows, row_len, columns)),
            shape_of((rows, heads, row_len, row_len)),
            shape_of((rows, row_len, columns // 3)),
        ),
        6e9,
        12e6,
        grid=(rows,),
        in_specs=[
            pl.BlockSpec(memory_space=pltpu.SMEM),
            pl.BlockSpec((1, row_len, width), lambda r: (r, 0, 0)),
            whole_block(gain.shape),
            whole_block(weight.shape),
            whole_block(cosine.shape),
            whole_block(sine.shape),
        ],
        out_specs=(
            pl.BlockSpec((width, row_len), lambda r: (0, r)),
            pl.BlockSpec((1, row_len, columns), lambda r: (r, 0, 0)),
            pl.BlockSpec((1, heads, row_len, row_len), lambda r: (r, 0, 0, 0)),
            pl.BlockSpec((1, row_len, columns // 3), lambda r: (r, 0, 0)),
        ),
        name="attention_forward",
    )(lengths, x, gain, weight, cosine, sine)


def attention_back_body(
    normed_ref, qkv_ref, prob_ref, d_att_ref, w_ref, cos_ref, sin_ref, grad_ref, back_ref, total
):
    head_count = prob_ref.shape[1]
    wide = w_ref.shape[1] // 3
    head_size = wide // head_count
    qkv = qkv_ref[0]
    d_att = d_att_ref[0]
    grads = ([], [], [])
    for head in range(head_count):
        span = slice(head * head_size, (head + 1) * head_size)
        query, key, value = (qkv[:, i * wide : (i + 1) * wide][:, span] for i in range(3))
        probs = prob_ref[0, head]
        weights = probs.astype(jnp.float32)
        slopes = nt_dot(d_att[:, span], value)
        delta = jnp.sum(weights * slopes, axis=-1, keepdims=True)
        d_scores = (weights * (slopes - delta)).astype(jnp.bfloat16)
        grads[0].append(0.125 * jnp.dot(d_scores, key, preferred_element_type=jnp.float32))
        grads[1].append(0.125 * tn_dot(d_scores, query))
        grads[2].append(tn_dot(probs, d_att[:, span]))
    both = jnp.concatenate(grads[0] + grads[1], axis=1)
    both = both * cos_ref[...] - swap_halves(both, head_size // 2) * sin_ref[...]
    d_qkv = jnp.concatenate([both] + grads[2], axis=1).astype(jnp.bfloat16)
    grad = jnp.dot(normed_ref[...], d_qkv, preferred_element_type=jnp.float32)

    @pl.when(pl.program_id(0) == 0)
    def _():
        total[...] = grad

    @pl.when(pl.program_id(0) > 0)
    def _():
        total[...] += grad

    grad_ref[...] = total[...].astype(jnp.bfloat16)
    back_ref[0] = nt_dot(d_qkv, w_ref[...]).astype(jnp.bfloat16)


def attention_backward(normed, qkv, probs, d_att, weight, cosine, sine):
    rows, row_len, columns = qkv.shape
    width, heads = weight.shape[0], probs.shape[1]
    return kernel_call(
        attention_back_body,
        (shape_of((width, columns)), shape_of((rows, row_len, width))),
        8e9,
        12e6,
        grid=(rows,),
        in_specs=[
            pl.BlockSpec((width, row_len), lambda r: (0, r)),
            pl.BlockSpec((1, row_len, columns), lambda r: (r, 0, 0)),
            pl.BlockSpec((1, heads, row_len, row_len), lambda r: (r, 0, 0, 0)),
            pl.BlockSpec((1, row_len, columns // 3), lambda r: (r, 0, 0)),
            whole_block(weight.shape),
            whole_block(cosine.shape),
            whole_block(sine.shape),
        ],
        out_specs=(
            whole_block((width, columns)),
            pl.BlockSpec((1, row_len, width), lambda r: (r, 0, 0)),
        ),
        scratch_shapes=[pltpu.VMEM((width, columns), jnp.float32)],
        name="attention_backward",
    )(normed, qkv, probs, d_att, weight, cosine, sine)


def middle_body(
    att_ref, x_ref, routes_ref, wout_ref, router_ref, gain_ref, mid_ref, normed_ref, turned_ref, gates_ref
):
    branch = jnp.dot(att_ref[...], wout_ref[...], preferred_element_type=jnp.float32)
    mid = x_ref[...].astype(jnp.float32) + branch
    inverse = lax.rsqrt(jnp.mean(mid * mid, axis=-1, keepdims=True) + NORM_EPSILON)
    normed = (mid * inverse * gain_ref[...]).astype(jnp.bfloat16)
    logits = jnp.dot(normed, router_ref[...], preferred_element_type=jnp.float32)
    lane = lax.broadcasted_iota(jnp.int32, logits.shape, 1)
    first, second = lane == routes_ref[:, 0:1], lane == routes_ref[:, 1:2]
    one = jnp.sum(jnp.where(first, logits, 0.0), axis=-1, keepdims=True)
    two = jnp.sum(jnp.where(second, logits, 0.0), axis=-1, keepdims=True)
    top = jnp.maximum(one, two)
    one, two = jnp.exp(one - top), jnp.exp(two - top)
    share = 1.0 / (one + two)
    mid_ref[...] = mid
    normed_ref[...] = normed
    turned_ref[...] = normed.T
    gates_ref[...] = jnp.where(first, one * share, 0.0) + jnp.where(second, two * share, 0.0)


def middle_forward(attended, x, routes, wout, router, gain):
    count, width = x.shape
    tile = min(256, count)
    rows = lambda i: (i, 0)
    return kernel_call(
        middle_body,
        (
            shape_of((count, width), jnp.float32),
            shape_of((count, width)),
            shape_of((width, count)),
            shape_of((count, LANES), jnp.float32),
        ),
        2 * count * width * width,
        12e6,
        grid=(count // tile,),
        in_specs=[
            pl.BlockSpec((tile, width), rows),
            pl.BlockSpec((tile, width), rows),
            pl.BlockSpec((tile, routes.shape[1]), rows),
            whole_block(wout.shape),
            whole_block(router.shape),
            whole_block(gain.shape),
        ],
        out_specs=(
            pl.BlockSpec((tile, width), rows),
            pl.BlockSpec((tile, width), rows),
            pl.BlockSpec((width, tile), lambda i: (0, i)),
            pl.BlockSpec((tile, LANES), rows),
        ),
        name="middle_forward",
    )(attended, x, routes, wout, router, gain)


def middle_back_body(
    mid_ref, d_out_ref, d_sum_ref, gates_ref, routes_ref, att_ref, normed_ref, wout_ref, router_ref,
    gain_ref, d_mid_ref, d_att_ref, grad_wout_ref, grad_router_ref, grad_gain_ref,
):
    width = mid_ref.shape[1]
    gates = gates_ref[...]
    lane = lax.broadcasted_iota(jnp.int32, gates.shape, 1)
    half = LANES // 2
    first, second = routes_ref[:, 0:1], routes_ref[:, 1:2]
    slopes = d_sum_ref[:, width:]

    def pick(table, place):
        return jnp.sum(jnp.where(lane == place, table, 0.0), axis=-1, keepdims=True)

    gate_one, gate_two = pick(gates, first), pick(gates, second)
    slope_one = pick(slopes, first) + pick(slopes, first + half)
    slope_two = pick(slopes, second) + pick(slopes, second + half)
    common = gate_one * slope_one + gate_two * slope_two
    d_logits = jnp.where(lane == first, gate_one * (slope_one - common), 0.0)
    d_logits = d_logits + jnp.where(lane == second, gate_two * (slope_two - common), 0.0)
    d_logits = d_logits.astype(jnp.bfloat16)
    grad_router_ref[...] = tn_dot(d_logits, normed_ref[...])
    d_normed = d_sum_ref[:, :width] + nt_dot(d_logits, router_ref[...])
    mid = mid_ref[...]
    inverse = lax.rsqrt(jnp.mean(mid * mid, axis=-1, keepdims=True) + NORM_EPSILON)
    scaled = mid * inverse
    grad_gain_ref[...] = jnp.sum(d_normed * scaled, axis=0, keepdims=True)
    through = d_normed * gain_ref[...]
    d_norm = inverse * (through - scaled * jnp.mean(through * scaled, axis=-1, keepdims=True))
    d_mid = d_out_ref[...].astype(jnp.float32) + d_norm
    d_mid_ref[...] = d_mid
    d_branch = d_mid.astype(jnp.bfloat16)
    grad_wout_ref[...] = tn_dot(att_ref[...], d_branch).astype(jnp.bfloat16)
    d_att_ref[...] = nt_dot(d_branch, wout_ref[...]).astype(jnp.bfloat16)


def middle_backward(*operands):
    count, width = operands[0].shape
    return kernel_call(
        middle_back_body,
        (
            shape_of((count, width), jnp.float32),
            shape_of((count, width)),
            shape_of((width, width)),
            shape_of((LANES, width), jnp.float32),
            shape_of((1, width), jnp.float32),
        ),
        4 * count * width * width,
        8e6,
        name="middle_backward",
    )(*operands)


def branch_step(normed_ref, turned_ref, d_out_ref, gate_column, weights, grads):
    both_weight, down_weight = weights
    tile = down_weight.shape[0]
    normed, d_out = normed_ref[...], d_out_ref[...]
    both = jnp.dot(normed, both_weight, preferred_element_type=jnp.float32)
    gate, up = both[:, :tile], both[:, tile:]
    slope = nt_dot(d_out, down_weight)
    logistic = 1.0 / (1.0 + jnp.exp(-gate))
    silu = gate * logistic
    act = silu * up
    d_gate = None
    if gate_column is not None:
        d_gate = jnp.sum(act * slope, axis=-1, keepdims=True)
        act = act * gate_column
        slope = slope * gate_column
    act = act.astype(jnp.bfloat16)
    d_both = jnp.concatenate(
        [
            (slope * up * (logistic * (1.0 + gate * (1.0 - logistic)))).astype(jnp.bfloat16),
            (slope * silu).astype(jnp.bfloat16),
        ],
        axis=1,
    )
    grads[0][...] = jnp.dot(
        turned_ref[...], d_both, preferred_element_type=jnp.float32
    ).astype(jnp.bfloat16)
    grads[1][...] = tn_dot(act, d_out).astype(jnp.bfloat16)
    out = jnp.dot(act, down_weight, preferred_element_type=jnp.float32)
    return out, nt_dot(d_both, both_weight), d_gate


def branch_body(
    expert_ref, normed_ref, turned_ref, d_out_ref, *refs, routed, chained, last
):
    refs = list(refs)
    gates_ref = refs.pop(0) if routed else None
    first = [refs.pop(0) for _ in range(3 if routed else 2)] if chained else None
    gate_ref, up_ref, down_ref, out_ref, back_ref = refs[:5]
    slope_ref = refs[5] if routed and not last else None
    grad_pair_ref, grad_down_ref = refs[6:8] if slope_ref is not None else refs[5:7]
    totals = refs[-3:]
    step = pl.program_id(0)
    out, back, d_gate = branch_step(
        normed_ref,
        turned_ref,
        d_out_ref,
        gates_ref[...] if routed else None,
        (jnp.concatenate([gate_ref[...], up_ref[...]], axis=1), down_ref[...]),
        (grad_pair_ref, grad_down_ref),
    )
    parts = [out, back] + ([d_gate] if routed else [])

    @pl.when(step == 0)
    def _():
        for i, part in enumerate(parts):
            kept = chained and i < len(first)
            totals[i][...] = first[i][...] + part if kept else part

    @pl.when(step > 0)
    def _():
        for i, part in enumerate(parts):
            totals[i][...] += part

    @pl.when(step == pl.num_programs(0) - 1)
    def _():
        if not last:
            out_ref[...] = totals[0][...]
            back_ref[...] = totals[1][...]
            if routed:
                slope_ref[...] = totals[2][...]
            return
        width = out_ref.shape[1]
        out_ref[...] = totals[0][...].astype(jnp.bfloat16)
        back_ref[:, :width] = totals[1][...].astype(jnp.bfloat16)
        slopes = totals[2][...]
        high = slopes.astype(jnp.bfloat16).astype(jnp.float32)
        lane = lax.broadcasted_iota(jnp.int32, (slopes.shape[0], LANES), 1)
        table = jnp.where(lane == expert_ref[0], high, 0.0)
        table = jnp.where(lane == expert_ref[0] + LANES // 2, slopes - high, table)
        back_ref[:, width:] = table.astype(jnp.bfloat16)


def branch(expert, normed, turned, d_out, gates, first, weights, blocks, last, name):
    (gate, gate_spec), (up, up_spec), down = weights
    count, width = normed.shape
    start, end, tile = blocks
    routed, chained = gates is not None, first is not None
    hidden = (end - start) * tile
    once = lambda shape: pl.BlockSpec(
        shape, lambda *_: (0,) * len(shape), pipeline_mode=pl.Buffered(1)
    )
    operands = [expert, normed, turned, d_out]
    if routed:
        operands.append(gates)
    if chained:
        operands += first
    full = [once(array.shape) for array in operands[1:]]
    outs = [shape_of((count, width), jnp.float32), shape_of((count, width), jnp.float32)]
    if routed and not last:
        outs.append(shape_of((count, 1), jnp.float32))
    if last:
        outs = [shape_of((count, width)), shape_of((count, width + LANES))]
    return kernel_call(
        functools.partial(branch_body, routed=routed, chained=chained, last=last),
        outs + [shape_of((width, 2 * hidden)), shape_of((hidden, width))],
        18 * count * width * hidden,
        12 * width * hidden + 16 * count * width,
        grid=(end - start,),
        in_specs=[pl.BlockSpec(memory_space=pltpu.SMEM)]
        + full
        + [gate_spec, up_spec, pl.BlockSpec((tile, width), lambda j: (start + j, 0))],
        out_specs=[once(out.shape) for out in outs]
        + [
            pl.BlockSpec((width, 2 * tile), lambda j: (0, j)),
            pl.BlockSpec((tile, width), lambda j: (j, 0)),
        ],
        scratch_shapes=[
            pltpu.VMEM((count, width), jnp.float32),
            pltpu.VMEM((count, width), jnp.float32),
            pltpu.VMEM((count, 1), jnp.float32),
        ],
        name=name,
    )(*operands, gate, up, down)


def orthogonal_body(info_ref, *refs):
    shards, results = refs[:DP], refs[DP : 2 * DP]
    current, gram, poly = refs[2 * DP :]
    size, length = current.shape
    kind, place = info_ref[0], info_ref[1]
    rows = shards[0].shape[0]
    columns = 2 * LANES
    tile = 256
    tiles = size // tile
    chunks = length // tile

    def spot(k, extent):
        return pl.multiple_of(lax.rem(place + k, DP) * extent, extent)

    def folds(k):
        for j in range(size // rows):
            yield (
                (slice(j * rows, (j + 1) * rows), pl.ds(spot(k, columns), columns)),
                (slice(None), slice(j * columns, (j + 1) * columns)),
            )

    @pl.when(kind == 1)
    def _():
        for k in range(DP):
            current[pl.ds(spot(k, rows), rows), :] = shards[k][...]

    @pl.when(kind == 2)
    def _():
        current[:, DP * columns :] = jnp.zeros((size, length - DP * columns), jnp.bfloat16)
        for k in range(DP):
            for there, here in folds(k):
                current[there] = shards[k][here]

    @pl.when(kind > 0)
    def _():
        def square(c, total):
            part = current[:, pl.ds(pl.multiple_of(c * tile, tile), tile)].astype(jnp.float32)
            return total + jnp.sum(part * part, axis=0, keepdims=True)

        squares = lax.fori_loop(0, chunks, square, jnp.zeros((1, tile), jnp.float32))
        scale = 1.0 / (jnp.sqrt(jnp.sum(squares, axis=1, keepdims=True)) + 1e-07)

        def scale_chunk(c, carry):
            span = pl.ds(pl.multiple_of(c * tile, tile), tile)
            part = current[:, span].astype(jnp.float32)
            current[:, span] = (part * scale).astype(jnp.bfloat16)
            return carry

        lax.fori_loop(0, chunks, scale_chunk, 0)

        def sweep(_, carry):
            for i in range(tiles):
                block = nt_dot(current[i * tile : (i + 1) * tile, :], current[i * tile :, :])
                gram[i * tile : (i + 1) * tile, i * tile :] = block.astype(jnp.bfloat16)
                poly[i * tile : (i + 1) * tile, i * tile :] = POLY_SECOND * block
            for i in range(tiles):
                for j in range(i):
                    gram[i * tile : (i + 1) * tile, j * tile : (j + 1) * tile] = gram[
                        j * tile : (j + 1) * tile, i * tile : (i + 1) * tile
                    ].T
            for i in range(tiles):
                block = jnp.dot(
                    gram[i * tile : (i + 1) * tile, :],
                    gram[:, i * tile :],
                    preferred_element_type=jnp.float32,
                )
                poly[i * tile : (i + 1) * tile, i * tile :] += POLY_THIRD * block
            for i in range(tiles):
                gram[i * tile : (i + 1) * tile, i * tile :] = poly[
                    i * tile : (i + 1) * tile, i * tile :
                ].astype(jnp.bfloat16)
            for i in range(tiles):
                for j in range(i):
                    gram[i * tile : (i + 1) * tile, j * tile : (j + 1) * tile] = gram[
                        j * tile : (j + 1) * tile, i * tile : (i + 1) * tile
                    ].T

            def update(c, carry):
                span = pl.ds(pl.multiple_of(c * tile, tile), tile)
                part = current[:, span]
                fresh = POLY_FIRST * part.astype(jnp.float32) + jnp.dot(
                    gram[...], part, preferred_element_type=jnp.float32
                )
                current[:, span] = fresh.astype(jnp.bfloat16)
                return carry

            return lax.fori_loop(0, chunks, update, carry)

        lax.fori_loop(0, NS_STEPS, sweep, 0)

    @pl.when(kind == 1)
    def _():
        for k in range(DP):
            results[k][...] = current[pl.ds(spot(k, rows), rows), :]

    @pl.when(kind == 2)
    def _():
        for k in range(DP):
            for there, here in folds(k):
                results[k][here] = current[there]


def orthogonal_shards(info, shards, size):
    rows, length = shards[0].shape
    vmem = pl.BlockSpec(memory_space=pltpu.VMEM)
    return kernel_call(
        orthogonal_body,
        [shape_of((rows, length))] * DP,
        26e9,
        8e6,
        in_specs=[pl.BlockSpec(memory_space=pltpu.SMEM)] + [vmem] * DP,
        out_specs=[vmem] * DP,
        scratch_shapes=[
            pltpu.VMEM((size, length), jnp.bfloat16),
            pltpu.VMEM((size, size), jnp.bfloat16),
            pltpu.VMEM((size, size), jnp.float32),
        ],
        name="orthogonal_shards",
    )(info, *shards)


def fold_tall(block, rows, length):
    columns, size = block.shape
    block = block.T.reshape(size // rows, rows, columns).transpose(1, 0, 2).reshape(rows, -1)
    return jnp.pad(block, ((0, 0), (0, length - block.shape[1])))


def unfold_tall(block, columns):
    rows = block.shape[0]
    size = rows * DP
    block = block[:, : size // rows * columns].reshape(rows, size // rows, columns)
    return block.transpose(1, 0, 2).reshape(size, columns).T


def orthogonal_router_body(matrix_ref, out_ref):
    current = matrix_ref[...]
    dot = functools.partial(
        lax.dot_general, precision=HIGHEST_PRECISION, preferred_element_type=jnp.float32
    )
    square = jnp.sum(jnp.sum(current * current, axis=1, keepdims=True), axis=0, keepdims=True)
    current = current / (jnp.sqrt(square) + 1e-07)
    for _ in range(NS_STEPS):
        gram = dot(current, current, (((1,), (1,)), ((), ())))
        poly = POLY_SECOND * gram + POLY_THIRD * dot(gram, gram, (((1,), (0,)), ((), ())))
        current = POLY_FIRST * current + dot(poly, current, (((1,), (0,)), ((), ())))
    out_ref[...] = current


def orthogonal_router(matrix):
    return kernel_call(
        orthogonal_router_body, shape_of(matrix.shape, jnp.float32), 2e9, 1e6, name="orthogonal_router"
    )(matrix)


def slot_table(owners):
    table = np.zeros((FS, DP), np.int32)
    for f, column in enumerate(owners):
        for slot, d in enumerate(column):
            table[f, d] = slot
    return table


def owner_pairs(owners, step, back):
    pairs = []
    for f, column in enumerate(owners):
        for d in column:
            other = (d + step) % DP
            pair = (other * FS + f, d * FS + f)
            pairs.append(pair[::-1] if back else pair)
    return pairs


def to_owners(stack, owners, dp_index, index):
    table = jnp.asarray(slot_table(owners))[index]
    got = []
    for step in range(DP):
        slot = table[lax.rem(dp_index - step + DP, DP)]
        block = lax.dynamic_index_in_dim(stack, slot, 0, keepdims=False)
        got.append(
            block if step == 0 else lax.ppermute(block, AXES, owner_pairs(owners, step, False))
        )
    return got


def from_owners(blocks, owners, dp_index, index):
    got = jnp.stack(
        [
            block if step == 0 else lax.ppermute(block, AXES, owner_pairs(owners, step, True))
            for step, block in enumerate(blocks)
        ]
    )
    count = max(len(column) for column in owners)
    table = np.array([list(column) + [0] * (count - len(column)) for column in owners], np.int32)
    places = jnp.asarray(table)[index]
    return [
        lax.dynamic_index_in_dim(got, lax.rem(dp_index - places[slot] + DP, DP), 0, keepdims=False)
        for slot in range(count)
    ]


def line_hop(value, step):
    pairs = [
        ((z * 2 + y) * FS + f, ((z + step) % LINE * 2 + y) * FS + f)
        for z in range(LINE)
        for y in range(2)
        for f in range(FS)
    ]
    return lax.ppermute(value, AXES, pairs)


def pair_hop(value):
    pairs = [(d * FS + f, (d ^ 1) * FS + f) for d in range(DP) for f in range(FS)]
    return lax.ppermute(value, AXES, pairs)


def place_body(places_ref, *refs):
    out_ref = refs[-1]
    rows = refs[0].shape[0]
    other_ref = refs[-2]
    for i, ref in enumerate(refs[:-2]):
        out_ref[pl.ds(pl.multiple_of(places_ref[i] * rows, rows), rows), :] = ref[...]
        start = pl.multiple_of(places_ref[LINE + i] * rows, rows)
        out_ref[pl.ds(start, rows), :] = other_ref[i]


class Gather:
    def __init__(self, block, place):
        _, self.side, self.level = place
        self.blocks = [block] + [line_hop(block, step) for step in range(1, LINE)]

    def cross(self, *events):
        self.stack = jnp.stack(self.blocks)
        if events:
            self.stack = after(self.stack, *events)
        self.other = pair_hop(self.stack)
        return self.other

    def last(self):
        levels = lax.rem(self.level + LINE - jnp.arange(LINE), LINE)
        places = jnp.concatenate([levels * 2 + self.side, levels * 2 + 1 - self.side])
        rows, columns = self.blocks[0].shape
        vmem = pl.BlockSpec(memory_space=pltpu.VMEM)
        return kernel_call(
            place_body,
            shape_of((DP * rows, columns), self.stack.dtype),
            0,
            4 * DP * rows * columns,
            in_specs=[pl.BlockSpec(memory_space=pltpu.SMEM)] + [vmem] * (LINE + 1),
            out_specs=vmem,
            name="place_rows",
        )(places.astype(jnp.int32), *self.blocks, self.other)


class Reduce:
    def __init__(self, grads, place):
        _, self.side, self.level = place
        rows, columns = grads.shape
        self.grads = grads.reshape(LINE, 2, rows // DP, columns)

    def pick(self, array, i, axis=0):
        return lax.dynamic_index_in_dim(array, i, axis, keepdims=False)

    def cross(self, *events):
        grads = after(self.grads, *events) if events else self.grads
        self.got = pair_hop(self.pick(grads, 1 - self.side, 1))
        return self.got

    def along(self, *events):
        got = after(self.got, *events) if events else self.got
        mine = self.pick(self.grads, self.side, 1)
        both = (mine.astype(jnp.float32) + got.astype(jnp.float32)).astype(mine.dtype)
        at = lambda step: self.pick(both, lax.rem(self.level + step, LINE))
        self.parts = [at(0)] + [line_hop(at(step), step) for step in range(1, LINE)]
        return self.parts[1]

    def last(self):
        return sum(part.astype(jnp.float32) for part in self.parts)


def split_plan(
    tokens,
    cotangent,
    lengths,
    routes,
    gains,
    gain_moms,
    w_dense,
    mom_dense,
    w_router,
    mom_router,
    w_down,
    mom_down,
    e_gate_up,
    e_mom_gate_up,
    e_down,
    e_mom_down,
):
    index, dp_index = lax.axis_index("fsdp"), lax.axis_index("dp")
    device_index = dp_index * FS + index
    rows, local_len, width = tokens.shape
    row_len = local_len * FS
    count = rows * row_len
    experts = w_router.shape[1]
    head_size = width // HEADS
    quarter = width // FS
    block_rows = w_dense.shape[0]
    down_rows = w_down.shape[0]
    ff_shared = down_rows * DP * FS
    ff_part = down_rows * DP
    bf16 = jnp.bfloat16

    def by_columns(matrix):
        qkv_parts = [
            matrix[:, i * width : (i + 1) * width].reshape(block_rows, FS, quarter)
            for i in range(3)
        ]
        shared_parts = [
            matrix[:, 4 * width + i * ff_shared : 4 * width + (i + 1) * ff_shared]
            .reshape(block_rows, DP, FS, down_rows)
            .transpose(0, 2, 1, 3)
            .reshape(block_rows, FS, ff_part)
            for i in range(2)
        ]
        return jnp.concatenate(qkv_parts + shared_parts, axis=2).transpose(1, 0, 2)

    dense = w_dense.astype(bf16)
    own_columns = by_columns(dense)
    qkv_columns = own_columns[..., : 3 * quarter]
    common = jnp.concatenate(
        [
            w_router.astype(bf16),
            gains.astype(bf16).T,
            jnp.zeros((block_rows, LANES - experts - 2), bf16),
        ],
        axis=1,
    )
    spread = lambda array: jnp.broadcast_to(array, (FS,) + array.shape)
    place = (index, dp_index % 2, dp_index // 2)
    gate_up_copy = lax.all_gather(e_gate_up[0].astype(bf16), "dp", axis=1, tiled=True)
    edown_copy = lax.all_gather(e_down[0].astype(bf16), "dp", axis=0, tiled=True)
    message = jnp.concatenate([qkv_columns, spread(common)], axis=2)
    message = jnp.concatenate(exchange_fsdp(message, index), axis=0)
    folds = message.shape[0]
    fold_down, fold_out = down_rows * width // folds, block_rows * width // folds
    own_out = dense[:, 3 * width : 4 * width].reshape(folds, fold_out)
    first_pack = Gather(jnp.concatenate([message, own_out], axis=1), place)
    routes_low = jnp.concatenate(
        [routes.astype(bf16), jnp.zeros((rows, local_len, LANES - routes.shape[2]), bf16)], axis=2
    )
    inputs = jnp.concatenate(
        gather_fsdp(jnp.concatenate([tokens, routes_low], axis=2), index), axis=1
    )
    message = jnp.concatenate(exchange_fsdp(own_columns[..., 3 * quarter :], index), axis=0)
    message = after(message, *first_pack.blocks[1:])
    second_pack = Gather(
        jnp.concatenate([message, w_down.astype(bf16).reshape(folds, fold_down)], axis=1), place
    )
    first_pack.cross()
    pack = first_pack.last()
    w_qkv, w_route = pack[:, : 3 * quarter], pack[:, 3 * quarter : 3 * quarter + LANES]
    w_out = pack[:, 3 * quarter + LANES :].reshape(DP, block_rows, width)
    gain_rows = w_route[:, experts : experts + 2].astype(jnp.float32).T
    gain_one, gain_two = gain_rows[0:1], gain_rows[1:2]

    x_all = inputs[..., :width]
    route_all = inputs[..., width:].astype(jnp.int32).reshape(count, LANES)
    all_places = jnp.arange(row_len)
    valid_all = all_places[None, :] < lengths[:, None]
    half = head_size // 2
    frequency = 10000.0 ** (-2.0 * jnp.arange(half, dtype=jnp.float32) / head_size)
    angles = all_places.astype(jnp.float32)[:, None] * frequency[None, :]
    repeats = (1, 2 * quarter // half)
    cosine, sine = jnp.tile(jnp.cos(angles), repeats), jnp.tile(jnp.sin(angles), repeats)

    normed_one, qkv, probs, attended = attention_forward(
        x_all, gain_one, w_qkv, cosine, sine, lengths
    )
    cot_all = jnp.concatenate(gather_fsdp(after(cotangent, pack), index), axis=1)
    d_out_all = jnp.where(valid_all[..., None], cot_all, 0).reshape(count, width)
    attended_all = jnp.concatenate(gather_fsdp(attended, index), axis=2)
    w_out = jnp.stack(gather_fsdp(w_out, index), axis=1).reshape(width, width)
    second_pack.cross()
    pack = second_pack.last()
    w_shared = pack[:, : 2 * ff_part]
    down_copy = pack[:, 2 * ff_part :].reshape(DP * down_rows, width)
    mid_all, normed_all, turned_all, gates_all = middle_forward(
        after(attended_all, second_pack.other).reshape(count, width), x_all.reshape(count, width), route_all, w_out, w_route,
        gain_two,
    )
    gate_column = lax.dynamic_slice_in_dim(gates_all, index, 1, 1)
    expert = index.reshape(1)
    tile = min(512, ff_part)
    shared_tiles = ff_part // tile
    columns_at = lambda start: pl.BlockSpec((width, tile), lambda j: (0, start + j))
    first_out, first_back, grad_pair, grad_down = branch(
        expert, normed_all, turned_all, d_out_all, None, None,
        ((w_shared, columns_at(0)), (w_shared, columns_at(shared_tiles)), down_copy),
        (0, shared_tiles, tile), False, "shared_branch",
    )
    part_at = lambda start, half: pl.BlockSpec(
        (None, width, tile), lambda j: (half, 0, start + j)
    )
    ff_width = e_gate_up.shape[3]
    sum_shared = Reduce(
        jnp.concatenate([grad_pair, grad_down.reshape(width, fold_down)], axis=1), place
    )
    sum_shared.cross()
    out_part, message, grad_pairs, grad_edown = branch(
        expert, after(normed_all, sum_shared.got), turned_all, d_out_all, gate_column,
        [first_out, first_back, jnp.zeros((count, 1), jnp.float32)],
        ((gate_up_copy, part_at(0, 0)), (gate_up_copy, part_at(0, 1)), edown_copy),
        (0, ff_width // tile, tile), True, "expert_branch",
    )

    sum_shared.along()
    part_pairs = lax.psum_scatter(grad_pairs, "dp", scatter_dimension=0, tiled=True)
    sum_edown = Reduce(grad_edown, place)

    def by_place(values):
        return values.reshape(rows, FS, local_len, values.shape[-1]).transpose(1, 0, 2, 3)

    def own_rows(values):
        part = lax.dynamic_slice_in_dim(
            values.reshape(rows, row_len, values.shape[-1]), index * local_len, local_len, 1
        )
        return part.reshape(rows * local_len, values.shape[-1])

    d_sum = reduce_fsdp(by_place(after(message, *sum_shared.parts[1:])), index)
    d_sum = d_sum.reshape(rows * local_len, width + LANES)
    sum_edown.cross()
    mid = own_rows(mid_all)
    d_out = own_rows(d_out_all)
    d_mid, d_att, grad_wout, grad_router, grad_gain_two = middle_backward(
        mid, d_out, d_sum, own_rows(gates_all),
        routes.reshape(rows * local_len, -1), own_rows(attended_all), own_rows(normed_all), w_out,
        w_route, gain_two,
    )
    d_att = d_att.reshape(rows, local_len, FS, quarter).transpose(2, 0, 1, 3)
    d_att = jnp.concatenate(exchange_fsdp(d_att, index), axis=1)
    grad_wout = grad_wout.reshape(DP, FS, block_rows, width).transpose(1, 0, 2, 3)
    grad_wout = reduce_fsdp(grad_wout, index).astype(bf16).reshape(width, fold_out)
    grad_qkv, back_part = attention_backward(
        normed_one, qkv, probs, after(d_att, grad_wout, sum_edown.got), w_qkv, cosine, sine
    )
    sum_last = Reduce(jnp.concatenate([grad_qkv, grad_wout], axis=1), place)
    sum_last.cross()
    sum_last.along()
    sum_edown.along(sum_last.got)

    split_pair = lambda part, half: part.reshape(part.shape[0], -1, 2, tile)[:, :, half].reshape(
        part.shape[0], -1
    )
    part_shared = sum_shared.last()
    part_down = part_shared[:, 2 * ff_part :].reshape(down_rows, width)
    part_pairs = part_pairs.astype(jnp.float32)
    part_gate_up = jnp.stack([split_pair(part_pairs, half) for half in range(2)])
    part_last = sum_last.last()
    part_edown = sum_edown.last()
    part_out = part_last[:, 3 * quarter :].reshape(block_rows, width)
    part_near = jnp.concatenate(
        [
            part_last[:, : 3 * quarter],
            split_pair(part_shared[:, : 2 * ff_part], 0),
            split_pair(part_shared[:, : 2 * ff_part], 1),
        ],
        axis=1,
    )
    part_dense = part_near.astype(bf16)

    out_sum = reduce_fsdp(by_place(out_part), index).reshape(rows * local_len, width)
    valid = (
        (index * local_len + jnp.arange(local_len))[None, :] < lengths[:, None]
    ).astype(jnp.float32)
    output = ((mid + out_sum).reshape(tokens.shape) * valid[..., None]).astype(bf16)
    d_one = reduce_fsdp(by_place(back_part), index).reshape(tokens.shape)
    scaled_one, inverse_one = statistics(tokens.astype(jnp.float32))
    d_in, grad_gain_one = norm_back(d_one, scaled_one, inverse_one, gain_one)
    d_tokens = (d_mid.reshape(tokens.shape) + d_in).astype(bf16)

    columns = (0, device_index * block_rows)
    zeros = jnp.zeros((8 - experts - 2, width), jnp.float32)
    small = jnp.concatenate(
        [grad_router[:experts], grad_gain_one[None], grad_gain_two, zeros], axis=0
    )
    old = jnp.concatenate(
        [MUON_DECAY * mom_router.T, GAIN_DECAY * gain_moms, zeros[:, :block_rows]], axis=0
    )
    small = small + lax.dynamic_update_slice(jnp.zeros_like(small), old, columns)
    small = sum_everywhere(small)
    own_small = lax.dynamic_slice(small, columns, (8, block_rows))
    new_mom_router = own_small[:experts].T
    new_gain_moms = own_small[experts : experts + 2]
    gain_rate = 0.1 / math.sqrt(count * DP)
    new_gains = gains - gain_rate * new_gain_moms
    orth_router = orthogonal_router(
        jnp.concatenate([small[:experts], jnp.zeros((LANES - experts, width), jnp.float32)], axis=0)
    )
    new_router = w_router - ROUTER_RATE * lax.dynamic_slice(
        orth_router, columns, (experts, block_rows)
    ).T

    old_near = exchange_fsdp(by_columns(after(mom_dense, normed_all).astype(bf16)), index)
    old_near = jnp.concatenate(old_near, axis=0).astype(jnp.float32)
    got = exchange_fsdp(part_dense.reshape(FS, block_rows, part_dense.shape[1]), index)
    got = [block.astype(jnp.float32) for block in got]
    cut = lambda start, size: [block[:, start : start + size] for block in got]
    interleave = lambda parts: jnp.stack(
        [part.reshape(block_rows, DP, down_rows) for part in parts], axis=2
    ).reshape(block_rows, ff_shared)
    grad_dense = jnp.concatenate(
        cut(0, quarter)
        + cut(quarter, quarter)
        + cut(2 * quarter, quarter)
        + [part_out]
        + [interleave(cut(3 * quarter, ff_part)), interleave(cut(3 * quarter + ff_part, ff_part))],
        axis=1,
    )
    new_mom_dense = MUON_DECAY * mom_dense + grad_dense
    new_mom_down = MUON_DECAY * mom_down + part_down
    new_e_mom_gate_up = MUON_DECAY * e_mom_gate_up + part_gate_up[None]
    new_e_mom_down = MUON_DECAY * e_mom_down + part_edown[None]

    length = 3 * width
    pad = lambda block: jnp.pad(block, ((0, 0), (0, length - block.shape[1])))
    edges = (0, 3 * width, 4 * width, 4 * width + ff_shared, 4 * width + 2 * ff_shared)
    spots = (0, 3 * quarter, 3 * quarter + ff_part, 3 * quarter + 2 * ff_part)
    near = (MUON_DECAY * old_near + part_near).astype(bf16)
    near_out = (MUON_DECAY * mom_dense[:, 3 * width : 4 * width] + part_out).astype(bf16)
    stripe = lambda block: jnp.pad(block, ((0, 0), (0, 3 * quarter - block.shape[1])))
    stripes = [near[:, spots[i] : spots[i + 1]] for i in range(3)]
    stripes.append(near_out.reshape(folds, fold_out))
    got = exchange_fsdp(jnp.stack([stripe(block) for block in stripes]), index)
    whole_out = jnp.concatenate(
        [block[:, :fold_out].reshape(block_rows, width) for block in got], axis=0
    )
    dense_block = jnp.where(index == FS - 1, pad(whole_out), jnp.concatenate(got, axis=1))
    low_experts = after(new_e_mom_gate_up[0].astype(bf16), orth_router)
    wide = [pad(low_experts[0]), pad(low_experts[1]), dense_block]
    low_down = new_mom_down.astype(bf16)
    column_pairs = lambda step, back: [
        (d * FS + DOWN_COLUMN, d * FS + (DOWN_COLUMN ^ step))[:: 1 if back else -1]
        for d in range(DP)
    ]
    down_block = jnp.concatenate(
        [
            low_down if f == DOWN_COLUMN else lax.ppermute(
                low_down, AXES, column_pairs(DOWN_COLUMN ^ f, False)
            )
            for f in range(FS)
        ],
        axis=0,
    )
    talls = [fold_tall(new_e_mom_down[0].astype(bf16), folds, length), fold_tall(down_block, folds, length)]
    shards = to_owners(jnp.stack(wide + talls), OWNERS, dp_index, index)
    kinds = np.zeros((FS, DP), np.int32)
    for f in range(FS):
        for slot, d in enumerate(OWNERS[f]):
            kinds[f, d] = 2 if slot in TALL_SLOTS else 1
    info = jnp.stack([jnp.asarray(kinds)[index, dp_index], dp_index.astype(jnp.int32)])
    shards = orthogonal_shards(info, shards, width)
    orth_gate, orth_up, orth_block, orth_edown, orth_down_block = from_owners(
        shards, OWNERS, dp_index, index
    )
    orth_edown = unfold_tall(orth_edown, e_down.shape[1])
    orth_down_block = unfold_tall(orth_down_block, e_down.shape[1])
    got = exchange_fsdp(orth_block.reshape(FS, block_rows, length), index)
    striped = lambda block: block.reshape(block_rows, FS, 3 * quarter)
    orth_qkv = striped(got[0]).reshape(block_rows, FS, 3, quarter).transpose(0, 2, 1, 3)
    orth_shared = [
        striped(got[i])[:, :, :ff_part]
        .reshape(block_rows, FS, DP, down_rows)
        .transpose(0, 2, 1, 3)
        .reshape(block_rows, ff_shared)
        for i in (1, 2)
    ]
    orth_dense = [orth_qkv.reshape(block_rows, 3 * width), got[3][:, :width]] + orth_shared
    orth_down_parts = orth_down_block.reshape(FS, down_rows, width)
    orth_down = jnp.where(index == DOWN_COLUMN, orth_down_parts[DOWN_COLUMN], 0)
    for f in range(FS):
        if f != DOWN_COLUMN:
            orth_down = orth_down + lax.ppermute(
                orth_down_parts[f], AXES, column_pairs(DOWN_COLUMN ^ f, True)
            )
    new_dense = jnp.concatenate(
        [
            w_dense[:, edges[i] : edges[i + 1]] - DENSE_RATES[i] * orth_dense[i].astype(jnp.float32)
            for i in range(4)
        ],
        axis=1,
    )
    new_down = w_down - DOWN_RATE * orth_down.astype(jnp.float32)
    new_e_gate_up = jnp.stack(
        [
            e_gate_up[0, i] - EXPERT_RATES[i] * part[:, :ff_width].astype(jnp.float32)
            for i, part in enumerate((orth_gate, orth_up))
        ]
    )[None]
    new_e_down = e_down - EXPERT_RATES[2] * orth_edown.astype(jnp.float32)[None]
    return (
        output,
        d_tokens,
        new_gain_moms,
        new_gains,
        new_mom_dense,
        new_dense,
        new_mom_router,
        new_router,
        new_mom_down,
        new_down,
        new_e_mom_gate_up,
        new_e_gate_up,
        new_e_mom_down,
        new_e_down,
    )


def solution(mesh):
    placed = (
        P("dp", "fsdp", None),
        P("dp", "fsdp", None),
        P("dp"),
        P("dp", "fsdp", None),
        P(None, ("dp", "fsdp")),
        P(None, ("dp", "fsdp")),
        P(("dp", "fsdp"), None),
        P(("dp", "fsdp"), None),
        P(("dp", "fsdp"), None),
        P(("dp", "fsdp"), None),
        P(("dp", "fsdp"), None),
        P(("dp", "fsdp"), None),
        P("fsdp", None, "dp", None),
        P("fsdp", None, "dp", None),
        P("fsdp", "dp", None),
        P("fsdp", "dp", None),
    )
    fits = dict(mesh.shape) == {"dp": DP, "fsdp": FS}
    return jax.shard_map(
        split_plan if fits else general_plan,
        mesh=mesh,
        in_specs=placed,
        out_specs=(
            P("dp", "fsdp", None),
            P("dp", "fsdp", None),
            P(None, ("dp", "fsdp")),
            P(None, ("dp", "fsdp")),
            P(("dp", "fsdp"), None),
            P(("dp", "fsdp"), None),
            P(("dp", "fsdp"), None),
            P(("dp", "fsdp"), None),
            P(("dp", "fsdp"), None),
            P(("dp", "fsdp"), None),
            P("fsdp", None, "dp", None),
            P("fsdp", None, "dp", None),
            P("fsdp", "dp", None),
            P("fsdp", "dp", None),
        ),
        check_vma=False,
    )
```

```python
import functools
import math

import jax
import jax.numpy as jnp
import numpy as np
from jax import lax
from jax.experimental import pallas as pl
from jax.experimental.pallas import tpu as pltpu
from jax.sharding import PartitionSpec as P

HEADS = 12
NS_STEPS = 5


NORM_EPSILON = 1e-06
POLY_FIRST = 3.4445
POLY_SECOND = -4.775
POLY_THIRD = 2.0315
HIGHEST_PRECISION = lax.Precision.HIGHEST
MASK_VALUE = -1e30
DENSE_RATES = (0.8, 5.0, 0.8, 0.8)
ROUTER_RATE = 0.4
DOWN_RATE = 0.5
EXPERT_RATES = (0.8, 0.8, 0.5)
GAIN_DECAY = 0.9
MUON_DECAY = 0.5


def bf_dot(left, right):
    return jnp.dot(left, right, preferred_element_type=jnp.float32)


def first_dot(left, right, precision=None):
    return lax.dot_general(
        left,
        right,
        (((0,), (0,)), ((), ())),
        precision=precision,
        preferred_element_type=jnp.float32,
    )


def last_dot(left, right, precision=None):
    return lax.dot_general(
        left,
        right,
        (((1,), (1,)), ((), ())),
        precision=precision,
        preferred_element_type=jnp.float32,
    )


def statistics(values):
    inverse = lax.rsqrt(jnp.mean(values * values, axis=-1, keepdims=True) + NORM_EPSILON)
    return (values * inverse, inverse)


def norm_back(grad_out, scaled, inverse, gain_row):
    gain_grad = jnp.sum(grad_out * scaled, axis=(0, 1))
    through = grad_out * gain_row
    grad_in = inverse * (through - scaled * jnp.mean(through * scaled, axis=-1, keepdims=True))
    return (grad_in, gain_grad)


def rotation_tables(head_size, places):
    half_size = head_size // 2
    frequency = 10000.0 ** (-2.0 * jnp.arange(half_size, dtype=jnp.float32) / head_size)
    angles = places.astype(jnp.float32)[:, None] * frequency[None, :]
    return (jnp.cos(angles)[:, None, :], jnp.sin(angles)[:, None, :], half_size)


def rotate(values, places):
    cosine, sine, half_size = rotation_tables(values.shape[-1], places)
    first_half = values[..., :half_size]
    second_half = values[..., half_size:]
    return jnp.concatenate(
        [first_half * cosine - second_half * sine, second_half * cosine + first_half * sine],
        axis=-1,
    )


def rotate_back(grads, places):
    cosine, sine, half_size = rotation_tables(grads.shape[-1], places)
    first_half = grads[..., :half_size]
    second_half = grads[..., half_size:]
    return jnp.concatenate(
        [first_half * cosine + second_half * sine, second_half * cosine - first_half * sine],
        axis=-1,
    )


def silu_slope(values):
    logistic = jax.nn.sigmoid(values)
    return logistic * (1.0 + values * (1.0 - logistic))


def orthogonal(matrix):
    if matrix.shape[0] > matrix.shape[1]:
        return orthogonal(matrix.T).T
    current = matrix / (jnp.sqrt(jnp.sum(matrix * matrix)) + 1e-07)

    def sweep(_, current):
        gram = jnp.dot(current, current.T, precision=HIGHEST_PRECISION)
        poly = POLY_SECOND * gram + POLY_THIRD * jnp.dot(gram, gram, precision=HIGHEST_PRECISION)
        return POLY_FIRST * current + jnp.dot(poly, current, precision=HIGHEST_PRECISION)

    return lax.fori_loop(0, NS_STEPS, sweep, current)


def general_plan(
    tokens,
    cotangent,
    lengths,
    routes,
    gains,
    gain_moms,
    w_dense,
    mom_dense,
    w_router,
    mom_router,
    w_down,
    mom_down,
    e_gate_up,
    e_mom_gate_up,
    e_down,
    e_mom_down,
):
    seq_rows, local_len, width = tokens.shape
    head_count = HEADS
    head_size = width // head_count
    seq_parts = lax.axis_size("fsdp")
    seq_index = lax.axis_index("fsdp")
    row_len = local_len * seq_parts
    expert_count = w_router.shape[1]
    top_count = routes.shape[2]
    most_rows = 2 * local_len * top_count // expert_count
    capacity = seq_rows * most_rows
    places = seq_index * local_len + jnp.arange(local_len)
    valid = (places[None, :] < lengths[:, None]).astype(jnp.float32)
    dense_copy, router_copy, down_copy, gain_copy = (
        lax.all_gather(w_dense.astype(jnp.bfloat16), ("dp", "fsdp"), axis=0, tiled=True),
        lax.all_gather(w_router.astype(jnp.bfloat16), ("dp", "fsdp"), axis=0, tiled=True),
        lax.all_gather(w_down.astype(jnp.bfloat16), ("dp", "fsdp"), axis=0, tiled=True),
        lax.all_gather(gains.astype(jnp.bfloat16), ("dp", "fsdp"), axis=1, tiled=True),
    )
    gate_up_copy, edown_copy = (
        lax.all_gather(e_gate_up.astype(jnp.bfloat16), "dp", axis=2, tiled=True),
        lax.all_gather(e_down.astype(jnp.bfloat16), "dp", axis=1, tiled=True),
    )
    gain_one = gain_copy[0].astype(jnp.float32)
    gain_two = gain_copy[1].astype(jnp.float32)
    ff_shared = down_copy.shape[0]
    gate_weight = gate_up_copy[0, 0]
    up_weight = gate_up_copy[0, 1]
    down_weight = edown_copy[0]
    ff_width = gate_weight.shape[1]
    inputs = tokens.astype(jnp.float32)
    scaled_one, inverse_one = statistics(inputs)
    normed_one = (scaled_one * gain_one).astype(jnp.bfloat16).reshape(-1, width)
    projected = bf_dot(normed_one, dense_copy[:, : 3 * width]).reshape(
        seq_rows, local_len, 3, head_count, head_size
    )
    queries = rotate(projected[:, :, 0], places).astype(jnp.bfloat16)
    keys_local = rotate(projected[:, :, 1], places).astype(jnp.bfloat16)
    values_local = projected[:, :, 2].astype(jnp.bfloat16)
    keys_all, values_all = (
        lax.all_gather(keys_local, "fsdp", axis=1, tiled=True),
        lax.all_gather(values_local, "fsdp", axis=1, tiled=True),
    )
    block_len = min(512, row_len)
    block_count = row_len // block_len
    stat_shape = (seq_rows, head_count, local_len)
    head_shape = (seq_rows, local_len, head_count, head_size)

    def masked_scores(query_part, query_places, key_part, key_places):
        raw_scores = (
            jnp.einsum("rqhd,rkhd->rhqk", query_part, key_part, preferred_element_type=jnp.float32)
            * 0.125
        )
        allowed = (key_places[None, None, :] <= query_places[None, :, None]) & (
            key_places[None, None, :] < lengths[:, None, None]
        )
        return jnp.where(allowed[:, None], raw_scores, MASK_VALUE)

    def key_block(index):
        start_at = index * block_len
        key_part = lax.dynamic_slice_in_dim(keys_all, start_at, block_len, 1)
        value_part = lax.dynamic_slice_in_dim(values_all, start_at, block_len, 1)
        return (key_part, value_part, start_at + jnp.arange(block_len))

    def running_max(carry, index):
        top_score, exp_total = carry
        key_part, value_part, key_places = key_block(index)
        scores = masked_scores(queries, places, key_part, key_places)
        new_top = jnp.maximum(top_score, jnp.max(scores, axis=-1))
        exp_total = exp_total * jnp.exp(top_score - new_top) + jnp.sum(
            jnp.exp(scores - new_top[..., None]), axis=-1
        )
        return ((new_top, exp_total), None)

    start_stats = (
        jnp.full(stat_shape, MASK_VALUE, jnp.float32),
        jnp.zeros(stat_shape, jnp.float32),
    )
    (top_score, exp_total), _ = lax.scan(running_max, start_stats, jnp.arange(block_count))
    log_total = top_score + jnp.log(exp_total)

    def weigh_values(total_acc, index):
        key_part, value_part, key_places = key_block(index)
        scores = masked_scores(queries, places, key_part, key_places)
        weights = jnp.exp(scores - log_total[..., None]).astype(jnp.bfloat16)
        return (
            total_acc
            + jnp.einsum(
                "rhqk,rkhd->rqhd", weights, value_part, preferred_element_type=jnp.float32
            ),
            None,
        )

    attended, _ = lax.scan(
        weigh_values, jnp.zeros(head_shape, jnp.float32), jnp.arange(block_count)
    )
    attended_copy = attended.reshape(-1, width).astype(jnp.bfloat16)
    branch = bf_dot(attended_copy, dense_copy[:, 3 * width : 4 * width]).reshape(
        seq_rows, local_len, width
    )
    middle = inputs + branch
    scaled_two, inverse_two = statistics(middle)
    normed_two = (scaled_two * gain_two).astype(jnp.bfloat16).reshape(-1, width)
    logits = bf_dot(normed_two, router_copy)
    route_rows = routes.reshape(-1, top_count)
    chosen = jnp.take_along_axis(logits, route_rows, axis=1)
    gates = jax.nn.softmax(chosen, axis=-1)
    shared_pre = bf_dot(normed_two, dense_copy[:, 4 * width :])
    shared_gate = shared_pre[:, :ff_shared]
    shared_up = shared_pre[:, ff_shared:]
    shared_act = (jax.nn.silu(shared_gate) * shared_up).astype(jnp.bfloat16)
    shared_out = bf_dot(shared_act, down_copy)
    pair_experts = routes.reshape(seq_rows, local_len * top_count)
    onehot = (pair_experts[..., None] == jnp.arange(expert_count, dtype=jnp.int32)).astype(
        jnp.int32
    )
    ranking = jnp.sum((jnp.cumsum(onehot, axis=1) - onehot) * onehot, axis=-1)
    slot_local = (jnp.arange(seq_rows, dtype=jnp.int32)[:, None] * most_rows + ranking).reshape(-1)
    slot_ids = pair_experts.reshape(-1) * capacity + slot_local
    pair_count = seq_rows * local_len * top_count
    table = (
        jnp.full((expert_count * capacity,), -1, jnp.int32)
        .at[slot_ids]
        .set(jnp.arange(pair_count, dtype=jnp.int32))
    )
    present = table >= 0
    picked = jnp.where(present, table, 0)
    outgoing = jnp.where(
        present[:, None], normed_two[picked // top_count], jnp.zeros((), jnp.bfloat16)
    ).reshape(expert_count, capacity, width)
    arrived = lax.all_to_all(outgoing, "fsdp", split_axis=0, concat_axis=0, tiled=True)
    sources, item_count, _ = arrived.shape
    arrived_rows = arrived.reshape(sources * item_count, width)
    pre_act = jnp.concatenate(
        [bf_dot(arrived_rows, gate_weight), bf_dot(arrived_rows, up_weight)], axis=-1
    )
    activated = (jax.nn.silu(pre_act[:, :ff_width]) * pre_act[:, ff_width:]).astype(jnp.bfloat16)
    result = bf_dot(activated, down_weight).astype(jnp.bfloat16).reshape(sources, item_count, width)
    returned_rows = lax.all_to_all(result, "fsdp", split_axis=0, concat_axis=0, tiled=True)
    pre_all = pre_act.reshape(sources, item_count, 2 * ff_width)
    pair_out = (
        returned_rows.reshape(expert_count * capacity, width)[slot_ids]
        .reshape(-1, top_count, width)
        .astype(jnp.float32)
    )
    mixed = jnp.sum(gates[..., None] * pair_out, axis=1)
    total = middle + (shared_out + mixed).reshape(seq_rows, local_len, width)
    output = (total * valid[..., None]).astype(jnp.bfloat16)
    d_out = cotangent.astype(jnp.float32) * valid[..., None]
    d_flat = d_out.reshape(-1, width)
    d_flat_copy = d_flat.astype(jnp.bfloat16)
    grad_down = first_dot(shared_act, d_flat_copy)
    d_sact = last_dot(d_flat_copy, down_copy)
    d_shared = jnp.concatenate(
        [d_sact * shared_up * silu_slope(shared_gate), d_sact * jax.nn.silu(shared_gate)], axis=-1
    ).astype(jnp.bfloat16)
    grad_shared = first_dot(normed_two, d_shared)
    d_normed = last_dot(d_shared, dense_copy[:, 4 * width :])
    d_gates = jnp.sum(d_flat[:, None, :] * pair_out, axis=-1)
    d_chosen = gates * (d_gates - jnp.sum(gates * d_gates, axis=-1, keepdims=True))
    route_table = (route_rows[..., None] == jnp.arange(expert_count, dtype=jnp.int32)).astype(
        jnp.float32
    )
    d_logits = jnp.sum(d_chosen[..., None] * route_table, axis=1).astype(jnp.bfloat16)
    grad_router = first_dot(normed_two, d_logits)
    d_normed = d_normed + last_dot(d_logits, router_copy)
    d_pairs = (gates[..., None] * d_flat[:, None, :]).reshape(-1, width).astype(jnp.bfloat16)
    d_outgoing = jnp.where(present[:, None], d_pairs[picked], jnp.zeros((), jnp.bfloat16)).reshape(
        expert_count, capacity, width
    )
    d_arrived = lax.all_to_all(d_outgoing, "fsdp", split_axis=0, concat_axis=0, tiled=True)
    d_result = d_arrived.reshape(-1, width)
    pre_rows = pre_all.reshape(-1, 2 * ff_width)
    expert_gate = pre_rows[:, :ff_width]
    expert_up = pre_rows[:, ff_width:]
    activated = (jax.nn.silu(expert_gate) * expert_up).astype(jnp.bfloat16)
    grad_edown = first_dot(activated, d_result)
    d_activated = last_dot(d_result, down_weight)
    d_pre = jnp.concatenate(
        [d_activated * expert_up * silu_slope(expert_gate), d_activated * jax.nn.silu(expert_gate)],
        axis=-1,
    ).astype(jnp.bfloat16)
    arrived_rows = arrived.reshape(-1, width)
    grad_gate = first_dot(arrived_rows, d_pre[:, :ff_width])
    grad_up = first_dot(arrived_rows, d_pre[:, ff_width:])
    d_inputs = (
        (last_dot(d_pre[:, :ff_width], gate_weight) + last_dot(d_pre[:, ff_width:], up_weight))
        .astype(jnp.bfloat16)
        .reshape(d_arrived.shape)
    )
    d_returned = lax.all_to_all(d_inputs, "fsdp", split_axis=0, concat_axis=0, tiled=True).reshape(
        expert_count * capacity, width
    )
    d_normed = d_normed + jnp.sum(
        d_returned[slot_ids].astype(jnp.float32).reshape(-1, top_count, width), axis=1
    )
    d_mid_norm, grad_gain_two = norm_back(
        d_normed.reshape(seq_rows, local_len, width), scaled_two, inverse_two, gain_two
    )
    d_middle = d_out + d_mid_norm
    d_branch = d_middle.reshape(-1, width).astype(jnp.bfloat16)
    grad_wout = first_dot(attended_copy, d_branch)
    d_attended = (
        last_dot(d_branch, dense_copy[:, 3 * width : 4 * width])
        .reshape(head_shape)
        .astype(jnp.bfloat16)
    )

    def delta_pass(delta_acc, index):
        key_part, value_part, key_places = key_block(index)
        weights = jnp.exp(
            masked_scores(queries, places, key_part, key_places) - log_total[..., None]
        )
        slopes = jnp.einsum(
            "rqhd,rkhd->rhqk", d_attended, value_part, preferred_element_type=jnp.float32
        )
        return (delta_acc + jnp.sum(weights * slopes, axis=-1), None)

    delta, _ = lax.scan(delta_pass, jnp.zeros(stat_shape, jnp.float32), jnp.arange(block_count))

    def make_pass():

        def query_pass(query_acc, index):
            key_part, value_part, key_places = key_block(index)
            weights = jnp.exp(
                masked_scores(queries, places, key_part, key_places) - log_total[..., None]
            )
            slopes = jnp.einsum(
                "rqhd,rkhd->rhqk", d_attended, value_part, preferred_element_type=jnp.float32
            )
            score_grad = (weights * (slopes - delta[..., None])).astype(jnp.bfloat16)
            query_acc = query_acc + 0.125 * jnp.einsum(
                "rhqk,rkhd->rqhd", score_grad, key_part, preferred_element_type=jnp.float32
            )
            key_grad = 0.125 * jnp.einsum(
                "rhqk,rqhd->rkhd", score_grad, queries, preferred_element_type=jnp.float32
            )
            value_grad = jnp.einsum(
                "rhqk,rqhd->rkhd",
                weights.astype(jnp.bfloat16),
                d_attended,
                preferred_element_type=jnp.float32,
            )
            return (query_acc, (key_grad, value_grad))

        return query_pass

    d_query, (key_parts, value_parts) = lax.scan(
        make_pass(), jnp.zeros(head_shape, jnp.float32), jnp.arange(block_count)
    )
    key_whole = jnp.moveaxis(key_parts, 0, 1).reshape(seq_rows, row_len, width)
    value_whole = jnp.moveaxis(value_parts, 0, 1).reshape(seq_rows, row_len, width)
    key_value = lax.psum_scatter(
        jnp.concatenate([key_whole, value_whole], axis=-1), "fsdp", scatter_dimension=1, tiled=True
    )
    d_key = key_value[..., :width].reshape(head_shape)
    d_value = key_value[..., width:].reshape(head_shape)
    d_qkv = (
        jnp.stack([rotate_back(d_query, places), rotate_back(d_key, places), d_value], axis=2)
        .reshape(-1, 3 * width)
        .astype(jnp.bfloat16)
    )
    grad_qkv = first_dot(normed_one, d_qkv)
    d_one = last_dot(d_qkv, dense_copy[:, : 3 * width]).reshape(seq_rows, local_len, width)
    d_in_norm, grad_gain_one = norm_back(d_one, scaled_one, inverse_one, gain_one)
    d_tokens = (d_middle + d_in_norm).astype(jnp.bfloat16)
    grad_dense = jnp.concatenate([grad_qkv, grad_wout, grad_shared], axis=1)
    grad_gains = jnp.stack([grad_gain_one, grad_gain_two])
    part_dense, part_router, part_down, part_gains = (
        lax.psum_scatter(grad_dense, ("dp", "fsdp"), scatter_dimension=0, tiled=True),
        lax.psum_scatter(grad_router, ("dp", "fsdp"), scatter_dimension=0, tiled=True),
        lax.psum_scatter(grad_down, ("dp", "fsdp"), scatter_dimension=0, tiled=True),
        lax.psum_scatter(grad_gains, ("dp", "fsdp"), scatter_dimension=1, tiled=True),
    )
    total_slots = seq_rows * lax.axis_size("dp") * row_len
    gain_rate = 0.1 / math.sqrt(total_slots)
    new_gain_moms = GAIN_DECAY * gain_moms + part_gains
    new_gains = gains - gain_rate * new_gain_moms
    new_mom_dense = MUON_DECAY * mom_dense + part_dense
    new_mom_router = MUON_DECAY * mom_router + part_router
    new_mom_down = MUON_DECAY * mom_down + part_down
    device_index = lax.axis_index(("dp", "fsdp"))
    device_count = lax.axis_size(("dp", "fsdp"))
    owners = [number * device_count // 6 for number in range(6)]

    def owned(number, matrix):
        return lax.cond(device_index == owners[number], orthogonal, jnp.zeros_like, matrix)

    edges = (0, 3 * width, 4 * width, 4 * width + ff_shared, 4 * width + 2 * ff_shared)
    whole_dense, whole_router, whole_down = (
        lax.all_gather(new_mom_dense, ("dp", "fsdp"), axis=0, tiled=True),
        lax.all_gather(new_mom_router, ("dp", "fsdp"), axis=0, tiled=True),
        lax.all_gather(new_mom_down, ("dp", "fsdp"), axis=0, tiled=True),
    )
    orth_dense = jnp.concatenate(
        [owned(number, whole_dense[:, edges[number] : edges[number + 1]]) for number in range(4)],
        axis=1,
    )
    orth_router = owned(4, whole_router)
    orth_down = owned(5, whole_down)
    share_dense, share_router, share_down = (
        lax.psum_scatter(orth_dense, ("dp", "fsdp"), scatter_dimension=0, tiled=True),
        lax.psum_scatter(orth_router, ("dp", "fsdp"), scatter_dimension=0, tiled=True),
        lax.psum_scatter(orth_down, ("dp", "fsdp"), scatter_dimension=0, tiled=True),
    )
    column_rates = jnp.concatenate(
        [
            jnp.full((edges[number + 1] - edges[number],), DENSE_RATES[number], jnp.float32)
            for number in range(4)
        ]
    )
    new_dense = w_dense - column_rates[None, :] * share_dense
    new_router = w_router - ROUTER_RATE * share_router
    new_down = w_down - DOWN_RATE * share_down
    dp_index = lax.axis_index("dp")
    gate_rows = e_gate_up.shape[2]
    down_rows = e_down.shape[1]
    gate_term = jnp.stack([grad_gate, grad_up])[None] + lax.dynamic_update_slice(
        jnp.zeros((1, 2, width, ff_width), jnp.float32),
        MUON_DECAY * e_mom_gate_up,
        (0, 0, dp_index * gate_rows, 0),
    )
    down_term = grad_edown[None] + lax.dynamic_update_slice(
        jnp.zeros((1, ff_width, width), jnp.float32),
        MUON_DECAY * e_mom_down,
        (0, dp_index * down_rows, 0),
    )
    whole_gate_up, whole_edown = lax.psum((gate_term, down_term), "dp")
    orth_gate_up = jnp.stack([orthogonal(whole_gate_up[0, 0]), orthogonal(whole_gate_up[0, 1])])[
        None
    ]
    orth_edown = orthogonal(whole_edown[0])[None]
    new_e_mom_gate_up = lax.dynamic_slice_in_dim(whole_gate_up, dp_index * gate_rows, gate_rows, 2)
    gate_rates = jnp.array(EXPERT_RATES[:2], jnp.float32)[None, :, None, None]
    new_e_gate_up = e_gate_up - gate_rates * lax.dynamic_slice_in_dim(
        orth_gate_up, dp_index * gate_rows, gate_rows, 2
    )
    new_e_mom_down = lax.dynamic_slice_in_dim(whole_edown, dp_index * down_rows, down_rows, 1)
    new_e_down = e_down - EXPERT_RATES[2] * lax.dynamic_slice_in_dim(
        orth_edown, dp_index * down_rows, down_rows, 1
    )
    return (
        output,
        d_tokens,
        new_gain_moms,
        new_gains,
        new_mom_dense,
        new_dense,
        new_mom_router,
        new_router,
        new_mom_down,
        new_down,
        new_e_mom_gate_up,
        new_e_gate_up,
        new_e_mom_down,
        new_e_down,
    )


DP = 8
FS = 4
AXES = ("dp", "fsdp")
LANES = 128
VMEM_BYTES = 60 * 2**20
LINE = 4
OWNERS = ((0, 3, 4, 7), (1, 2, 5, 6), (0, 3, 4, 7), (1, 2, 5, 6, 4))
TALL_SLOTS = (3, 4)
DOWN_COLUMN = 3


def tn_dot(left, right):
    return lax.dot_general(
        left, right, (((0,), (0,)), ((), ())), preferred_element_type=jnp.float32
    )


def nt_dot(left, right):
    return lax.dot_general(
        left, right, (((1,), (1,)), ((), ())), preferred_element_type=jnp.float32
    )


def kernel_call(body, out_shape, flops, bytes_accessed, **options):
    return pl.pallas_call(
        body,
        out_shape=out_shape,
        compiler_params=pltpu.CompilerParams(vmem_limit_bytes=VMEM_BYTES),
        cost_estimate=pl.CostEstimate(
            flops=int(flops), bytes_accessed=int(bytes_accessed), transcendentals=0
        ),
        **options,
    )


def shape_of(shape, dtype=jnp.bfloat16):
    return jax.ShapeDtypeStruct(shape, dtype)


def whole_block(shape):
    return pl.BlockSpec(shape, lambda *_: (0,) * len(shape))


def after(value, *events):
    return lax.optimization_barrier((value,) + events)[0]


def fsdp_hop(value, step):
    pairs = [(d * FS + f, d * FS + (f ^ step)) for d in range(DP) for f in range(FS)]
    return lax.ppermute(value, AXES, pairs)


def by_source(own, near, far, cross, index):
    low_x, even = index < 2, index % 2 == 0
    own_low, own_high = jnp.where(low_x, own, far), jnp.where(low_x, far, own)
    near_low, near_high = jnp.where(low_x, near, cross), jnp.where(low_x, cross, near)
    return [
        jnp.where(even, own_low, near_low),
        jnp.where(even, near_low, own_low),
        jnp.where(even, own_high, near_high),
        jnp.where(even, near_high, own_high),
    ]


def gather_fsdp(block, index):
    far = fsdp_hop(block, 2)
    near = fsdp_hop(block, 1)
    cross = fsdp_hop(far, 1)
    return by_source(block, near, far, cross, index)


def exchange_fsdp(blocks, index):
    pick = lambda step: lax.dynamic_index_in_dim(blocks, index ^ step, 0, keepdims=False)
    got = [pick(0)] + [fsdp_hop(pick(step), step) for step in (1, 2, 3)]
    return by_source(*got, index)


def reduce_fsdp(blocks, index):
    core, place = index % 2, index // 2
    pairs = blocks.reshape((2, 2) + blocks.shape[1:])
    send = lax.dynamic_index_in_dim(pairs, 1 - core, 1, keepdims=False)
    keep = lax.dynamic_index_in_dim(pairs, core, 1, keepdims=False)
    both = keep.astype(jnp.float32) + fsdp_hop(send, 1).astype(jnp.float32)
    away = lax.dynamic_index_in_dim(both, 1 - place, 0, keepdims=False).astype(blocks.dtype)
    here = lax.dynamic_index_in_dim(both, place, 0, keepdims=False)
    return here + fsdp_hop(away, 2).astype(jnp.float32)


def sum_everywhere(value):
    for d_step, f_step in ((0, 1), (0, 2), (1, 0), (2, 0), (4, 0)):
        pairs = [
            (d * FS + f, (d ^ d_step) * FS + (f ^ f_step)) for d in range(DP) for f in range(FS)
        ]
        value = value + lax.ppermute(value, AXES, pairs)
    return value


def swap_halves(values, half_size):
    width = values.shape[1]
    lane = lax.broadcasted_iota(jnp.int32, values.shape, 1)
    return jnp.where(
        lane % (2 * half_size) < half_size,
        -pltpu.roll(values, width - half_size, 1),
        pltpu.roll(values, half_size, 1),
    )


def attention_body(
    lengths_ref, x_ref, gain_ref, w_ref, cos_ref, sin_ref, normed_ref, qkv_ref, prob_ref, att_ref
):
    head_count, row_len = prob_ref.shape[1], prob_ref.shape[2]
    wide = w_ref.shape[1] // 3
    head_size = wide // head_count
    x = x_ref[0].astype(jnp.float32)
    inverse = lax.rsqrt(jnp.mean(x * x, axis=-1, keepdims=True) + NORM_EPSILON)
    normed = (x * inverse * gain_ref[...]).astype(jnp.bfloat16)
    normed_ref[...] = normed.T
    projected = jnp.dot(normed, w_ref[...], preferred_element_type=jnp.float32)
    both = projected[:, : 2 * wide]
    both = both * cos_ref[...] + swap_halves(both, head_size // 2) * sin_ref[...]
    both = both.astype(jnp.bfloat16)
    values = projected[:, 2 * wide :].astype(jnp.bfloat16)
    qkv_ref[0, :, : 2 * wide] = both
    qkv_ref[0, :, 2 * wide :] = values
    length = lengths_ref[pl.program_id(0)]
    row = lax.broadcasted_iota(jnp.int32, (row_len, row_len), 0)
    column = lax.broadcasted_iota(jnp.int32, (row_len, row_len), 1)
    allowed = (column <= row) & (column < length)
    parts = []
    for head in range(head_count):
        span = slice(head * head_size, (head + 1) * head_size)
        scores = nt_dot(both[:, span], both[:, wide:][:, span]) * 0.125
        scores = jnp.where(allowed, scores, MASK_VALUE)
        weights = jnp.exp(scores - jnp.max(scores, axis=-1, keepdims=True))
        share = 1.0 / jnp.sum(weights, axis=-1, keepdims=True)
        probs = (weights * share).astype(jnp.bfloat16)
        prob_ref[0, head] = probs
        parts.append(jnp.dot(probs, values[:, span], preferred_element_type=jnp.float32))
    att_ref[0] = jnp.concatenate(parts, axis=1).astype(jnp.bfloat16)


def attention_forward(x, gain, weight, cosine, sine, lengths):
    rows, row_len, width = x.shape
    columns = weight.shape[1]
    heads = columns // 3 // (width // HEADS)
    return kernel_call(
        attention_body,
        (
            shape_of((width, rows * row_len)),
            shape_of((rows, row_len, columns)),
            shape_of((rows, heads, row_len, row_len)),
            shape_of((rows, row_len, columns // 3)),
        ),
        6e9,
        12e6,
        grid=(rows,),
        in_specs=[
            pl.BlockSpec(memory_space=pltpu.SMEM),
            pl.BlockSpec((1, row_len, width), lambda r: (r, 0, 0)),
            whole_block(gain.shape),
            whole_block(weight.shape),
            whole_block(cosine.shape),
            whole_block(sine.shape),
        ],
        out_specs=(
            pl.BlockSpec((width, row_len), lambda r: (0, r)),
            pl.BlockSpec((1, row_len, columns), lambda r: (r, 0, 0)),
            pl.BlockSpec((1, heads, row_len, row_len), lambda r: (r, 0, 0, 0)),
            pl.BlockSpec((1, row_len, columns // 3), lambda r: (r, 0, 0)),
        ),
        name="attention_forward",
    )(lengths, x, gain, weight, cosine, sine)


def attention_back_body(
    normed_ref, qkv_ref, prob_ref, d_att_ref, w_ref, cos_ref, sin_ref, grad_ref, back_ref, total
):
    head_count = prob_ref.shape[1]
    wide = w_ref.shape[1] // 3
    head_size = wide // head_count
    qkv = qkv_ref[0]
    d_att = d_att_ref[0]
    grads = ([], [], [])
    for head in range(head_count):
        span = slice(head * head_size, (head + 1) * head_size)
        query, key, value = (qkv[:, i * wide : (i + 1) * wide][:, span] for i in range(3))
        probs = prob_ref[0, head]
        weights = probs.astype(jnp.float32)
        slopes = nt_dot(d_att[:, span], value)
        delta = jnp.sum(weights * slopes, axis=-1, keepdims=True)
        d_scores = (weights * (slopes - delta)).astype(jnp.bfloat16)
        grads[0].append(0.125 * jnp.dot(d_scores, key, preferred_element_type=jnp.float32))
        grads[1].append(0.125 * tn_dot(d_scores, query))
        grads[2].append(tn_dot(probs, d_att[:, span]))
    both = jnp.concatenate(grads[0] + grads[1], axis=1)
    both = both * cos_ref[...] - swap_halves(both, head_size // 2) * sin_ref[...]
    d_qkv = jnp.concatenate([both] + grads[2], axis=1).astype(jnp.bfloat16)
    grad = jnp.dot(normed_ref[...], d_qkv, preferred_element_type=jnp.float32)

    @pl.when(pl.program_id(0) == 0)
    def _():
        total[...] = grad

    @pl.when(pl.program_id(0) > 0)
    def _():
        total[...] += grad

    grad_ref[...] = total[...].astype(jnp.bfloat16)
    back_ref[0] = nt_dot(d_qkv, w_ref[...]).astype(jnp.bfloat16)


def attention_backward(normed, qkv, probs, d_att, weight, cosine, sine):
    rows, row_len, columns = qkv.shape
    width, heads = weight.shape[0], probs.shape[1]
    return kernel_call(
        attention_back_body,
        (shape_of((width, columns)), shape_of((rows, row_len, width))),
        8e9,
        12e6,
        grid=(rows,),
        in_specs=[
            pl.BlockSpec((width, row_len), lambda r: (0, r)),
            pl.BlockSpec((1, row_len, columns), lambda r: (r, 0, 0)),
            pl.BlockSpec((1, heads, row_len, row_len), lambda r: (r, 0, 0, 0)),
            pl.BlockSpec((1, row_len, columns // 3), lambda r: (r, 0, 0)),
            whole_block(weight.shape),
            whole_block(cosine.shape),
            whole_block(sine.shape),
        ],
        out_specs=(
            whole_block((width, columns)),
            pl.BlockSpec((1, row_len, width), lambda r: (r, 0, 0)),
        ),
        scratch_shapes=[pltpu.VMEM((width, columns), jnp.float32)],
        name="attention_backward",
    )(normed, qkv, probs, d_att, weight, cosine, sine)


def middle_body(
    att_ref, x_ref, routes_ref, wout_ref, router_ref, gain_ref, mid_ref, normed_ref, turned_ref, gates_ref
):
    branch = jnp.dot(att_ref[...], wout_ref[...], preferred_element_type=jnp.float32)
    mid = x_ref[...].astype(jnp.float32) + branch
    inverse = lax.rsqrt(jnp.mean(mid * mid, axis=-1, keepdims=True) + NORM_EPSILON)
    normed = (mid * inverse * gain_ref[...]).astype(jnp.bfloat16)
    logits = jnp.dot(normed, router_ref[...], preferred_element_type=jnp.float32)
    lane = lax.broadcasted_iota(jnp.int32, logits.shape, 1)
    first, second = lane == routes_ref[:, 0:1], lane == routes_ref[:, 1:2]
    one = jnp.sum(jnp.where(first, logits, 0.0), axis=-1, keepdims=True)
    two = jnp.sum(jnp.where(second, logits, 0.0), axis=-1, keepdims=True)
    top = jnp.maximum(one, two)
    one, two = jnp.exp(one - top), jnp.exp(two - top)
    share = 1.0 / (one + two)
    mid_ref[...] = mid
    normed_ref[...] = normed
    turned_ref[...] = normed.T
    gates_ref[...] = jnp.where(first, one * share, 0.0) + jnp.where(second, two * share, 0.0)


def middle_forward(attended, x, routes, wout, router, gain):
    count, width = x.shape
    tile = min(256, count)
    rows = lambda i: (i, 0)
    return kernel_call(
        middle_body,
        (
            shape_of((count, width), jnp.float32),
            shape_of((count, width)),
            shape_of((width, count)),
            shape_of((count, LANES), jnp.float32),
        ),
        2 * count * width * width,
        12e6,
        grid=(count // tile,),
        in_specs=[
            pl.BlockSpec((tile, width), rows),
            pl.BlockSpec((tile, width), rows),
            pl.BlockSpec((tile, routes.shape[1]), rows),
            whole_block(wout.shape),
            whole_block(router.shape),
            whole_block(gain.shape),
        ],
        out_specs=(
            pl.BlockSpec((tile, width), rows),
            pl.BlockSpec((tile, width), rows),
            pl.BlockSpec((width, tile), lambda i: (0, i)),
            pl.BlockSpec((tile, LANES), rows),
        ),
        name="middle_forward",
    )(attended, x, routes, wout, router, gain)


def middle_back_body(
    mid_ref, d_out_ref, d_sum_ref, gates_ref, routes_ref, att_ref, normed_ref, wout_ref, router_ref,
    gain_ref, d_mid_ref, d_att_ref, grad_wout_ref, grad_router_ref, grad_gain_ref,
):
    width = mid_ref.shape[1]
    gates = gates_ref[...]
    lane = lax.broadcasted_iota(jnp.int32, gates.shape, 1)
    half = LANES // 2
    first, second = routes_ref[:, 0:1], routes_ref[:, 1:2]
    slopes = d_sum_ref[:, width:]

    def pick(table, place):
        return jnp.sum(jnp.where(lane == place, table, 0.0), axis=-1, keepdims=True)

    gate_one, gate_two = pick(gates, first), pick(gates, second)
    slope_one = pick(slopes, first) + pick(slopes, first + half)
    slope_two = pick(slopes, second) + pick(slopes, second + half)
    common = gate_one * slope_one + gate_two * slope_two
    d_logits = jnp.where(lane == first, gate_one * (slope_one - common), 0.0)
    d_logits = d_logits + jnp.where(lane == second, gate_two * (slope_two - common), 0.0)
    d_logits = d_logits.astype(jnp.bfloat16)
    grad_router_ref[...] = tn_dot(d_logits, normed_ref[...])
    d_normed = d_sum_ref[:, :width] + nt_dot(d_logits, router_ref[...])
    mid = mid_ref[...]
    inverse = lax.rsqrt(jnp.mean(mid * mid, axis=-1, keepdims=True) + NORM_EPSILON)
    scaled = mid * inverse
    grad_gain_ref[...] = jnp.sum(d_normed * scaled, axis=0, keepdims=True)
    through = d_normed * gain_ref[...]
    d_norm = inverse * (through - scaled * jnp.mean(through * scaled, axis=-1, keepdims=True))
    d_mid = d_out_ref[...].astype(jnp.float32) + d_norm
    d_mid_ref[...] = d_mid
    d_branch = d_mid.astype(jnp.bfloat16)
    grad_wout_ref[...] = tn_dot(att_ref[...], d_branch).astype(jnp.bfloat16)
    d_att_ref[...] = nt_dot(d_branch, wout_ref[...]).astype(jnp.bfloat16)


def middle_backward(*operands):
    count, width = operands[0].shape
    return kernel_call(
        middle_back_body,
        (
            shape_of((count, width), jnp.float32),
            shape_of((count, width)),
            shape_of((width, width)),
            shape_of((LANES, width), jnp.float32),
            shape_of((1, width), jnp.float32),
        ),
        4 * count * width * width,
        8e6,
        name="middle_backward",
    )(*operands)


def branch_step(normed_ref, turned_ref, d_out_ref, gate_column, weights, grads):
    both_weight, down_weight = weights
    tile = down_weight.shape[0]
    normed, d_out = normed_ref[...], d_out_ref[...]
    both = jnp.dot(normed, both_weight, preferred_element_type=jnp.float32)
    gate, up = both[:, :tile], both[:, tile:]
    slope = nt_dot(d_out, down_weight)
    logistic = 1.0 / (1.0 + jnp.exp(-gate))
    silu = gate * logistic
    act = silu * up
    d_gate = None
    if gate_column is not None:
        d_gate = jnp.sum(act * slope, axis=-1, keepdims=True)
        act = act * gate_column
        slope = slope * gate_column
    act = act.astype(jnp.bfloat16)
    d_both = jnp.concatenate(
        [
            (slope * up * (logistic * (1.0 + gate * (1.0 - logistic)))).astype(jnp.bfloat16),
            (slope * silu).astype(jnp.bfloat16),
        ],
        axis=1,
    )
    grads[0][...] = jnp.dot(
        turned_ref[...], d_both, preferred_element_type=jnp.float32
    ).astype(jnp.bfloat16)
    grads[1][...] = tn_dot(act, d_out).astype(jnp.bfloat16)
    out = jnp.dot(act, down_weight, preferred_element_type=jnp.float32)
    return out, nt_dot(d_both, both_weight), d_gate


def branch_body(
    expert_ref, normed_ref, turned_ref, d_out_ref, *refs, routed, chained, last
):
    refs = list(refs)
    gates_ref = refs.pop(0) if routed else None
    first = [refs.pop(0) for _ in range(3 if routed else 2)] if chained else None
    gate_ref, up_ref, down_ref, out_ref, back_ref = refs[:5]
    slope_ref = refs[5] if routed and not last else None
    grad_pair_ref, grad_down_ref = refs[6:8] if slope_ref is not None else refs[5:7]
    totals = refs[-3:]
    step = pl.program_id(0)
    out, back, d_gate = branch_step(
        normed_ref,
        turned_ref,
        d_out_ref,
        gates_ref[...] if routed else None,
        (jnp.concatenate([gate_ref[...], up_ref[...]], axis=1), down_ref[...]),
        (grad_pair_ref, grad_down_ref),
    )
    parts = [out, back] + ([d_gate] if routed else [])

    @pl.when(step == 0)
    def _():
        for i, part in enumerate(parts):
            kept = chained and i < len(first)
            totals[i][...] = first[i][...] + part if kept else part

    @pl.when(step > 0)
    def _():
        for i, part in enumerate(parts):
            totals[i][...] += part

    @pl.when(step == pl.num_programs(0) - 1)
    def _():
        if not last:
            out_ref[...] = totals[0][...]
            back_ref[...] = totals[1][...]
            if routed:
                slope_ref[...] = totals[2][...]
            return
        width = out_ref.shape[1]
        out_ref[...] = totals[0][...].astype(jnp.bfloat16)
        back_ref[:, :width] = totals[1][...].astype(jnp.bfloat16)
        slopes = totals[2][...]
        high = slopes.astype(jnp.bfloat16).astype(jnp.float32)
        lane = lax.broadcasted_iota(jnp.int32, (slopes.shape[0], LANES), 1)
        table = jnp.where(lane == expert_ref[0], high, 0.0)
        table = jnp.where(lane == expert_ref[0] + LANES // 2, slopes - high, table)
        back_ref[:, width:] = table.astype(jnp.bfloat16)


def branch(expert, normed, turned, d_out, gates, first, weights, blocks, last, name):
    (gate, gate_spec), (up, up_spec), down = weights
    count, width = normed.shape
    start, end, tile = blocks
    routed, chained = gates is not None, first is not None
    hidden = (end - start) * tile
    once = lambda shape: pl.BlockSpec(
        shape, lambda *_: (0,) * len(shape), pipeline_mode=pl.Buffered(1)
    )
    operands = [expert, normed, turned, d_out]
    if routed:
        operands.append(gates)
    if chained:
        operands += first
    full = [once(array.shape) for array in operands[1:]]
    outs = [shape_of((count, width), jnp.float32), shape_of((count, width), jnp.float32)]
    if routed and not last:
        outs.append(shape_of((count, 1), jnp.float32))
    if last:
        outs = [shape_of((count, width)), shape_of((count, width + LANES))]
    return kernel_call(
        functools.partial(branch_body, routed=routed, chained=chained, last=last),
        outs + [shape_of((width, 2 * hidden)), shape_of((hidden, width))],
        18 * count * width * hidden,
        12 * width * hidden + 16 * count * width,
        grid=(end - start,),
        in_specs=[pl.BlockSpec(memory_space=pltpu.SMEM)]
        + full
        + [gate_spec, up_spec, pl.BlockSpec((tile, width), lambda j: (start + j, 0))],
        out_specs=[once(out.shape) for out in outs]
        + [
            pl.BlockSpec((width, 2 * tile), lambda j: (0, j)),
            pl.BlockSpec((tile, width), lambda j: (j, 0)),
        ],
        scratch_shapes=[
            pltpu.VMEM((count, width), jnp.float32),
            pltpu.VMEM((count, width), jnp.float32),
            pltpu.VMEM((count, 1), jnp.float32),
        ],
        name=name,
    )(*operands, gate, up, down)


def orthogonal_body(info_ref, *refs):
    shards, results = refs[:DP], refs[DP : 2 * DP]
    current, gram, poly = refs[2 * DP :]
    size, length = current.shape
    kind, place = info_ref[0], info_ref[1]
    rows = shards[0].shape[0]
    columns = 2 * LANES
    tile = 256
    tiles = size // tile
    chunks = length // tile

    def spot(k, extent):
        return pl.multiple_of(lax.rem(place + k, DP) * extent, extent)

    def folds(k):
        for j in range(size // rows):
            yield (
                (slice(j * rows, (j + 1) * rows), pl.ds(spot(k, columns), columns)),
                (slice(None), slice(j * columns, (j + 1) * columns)),
            )

    @pl.when(kind == 1)
    def _():
        for k in range(DP):
            current[pl.ds(spot(k, rows), rows), :] = shards[k][...]

    @pl.when(kind == 2)
    def _():
        current[:, DP * columns :] = jnp.zeros((size, length - DP * columns), jnp.bfloat16)
        for k in range(DP):
            for there, here in folds(k):
                current[there] = shards[k][here]

    @pl.when(kind > 0)
    def _():
        def square(c, total):
            part = current[:, pl.ds(pl.multiple_of(c * tile, tile), tile)].astype(jnp.float32)
            return total + jnp.sum(part * part, axis=0, keepdims=True)

        squares = lax.fori_loop(0, chunks, square, jnp.zeros((1, tile), jnp.float32))
        scale = 1.0 / (jnp.sqrt(jnp.sum(squares, axis=1, keepdims=True)) + 1e-07)

        def scale_chunk(c, carry):
            span = pl.ds(pl.multiple_of(c * tile, tile), tile)
            part = current[:, span].astype(jnp.float32)
            current[:, span] = (part * scale).astype(jnp.bfloat16)
            return carry

        lax.fori_loop(0, chunks, scale_chunk, 0)

        def sweep(_, carry):
            for i in range(tiles):
                block = nt_dot(current[i * tile : (i + 1) * tile, :], current[i * tile :, :])
                gram[i * tile : (i + 1) * tile, i * tile :] = block.astype(jnp.bfloat16)
                poly[i * tile : (i + 1) * tile, i * tile :] = POLY_SECOND * block
            for i in range(tiles):
                for j in range(i):
                    gram[i * tile : (i + 1) * tile, j * tile : (j + 1) * tile] = gram[
                        j * tile : (j + 1) * tile, i * tile : (i + 1) * tile
                    ].T
            for i in range(tiles):
                block = jnp.dot(
                    gram[i * tile : (i + 1) * tile, :],
                    gram[:, i * tile :],
                    preferred_element_type=jnp.float32,
                )
                poly[i * tile : (i + 1) * tile, i * tile :] += POLY_THIRD * block
            for i in range(tiles):
                gram[i * tile : (i + 1) * tile, i * tile :] = poly[
                    i * tile : (i + 1) * tile, i * tile :
                ].astype(jnp.bfloat16)
            for i in range(tiles):
                for j in range(i):
                    gram[i * tile : (i + 1) * tile, j * tile : (j + 1) * tile] = gram[
                        j * tile : (j + 1) * tile, i * tile : (i + 1) * tile
                    ].T

            def update(c, carry):
                span = pl.ds(pl.multiple_of(c * tile, tile), tile)
                part = current[:, span]
                fresh = POLY_FIRST * part.astype(jnp.float32) + jnp.dot(
                    gram[...], part, preferred_element_type=jnp.float32
                )
                current[:, span] = fresh.astype(jnp.bfloat16)
                return carry

            return lax.fori_loop(0, chunks, update, carry)

        lax.fori_loop(0, NS_STEPS, sweep, 0)

    @pl.when(kind == 1)
    def _():
        for k in range(DP):
            results[k][...] = current[pl.ds(spot(k, rows), rows), :]

    @pl.when(kind == 2)
    def _():
        for k in range(DP):
            for there, here in folds(k):
                results[k][here] = current[there]


def orthogonal_shards(info, shards, size):
    rows, length = shards[0].shape
    vmem = pl.BlockSpec(memory_space=pltpu.VMEM)
    return kernel_call(
        orthogonal_body,
        [shape_of((rows, length))] * DP,
        26e9,
        8e6,
        in_specs=[pl.BlockSpec(memory_space=pltpu.SMEM)] + [vmem] * DP,
        out_specs=[vmem] * DP,
        scratch_shapes=[
            pltpu.VMEM((size, length), jnp.bfloat16),
            pltpu.VMEM((size, size), jnp.bfloat16),
            pltpu.VMEM((size, size), jnp.float32),
        ],
        name="orthogonal_shards",
    )(info, *shards)


def fold_tall(block, rows, length):
    columns, size = block.shape
    block = block.T.reshape(size // rows, rows, columns).transpose(1, 0, 2).reshape(rows, -1)
    return jnp.pad(block, ((0, 0), (0, length - block.shape[1])))


def unfold_tall(block, columns):
    rows = block.shape[0]
    size = rows * DP
    block = block[:, : size // rows * columns].reshape(rows, size // rows, columns)
    return block.transpose(1, 0, 2).reshape(size, columns).T


def orthogonal_router_body(matrix_ref, out_ref):
    current = matrix_ref[...]
    dot = functools.partial(
        lax.dot_general, precision=HIGHEST_PRECISION, preferred_element_type=jnp.float32
    )
    square = jnp.sum(jnp.sum(current * current, axis=1, keepdims=True), axis=0, keepdims=True)
    current = current / (jnp.sqrt(square) + 1e-07)
    for _ in range(NS_STEPS):
        gram = dot(current, current, (((1,), (1,)), ((), ())))
        poly = POLY_SECOND * gram + POLY_THIRD * dot(gram, gram, (((1,), (0,)), ((), ())))
        current = POLY_FIRST * current + dot(poly, current, (((1,), (0,)), ((), ())))
    out_ref[...] = current


def orthogonal_router(matrix):
    return kernel_call(
        orthogonal_router_body, shape_of(matrix.shape, jnp.float32), 2e9, 1e6, name="orthogonal_router"
    )(matrix)


def slot_table(owners):
    table = np.zeros((FS, DP), np.int32)
    for f, column in enumerate(owners):
        for slot, d in enumerate(column):
            table[f, d] = slot
    return table


def owner_pairs(owners, step, back):
    pairs = []
    for f, column in enumerate(owners):
        for d in column:
            other = (d + step) % DP
            pair = (other * FS + f, d * FS + f)
            pairs.append(pair[::-1] if back else pair)
    return pairs


def to_owners(stack, owners, dp_index, index):
    table = jnp.asarray(slot_table(owners))[index]
    got = []
    for step in range(DP):
        slot = table[lax.rem(dp_index - step + DP, DP)]
        block = lax.dynamic_index_in_dim(stack, slot, 0, keepdims=False)
        got.append(
            block if step == 0 else lax.ppermute(block, AXES, owner_pairs(owners, step, False))
        )
    return got


def from_owners(blocks, owners, dp_index, index):
    got = jnp.stack(
        [
            block if step == 0 else lax.ppermute(block, AXES, owner_pairs(owners, step, True))
            for step, block in enumerate(blocks)
        ]
    )
    count = max(len(column) for column in owners)
    table = np.array([list(column) + [0] * (count - len(column)) for column in owners], np.int32)
    places = jnp.asarray(table)[index]
    return [
        lax.dynamic_index_in_dim(got, lax.rem(dp_index - places[slot] + DP, DP), 0, keepdims=False)
        for slot in range(count)
    ]


def line_hop(value, step):
    pairs = [
        ((z * 2 + y) * FS + f, ((z + step) % LINE * 2 + y) * FS + f)
        for z in range(LINE)
        for y in range(2)
        for f in range(FS)
    ]
    return lax.ppermute(value, AXES, pairs)


def pair_hop(value):
    pairs = [(d * FS + f, (d ^ 1) * FS + f) for d in range(DP) for f in range(FS)]
    return lax.ppermute(value, AXES, pairs)


def place_body(places_ref, *refs):
    out_ref = refs[-1]
    rows = refs[0].shape[0]
    other_ref = refs[-2]
    for i, ref in enumerate(refs[:-2]):
        out_ref[pl.ds(pl.multiple_of(places_ref[i] * rows, rows), rows), :] = ref[...]
        start = pl.multiple_of(places_ref[LINE + i] * rows, rows)
        out_ref[pl.ds(start, rows), :] = other_ref[i]


class Gather:
    def __init__(self, block, place):
        _, self.side, self.level = place
        self.blocks = [block] + [line_hop(block, step) for step in range(1, LINE)]

    def cross(self, *events):
        self.stack = jnp.stack(self.blocks)
        if events:
            self.stack = after(self.stack, *events)
        self.other = pair_hop(self.stack)
        return self.other

    def last(self):
        levels = lax.rem(self.level + LINE - jnp.arange(LINE), LINE)
        places = jnp.concatenate([levels * 2 + self.side, levels * 2 + 1 - self.side])
        rows, columns = self.blocks[0].shape
        vmem = pl.BlockSpec(memory_space=pltpu.VMEM)
        return kernel_call(
            place_body,
            shape_of((DP * rows, columns), self.stack.dtype),
            0,
            4 * DP * rows * columns,
            in_specs=[pl.BlockSpec(memory_space=pltpu.SMEM)] + [vmem] * (LINE + 1),
            out_specs=vmem,
            name="place_rows",
        )(places.astype(jnp.int32), *self.blocks, self.other)


class Reduce:
    def __init__(self, grads, place):
        _, self.side, self.level = place
        rows, columns = grads.shape
        self.grads = grads.reshape(LINE, 2, rows // DP, columns)

    def pick(self, array, i, axis=0):
        return lax.dynamic_index_in_dim(array, i, axis, keepdims=False)

    def cross(self, *events):
        grads = after(self.grads, *events) if events else self.grads
        self.got = pair_hop(self.pick(grads, 1 - self.side, 1))
        return self.got

    def along(self, *events):
        got = after(self.got, *events) if events else self.got
        mine = self.pick(self.grads, self.side, 1)
        both = (mine.astype(jnp.float32) + got.astype(jnp.float32)).astype(mine.dtype)
        at = lambda step: self.pick(both, lax.rem(self.level + step, LINE))
        self.parts = [at(0)] + [line_hop(at(step), step) for step in range(1, LINE)]
        return self.parts[1]

    def last(self):
        return sum(part.astype(jnp.float32) for part in self.parts)


def split_plan(
    tokens,
    cotangent,
    lengths,
    routes,
    gains,
    gain_moms,
    w_dense,
    mom_dense,
    w_router,
    mom_router,
    w_down,
    mom_down,
    e_gate_up,
    e_mom_gate_up,
    e_down,
    e_mom_down,
):
    index, dp_index = lax.axis_index("fsdp"), lax.axis_index("dp")
    device_index = dp_index * FS + index
    rows, local_len, width = tokens.shape
    row_len = local_len * FS
    count = rows * row_len
    experts = w_router.shape[1]
    head_size = width // HEADS
    quarter = width // FS
    block_rows = w_dense.shape[0]
    down_rows = w_down.shape[0]
    ff_shared = down_rows * DP * FS
    ff_part = down_rows * DP
    bf16 = jnp.bfloat16

    def by_columns(matrix):
        qkv_parts = [
            matrix[:, i * width : (i + 1) * width].reshape(block_rows, FS, quarter)
            for i in range(3)
        ]
        shared_parts = [
            matrix[:, 4 * width + i * ff_shared : 4 * width + (i + 1) * ff_shared]
            .reshape(block_rows, DP, FS, down_rows)
            .transpose(0, 2, 1, 3)
            .reshape(block_rows, FS, ff_part)
            for i in range(2)
        ]
        return jnp.concatenate(qkv_parts + shared_parts, axis=2).transpose(1, 0, 2)

    dense = w_dense.astype(bf16)
    own_columns = by_columns(dense)
    qkv_columns = own_columns[..., : 3 * quarter]
    common = jnp.concatenate(
        [
            w_router.astype(bf16),
            gains.astype(bf16).T,
            jnp.zeros((block_rows, LANES - experts - 2), bf16),
        ],
        axis=1,
    )
    spread = lambda array: jnp.broadcast_to(array, (FS,) + array.shape)
    place = (index, dp_index % 2, dp_index // 2)
    gate_up_copy = lax.all_gather(e_gate_up[0].astype(bf16), "dp", axis=1, tiled=True)
    edown_copy = lax.all_gather(e_down[0].astype(bf16), "dp", axis=0, tiled=True)
    message = jnp.concatenate([qkv_columns, spread(common)], axis=2)
    message = jnp.concatenate(exchange_fsdp(message, index), axis=0)
    folds = message.shape[0]
    fold_down, fold_out = down_rows * width // folds, block_rows * width // folds
    own_out = dense[:, 3 * width : 4 * width].reshape(folds, fold_out)
    first_pack = Gather(jnp.concatenate([message, own_out], axis=1), place)
    routes_low = jnp.concatenate(
        [routes.astype(bf16), jnp.zeros((rows, local_len, LANES - routes.shape[2]), bf16)], axis=2
    )
    inputs = jnp.concatenate(
        gather_fsdp(jnp.concatenate([tokens, routes_low], axis=2), index), axis=1
    )
    message = jnp.concatenate(exchange_fsdp(own_columns[..., 3 * quarter :], index), axis=0)
    message = after(message, *first_pack.blocks[1:])
    second_pack = Gather(
        jnp.concatenate([message, w_down.astype(bf16).reshape(folds, fold_down)], axis=1), place
    )
    first_pack.cross()
    pack = first_pack.last()
    w_qkv, w_route = pack[:, : 3 * quarter], pack[:, 3 * quarter : 3 * quarter + LANES]
    w_out = pack[:, 3 * quarter + LANES :].reshape(DP, block_rows, width)
    gain_rows = w_route[:, experts : experts + 2].astype(jnp.float32).T
    gain_one, gain_two = gain_rows[0:1], gain_rows[1:2]

    x_all = inputs[..., :width]
    route_all = inputs[..., width:].astype(jnp.int32).reshape(count, LANES)
    all_places = jnp.arange(row_len)
    valid_all = all_places[None, :] < lengths[:, None]
    half = head_size // 2
    frequency = 10000.0 ** (-2.0 * jnp.arange(half, dtype=jnp.float32) / head_size)
    angles = all_places.astype(jnp.float32)[:, None] * frequency[None, :]
    repeats = (1, 2 * quarter // half)
    cosine, sine = jnp.tile(jnp.cos(angles), repeats), jnp.tile(jnp.sin(angles), repeats)

    normed_one, qkv, probs, attended = attention_forward(
        x_all, gain_one, w_qkv, cosine, sine, lengths
    )
    cot_all = jnp.concatenate(gather_fsdp(after(cotangent, pack), index), axis=1)
    d_out_all = jnp.where(valid_all[..., None], cot_all, 0).reshape(count, width)
    attended_all = jnp.concatenate(gather_fsdp(attended, index), axis=2)
    w_out = jnp.stack(gather_fsdp(w_out, index), axis=1).reshape(width, width)
    second_pack.cross()
    pack = second_pack.last()
    w_shared = pack[:, : 2 * ff_part]
    down_copy = pack[:, 2 * ff_part :].reshape(DP * down_rows, width)
    mid_all, normed_all, turned_all, gates_all = middle_forward(
        after(attended_all, second_pack.other).reshape(count, width), x_all.reshape(count, width), route_all, w_out, w_route,
        gain_two,
    )
    gate_column = lax.dynamic_slice_in_dim(gates_all, index, 1, 1)
    expert = index.reshape(1)
    tile = min(512, ff_part)
    shared_tiles = ff_part // tile
    columns_at = lambda start: pl.BlockSpec((width, tile), lambda j: (0, start + j))
    first_out, first_back, grad_pair, grad_down = branch(
        expert, normed_all, turned_all, d_out_all, None, None,
        ((w_shared, columns_at(0)), (w_shared, columns_at(shared_tiles)), down_copy),
        (0, shared_tiles, tile), False, "shared_branch",
    )
    part_at = lambda start, half: pl.BlockSpec(
        (None, width, tile), lambda j: (half, 0, start + j)
    )
    ff_width = e_gate_up.shape[3]
    sum_shared = Reduce(
        jnp.concatenate([grad_pair, grad_down.reshape(width, fold_down)], axis=1), place
    )
    sum_shared.cross()
    out_part, message, grad_pairs, grad_edown = branch(
        expert, after(normed_all, sum_shared.got), turned_all, d_out_all, gate_column,
        [first_out, first_back, jnp.zeros((count, 1), jnp.float32)],
        ((gate_up_copy, part_at(0, 0)), (gate_up_copy, part_at(0, 1)), edown_copy),
        (0, ff_width // tile, tile), True, "expert_branch",
    )

    sum_shared.along()
    part_pairs = lax.psum_scatter(grad_pairs, "dp", scatter_dimension=0, tiled=True)
    sum_edown = Reduce(grad_edown, place)

    def by_place(values):
        return values.reshape(rows, FS, local_len, values.shape[-1]).transpose(1, 0, 2, 3)

    def own_rows(values):
        part = lax.dynamic_slice_in_dim(
            values.reshape(rows, row_len, values.shape[-1]), index * local_len, local_len, 1
        )
        return part.reshape(rows * local_len, values.shape[-1])

    d_sum = reduce_fsdp(by_place(after(message, *sum_shared.parts[1:])), index)
    d_sum = d_sum.reshape(rows * local_len, width + LANES)
    sum_edown.cross()
    mid = own_rows(mid_all)
    d_out = own_rows(d_out_all)
    d_mid, d_att, grad_wout, grad_router, grad_gain_two = middle_backward(
        mid, d_out, d_sum, own_rows(gates_all),
        routes.reshape(rows * local_len, -1), own_rows(attended_all), own_rows(normed_all), w_out,
        w_route, gain_two,
    )
    d_att = d_att.reshape(rows, local_len, FS, quarter).transpose(2, 0, 1, 3)
    d_att = jnp.concatenate(exchange_fsdp(d_att, index), axis=1)
    grad_wout = grad_wout.reshape(DP, FS, block_rows, width).transpose(1, 0, 2, 3)
    grad_wout = reduce_fsdp(grad_wout, index).astype(bf16).reshape(width, fold_out)
    grad_qkv, back_part = attention_backward(
        normed_one, qkv, probs, after(d_att, grad_wout, sum_edown.got), w_qkv, cosine, sine
    )
    sum_last = Reduce(jnp.concatenate([grad_qkv, grad_wout], axis=1), place)
    sum_last.cross()
    sum_last.along()
    sum_edown.along(sum_last.got)

    split_pair = lambda part, half: part.reshape(part.shape[0], -1, 2, tile)[:, :, half].reshape(
        part.shape[0], -1
    )
    part_shared = sum_shared.last()
    part_down = part_shared[:, 2 * ff_part :].reshape(down_rows, width)
    part_pairs = part_pairs.astype(jnp.float32)
    part_gate_up = jnp.stack([split_pair(part_pairs, half) for half in range(2)])
    part_last = sum_last.last()
    part_edown = sum_edown.last()
    part_out = part_last[:, 3 * quarter :].reshape(block_rows, width)
    part_near = jnp.concatenate(
        [
            part_last[:, : 3 * quarter],
            split_pair(part_shared[:, : 2 * ff_part], 0),
            split_pair(part_shared[:, : 2 * ff_part], 1),
        ],
        axis=1,
    )
    part_dense = part_near.astype(bf16)

    out_sum = reduce_fsdp(by_place(out_part), index).reshape(rows * local_len, width)
    valid = (
        (index * local_len + jnp.arange(local_len))[None, :] < lengths[:, None]
    ).astype(jnp.float32)
    output = ((mid + out_sum).reshape(tokens.shape) * valid[..., None]).astype(bf16)
    d_one = reduce_fsdp(by_place(back_part), index).reshape(tokens.shape)
    scaled_one, inverse_one = statistics(tokens.astype(jnp.float32))
    d_in, grad_gain_one = norm_back(d_one, scaled_one, inverse_one, gain_one)
    d_tokens = (d_mid.reshape(tokens.shape) + d_in).astype(bf16)

    columns = (0, device_index * block_rows)
    zeros = jnp.zeros((8 - experts - 2, width), jnp.float32)
    small = jnp.concatenate(
        [grad_router[:experts], grad_gain_one[None], grad_gain_two, zeros], axis=0
    )
    old = jnp.concatenate(
        [MUON_DECAY * mom_router.T, GAIN_DECAY * gain_moms, zeros[:, :block_rows]], axis=0
    )
    small = small + lax.dynamic_update_slice(jnp.zeros_like(small), old, columns)
    small = sum_everywhere(small)
    own_small = lax.dynamic_slice(small, columns, (8, block_rows))
    new_mom_router = own_small[:experts].T
    new_gain_moms = own_small[experts : experts + 2]
    gain_rate = 0.1 / math.sqrt(count * DP)
    new_gains = gains - gain_rate * new_gain_moms
    old_near = exchange_fsdp(by_columns(after(mom_dense, normed_all).astype(bf16)), index)
    old_near = jnp.concatenate(old_near, axis=0).astype(jnp.float32)
    got = exchange_fsdp(part_dense.reshape(FS, block_rows, part_dense.shape[1]), index)
    got = [block.astype(jnp.float32) for block in got]
    cut = lambda start, size: [block[:, start : start + size] for block in got]
    interleave = lambda parts: jnp.stack(
        [part.reshape(block_rows, DP, down_rows) for part in parts], axis=2
    ).reshape(block_rows, ff_shared)
    grad_dense = jnp.concatenate(
        cut(0, quarter)
        + cut(quarter, quarter)
        + cut(2 * quarter, quarter)
        + [part_out]
        + [interleave(cut(3 * quarter, ff_part)), interleave(cut(3 * quarter + ff_part, ff_part))],
        axis=1,
    )
    new_mom_dense = MUON_DECAY * mom_dense + grad_dense
    new_mom_down = MUON_DECAY * mom_down + part_down
    new_e_mom_gate_up = MUON_DECAY * e_mom_gate_up + part_gate_up[None]
    new_e_mom_down = MUON_DECAY * e_mom_down + part_edown[None]

    length = 3 * width
    pad = lambda block: jnp.pad(block, ((0, 0), (0, length - block.shape[1])))
    edges = (0, 3 * width, 4 * width, 4 * width + ff_shared, 4 * width + 2 * ff_shared)
    spots = (0, 3 * quarter, 3 * quarter + ff_part, 3 * quarter + 2 * ff_part)
    near = (MUON_DECAY * old_near + part_near).astype(bf16)
    near_out = (MUON_DECAY * mom_dense[:, 3 * width : 4 * width] + part_out).astype(bf16)
    stripe = lambda block: jnp.pad(block, ((0, 0), (0, 3 * quarter - block.shape[1])))
    stripes = [near[:, spots[i] : spots[i + 1]] for i in range(3)]
    stripes.append(near_out.reshape(folds, fold_out))
    got = exchange_fsdp(jnp.stack([stripe(block) for block in stripes]), index)
    whole_out = jnp.concatenate(
        [block[:, :fold_out].reshape(block_rows, width) for block in got], axis=0
    )
    dense_block = jnp.where(index == FS - 1, pad(whole_out), jnp.concatenate(got, axis=1))
    low_experts = after(new_e_mom_gate_up[0].astype(bf16), small)
    wide = [pad(low_experts[0]), pad(low_experts[1]), dense_block]
    low_down = new_mom_down.astype(bf16)
    column_pairs = lambda step, back: [
        (d * FS + DOWN_COLUMN, d * FS + (DOWN_COLUMN ^ step))[:: 1 if back else -1]
        for d in range(DP)
    ]
    down_block = jnp.concatenate(
        [
            low_down if f == DOWN_COLUMN else lax.ppermute(
                low_down, AXES, column_pairs(DOWN_COLUMN ^ f, False)
            )
            for f in range(FS)
        ],
        axis=0,
    )
    talls = [fold_tall(new_e_mom_down[0].astype(bf16), folds, length), fold_tall(down_block, folds, length)]
    shards = to_owners(jnp.stack(wide + talls), OWNERS, dp_index, index)
    kinds = np.zeros((FS, DP), np.int32)
    for f in range(FS):
        for slot, d in enumerate(OWNERS[f]):
            kinds[f, d] = 2 if slot in TALL_SLOTS else 1
    info = jnp.stack([jnp.asarray(kinds)[index, dp_index], dp_index.astype(jnp.int32)])
    shards = orthogonal_shards(info, shards, width)
    orth_router = orthogonal_router(
        jnp.concatenate([after(small, *shards)[:experts], jnp.zeros((LANES - experts, width), jnp.float32)], axis=0)
    )
    new_router = w_router - ROUTER_RATE * lax.dynamic_slice(
        orth_router, columns, (experts, block_rows)
    ).T

    orth_gate, orth_up, orth_block, orth_edown, orth_down_block = from_owners(
        shards, OWNERS, dp_index, index
    )
    orth_edown = unfold_tall(orth_edown, e_down.shape[1])
    orth_down_block = unfold_tall(orth_down_block, e_down.shape[1])
    got = exchange_fsdp(orth_block.reshape(FS, block_rows, length), index)
    striped = lambda block: block.reshape(block_rows, FS, 3 * quarter)
    orth_qkv = striped(got[0]).reshape(block_rows, FS, 3, quarter).transpose(0, 2, 1, 3)
    orth_shared = [
        striped(got[i])[:, :, :ff_part]
        .reshape(block_rows, FS, DP, down_rows)
        .transpose(0, 2, 1, 3)
        .reshape(block_rows, ff_shared)
        for i in (1, 2)
    ]
    orth_dense = [orth_qkv.reshape(block_rows, 3 * width), got[3][:, :width]] + orth_shared
    orth_down_parts = orth_down_block.reshape(FS, down_rows, width)
    orth_down = jnp.where(index == DOWN_COLUMN, orth_down_parts[DOWN_COLUMN], 0)
    for f in range(FS):
        if f != DOWN_COLUMN:
            orth_down = orth_down + lax.ppermute(
                orth_down_parts[f], AXES, column_pairs(DOWN_COLUMN ^ f, True)
            )
    new_dense = jnp.concatenate(
        [
            w_dense[:, edges[i] : edges[i + 1]] - DENSE_RATES[i] * orth_dense[i].astype(jnp.float32)
            for i in range(4)
        ],
        axis=1,
    )
    new_down = w_down - DOWN_RATE * orth_down.astype(jnp.float32)
    new_e_gate_up = jnp.stack(
        [
            e_gate_up[0, i] - EXPERT_RATES[i] * part[:, :ff_width].astype(jnp.float32)
            for i, part in enumerate((orth_gate, orth_up))
        ]
    )[None]
    new_e_down = e_down - EXPERT_RATES[2] * orth_edown.astype(jnp.float32)[None]
    return (
        output,
        d_tokens,
        new_gain_moms,
        new_gains,
        new_mom_dense,
        new_dense,
        new_mom_router,
        new_router,
        new_mom_down,
        new_down,
        new_e_mom_gate_up,
        new_e_gate_up,
        new_e_mom_down,
        new_e_down,
    )


def solution(mesh):
    placed = (
        P("dp", "fsdp", None),
        P("dp", "fsdp", None),
        P("dp"),
        P("dp", "fsdp", None),
        P(None, ("dp", "fsdp")),
        P(None, ("dp", "fsdp")),
        P(("dp", "fsdp"), None),
        P(("dp", "fsdp"), None),
        P(("dp", "fsdp"), None),
        P(("dp", "fsdp"), None),
        P(("dp", "fsdp"), None),
        P(("dp", "fsdp"), None),
        P("fsdp", None, "dp", None),
        P("fsdp", None, "dp", None),
        P("fsdp", "dp", None),
        P("fsdp", "dp", None),
    )
    fits = dict(mesh.shape) == {"dp": DP, "fsdp": FS}
    return jax.shard_map(
        split_plan if fits else general_plan,
        mesh=mesh,
        in_specs=placed,
        out_specs=(
            P("dp", "fsdp", None),
            P("dp", "fsdp", None),
            P(None, ("dp", "fsdp")),
            P(None, ("dp", "fsdp")),
            P(("dp", "fsdp"), None),
            P(("dp", "fsdp"), None),
            P(("dp", "fsdp"), None),
            P(("dp", "fsdp"), None),
            P(("dp", "fsdp"), None),
            P(("dp", "fsdp"), None),
            P("fsdp", None, "dp", None),
            P("fsdp", None, "dp", None),
            P("fsdp", "dp", None),
            P("fsdp", "dp", None),
        ),
        check_vma=False,
    )
```
